32 devices in a mesh: section: 4 (over y, x), dp: 8 (over z, core).
Axes of the slice: x: 2, y: 2, z: 4, core: 2. Of those that a mesh axis runs over, the one named last changes fastest.
Arguments:
- stream_input: bfloat16 [16384, 512], P('dp', 'section'), may hold values from -6 to 6
- accum_input: bfloat16 [16384, 512], P('dp', 'section'), may hold values from -6 to 6
- section_weights: bfloat16 [4, 512, 3072], P('section')
- section_norms: bfloat16 [4, 2, 512], P('section')
- final_norm: bfloat16 [2, 512], P(None, 'section')
- seq_lengths: int32 [16, 16], P('dp'), may hold values from 0 to 1024, as said below
- out_cotangent: bfloat16 [16384, 512], P('dp', 'section'), may hold values from -6 to 6
Outputs:
- final_output: bfloat16 [16384, 512], P('dp', 'section')
- stream_input_grad: float32 [16384, 512], P('dp', 'section')
- accum_input_grad: float32 [16384, 512], P('dp', 'section')
- section_weights_grad: float32 [4, 512, 3072], P('section', None, 'dp')
- section_norms_grad: float32 [4, 2, 512], P('section', None, 'dp')
- final_norm_grad: float32 [2, 512], P(None, 'section')
The draws below stay inside these ranges and needn't reach their ends.
Inputs may be any that keep to these rules, and one draw needn't show every extreme that they name: `seq_lengths`: A row is either one sequence of 512 to 1024 tokens followed by zeros, or 16 sequences of 1 to 64 tokens each; a row sums to at most 1024, and some row holds one sequence of 1024 tokens.
All inputs are finite; a program needn't handle non-finite values.
Results may differ from the reference program's by a relative error of at most 0.02.
Values may be sent and summed in bfloat16 or wider, within the bound.
No kernel may reach another device: no remote copies, remote signals or barrier semaphores. Data moves between devices by JAX's collectives and lax.ppermute only.
A program may use at most 256 MiB of HBM per device.

```python
import jax
import jax.numpy as jnp
from jax import lax

D = 512
HEADS = 8
HEAD = 64
FF = 2048
PACK = 1024
SEQS = 16
SECTIONS = 4
PACKS = 16
TOKENS = 16384


def draw_section_weights(key, part):
    key = jax.random.fold_in(key, 11)
    entries = jax.random.normal(key, (SECTIONS, D, 6 * D), jnp.float32)
    column = jnp.arange(6 * D)
    parity = jnp.arange(SECTIONS) % 2
    even_scale = jnp.where((column >= 3 * D) & (column < 4 * D), 3.0, 1.0) * D ** (-0.5)
    odd_scale = jnp.where(column < 2 * D, D ** (-0.5), 1.5 * FF ** (-0.5))
    factor = jnp.where(parity[:, None] == 0, even_scale[None, :], odd_scale[None, :])
    return (entries * factor[:, None, :]).astype(jnp.bfloat16)


def draw_section_norms(key, part):
    key = jax.random.fold_in(key, 12)
    gain_key, shift_key = jax.random.split(key)
    gain_rows = jax.random.uniform(gain_key, (SECTIONS, D), jnp.float32, 0.7, 1.3)
    shifts = 0.3 * jax.random.normal(shift_key, (SECTIONS, D), jnp.float32)
    return jnp.stack([gain_rows, shifts], axis=1).astype(jnp.bfloat16)


def draw_final_norm(key, part):
    key = jax.random.fold_in(key, 13)
    gain_key, shift_key = jax.random.split(key)
    gain_rows = jax.random.uniform(gain_key, (D,), jnp.float32, 0.7, 1.3)
    shifts = 0.3 * jax.random.normal(shift_key, (D,), jnp.float32)
    return jnp.stack([gain_rows, shifts], axis=0).astype(jnp.bfloat16)


def draw_seq_lengths(key, part):
    key = jax.random.fold_in(key, 14)
    subkeys = jax.random.split(key, 4)
    longish = jax.random.randint(subkeys[0], (PACKS,), 0, 4) == 0
    long_len = jax.random.randint(subkeys[1], (PACKS,), PACK // 2, PACK + 1)
    shorts = jax.random.randint(subkeys[2], (PACKS, SEQS), 1, PACK // SEQS + 1)
    chosen = jax.random.randint(subkeys[3], (), 0, PACKS)
    pack_ids = jnp.arange(PACKS)
    longish = longish | (pack_ids == chosen)
    long_len = jnp.where(pack_ids == chosen, PACK, long_len)
    slot_ids = jnp.arange(SEQS)
    single = jnp.where(slot_ids[None, :] == 0, long_len[:, None], 0)
    return jnp.where(longish[:, None], single, shorts).astype(jnp.int32)


def levels(own_key, shape, pieces, low, largest):
    def one(position, parts):
        draws = jax.random.uniform(jax.random.fold_in(jax.random.fold_in(own_key, 6), position), (parts,), jnp.float32, low / len(pieces), largest / len(pieces))
        return jnp.repeat(jnp.exp(draws), shape[position] // parts).reshape((-1,) + (1,) * (len(shape) - position - 1))

    gain = one(*pieces[0])
    for cut in pieces[1:]:
        gain = gain * one(*cut)
    return gain


def normal_values(rng, shape, scale, bound, shards=(), held_as=jnp.bfloat16):
    level = levels(rng, shape, shards, -0.22, 0.18) if shards else 1.0
    values = jax.random.normal(rng, shape, jnp.float32) * scale * level
    return jnp.minimum(jnp.maximum(values, -bound), bound).astype(held_as)


def setup_inputs(seed: int = 0) -> dict:
    keys = jax.random.split(jax.random.key(seed), 8)
    stream_input = normal_values(keys[0], (TOKENS, D), 1.0, 6.0, ((0, 8), (1, 4)))
    accum_input = normal_values(keys[1], (TOKENS, D), 1.0, 6.0, ((0, 8), (1, 4)))
    section_weights = draw_section_weights(jax.random.fold_in(keys[7], 71), 0)
    section_norms = draw_section_norms(jax.random.fold_in(keys[7], 71), 0)
    final_norm = draw_final_norm(jax.random.fold_in(keys[7], 71), 0)
    seq_lengths = draw_seq_lengths(jax.random.fold_in(keys[7], 71), 0)
    out_cotangent = normal_values(keys[6], (TOKENS, D), 1.0, 6.0, ((0, 8), (1, 4)))
    return {"stream_input": stream_input, "accum_input": accum_input, "section_weights": section_weights, "section_norms": section_norms, "final_norm": final_norm, "seq_lengths": seq_lengths, "out_cotangent": out_cotangent}


@jax.custom_vjp
def low(v):
    return lax.optimization_barrier(v.astype(jnp.bfloat16)).astype(jnp.float32)

@jax.custom_vjp
def low_back(v):
    return v

def low_keep(v):
    return (low(v), None)

def low_pass(kept, grad):
    return (grad,)

def back_keep(v):
    return (v, None)

def back_low(kept, grad):
    return (low(grad),)
low.defvjp(low_keep, low_pass)
low_back.defvjp(back_keep, back_low)
NEG_FILL = -1e+30

def both_low(value):
    return low(low_back(value))

def highest_dot(left, right):
    return jnp.dot(left, right, precision=lax.Precision.HIGHEST)

def norm_rows(summed, row_gain, row_shift):
    average = lax.optimization_barrier(jnp.mean(summed, axis=-1, keepdims=True))
    centered = summed - average
    spread = lax.optimization_barrier(jnp.mean(centered * centered, axis=-1, keepdims=True))
    return centered * lax.rsqrt(spread + 1e-05) * row_gain + row_shift

def segments_of(lengths):
    ending = jnp.cumsum(lengths, dtype=jnp.int32)
    places = jnp.arange(PACK, dtype=jnp.int32)
    segment = lax.optimization_barrier(jnp.sum((places[:, None] >= ending[None, :]).astype(jnp.int32), axis=1, dtype=jnp.int32))
    living = (places < ending[-1]).astype(jnp.float32)
    return (segment, living)

def attention_branch(stream, weights, segment):
    projected = both_low(highest_dot(stream, weights[:, :3 * D]))
    queries = projected[:, :D].reshape(PACK, HEADS, HEAD)
    key_rows = projected[:, D:2 * D].reshape(PACK, HEADS, HEAD)
    value_rows = projected[:, 2 * D:].reshape(PACK, HEADS, HEAD)
    scores = jnp.einsum('qhd,khd->hqk', queries, key_rows, precision=lax.Precision.HIGHEST) * HEAD ** (-0.5)
    scores = low_back(scores)
    same_seq = segment[:, None] == segment[None, :]
    scores = jnp.where(same_seq[None], scores, NEG_FILL)
    probability = low(jax.nn.softmax(scores, axis=-1))
    context = jnp.einsum('hqk,khd->qhd', probability, value_rows, precision=lax.Precision.HIGHEST)
    context = both_low(context.reshape(PACK, D))
    return low_back(highest_dot(context, weights[:, 3 * D:4 * D]))

def feed_branch(stream, inward, outward_t):
    preact = low_back(highest_dot(stream, inward))
    hidden = low(jax.nn.gelu(preact))
    product = lax.dot_general(hidden, outward_t, (((1,), (1,)), ((), ())), precision=lax.Precision.HIGHEST)
    return low_back(product)

def pack_forward(stream, accum, weights_f, norms_f, final_f, segment):
    for sublayer in range(4):
        if sublayer % 2 == 0:
            branch = attention_branch(stream, weights_f[sublayer], segment)
        else:
            inward = jnp.concatenate([weights_f[sublayer - 1][:, 4 * D:], weights_f[sublayer][:, :2 * D]], axis=1)
            branch = feed_branch(stream, inward, weights_f[sublayer][:, 2 * D:])
        stream = norm_rows(stream + branch, norms_f[sublayer, 0], norms_f[sublayer, 1])
        accum = accum + branch
        if sublayer < 3:
            stream = both_low(stream)
    return stream + norm_rows(accum, final_f[0], final_f[1])

def reference(stream_input, accum_input, section_weights, section_norms, final_norm, seq_lengths, out_cotangent):
    segment, living = jax.vmap(segments_of)(seq_lengths)
    stream_all = stream_input.astype(jnp.float32).reshape(PACKS, PACK, D)
    accum_all = accum_input.astype(jnp.float32).reshape(PACKS, PACK, D)

    def whole_run(stream_f, accum_f, weights_f, norms_f, final_f):

        def per_pack(running, pack_items):
            return (running, pack_forward(pack_items[0], pack_items[1], weights_f, norms_f, final_f, pack_items[2]))
        _, outputs = lax.scan(jax.checkpoint(per_pack), jnp.zeros((), jnp.float32), (stream_f, accum_f, segment))
        return outputs
    result, pullback = jax.vjp(whole_run, stream_all, accum_all, section_weights.astype(jnp.float32), section_norms.astype(jnp.float32), final_norm.astype(jnp.float32))
    cotangent = out_cotangent.astype(jnp.float32).reshape(PACKS, PACK, D) * living[:, :, None]
    stream_grad, accum_grad, weights_grad, norms_grad, final_grad = pullback(cotangent)
    return (result.reshape(TOKENS, D).astype(jnp.bfloat16), stream_grad.reshape(TOKENS, D), accum_grad.reshape(TOKENS, D), weights_grad, norms_grad, final_grad)
```

```python
import functools

import jax
import jax.numpy as jnp
from jax import lax
from jax.experimental import pallas as pl
from jax.experimental.pallas import tpu as pltpu
from jax.sharding import PartitionSpec as P

D = 512
HEADS = 8
HEAD = 64
PACK = 1024
HALF = PACK // 2
PAIRS = HEADS // 2
LANES = 2 * HEAD
SECTIONS = 4
FAR = 1e30
SCALE = HEAD ** (-0.5)
BF = jnp.bfloat16
F32 = jnp.float32
NT = (((1,), (1,)), ((), ()))
TN = (((0,), (0,)), ((), ()))


def mm(left, right):
    return jnp.dot(left, right, preferred_element_type=F32)


def mm_nt(left, right):
    return lax.dot_general(left, right, NT, preferred_element_type=F32)


def mm_tn(left, right):
    return lax.dot_general(left, right, TN, preferred_element_type=F32)


def params():
    return pltpu.CompilerParams(
        dimension_semantics=("arbitrary",), vmem_limit_bytes=48 * 1024 * 1024
    )


def shaped(rows, cols, dtype):
    return jax.ShapeDtypeStruct((rows, cols), dtype)


def whole(rows, cols):
    return pl.BlockSpec((rows, cols), lambda i: (0, 0))


def cost(flops, moved, transcendentals=0):
    return pl.CostEstimate(
        flops=int(flops), bytes_accessed=int(moved), transcendentals=int(transcendentals)
    )


def norm_parts(summed):
    average = jnp.mean(summed, axis=-1, keepdims=True)
    centered = summed - average
    spread = jnp.mean(centered * centered, axis=-1, keepdims=True)
    inverse = lax.rsqrt(spread + 1e-05)
    return centered * inverse, inverse


def norm_back(summed, gain, upstream):
    normal, inverse = norm_parts(summed)
    scaled = upstream * gain
    mean_one = jnp.mean(scaled, axis=-1, keepdims=True)
    mean_two = jnp.mean(scaled * normal, axis=-1, keepdims=True)
    grad = (scaled - mean_one - normal * mean_two) * inverse
    gain_grad = jnp.sum(upstream * normal, axis=0, keepdims=True)
    shift_grad = jnp.sum(upstream, axis=0, keepdims=True)
    return grad, gain_grad, shift_grad


def head_mask(which):
    lane = lax.broadcasted_iota(jnp.int32, (1, LANES), 1)
    return (lane // HEAD) == which


def three_way(column):
    high = column.astype(BF)
    rest = column - high.astype(F32)
    middle = rest.astype(BF)
    low = (rest - middle.astype(F32)).astype(BF)
    return high, middle, low


def project_kernel(x_ref, w_ref, out_ref):
    out_ref[...] = mm(x_ref[...], w_ref[0]).astype(BF)


def project(stream, weights, layer):
    return pl.pallas_call(
        project_kernel,
        grid=(3,),
        in_specs=[
            whole(HALF, D),
            pl.BlockSpec((1, D, D), lambda i: (layer, 0, i)),
        ],
        out_specs=pl.BlockSpec((HALF, D), lambda i: (0, i)),
        out_shape=shaped(HALF, 3 * D, BF),
        compiler_params=params(),
        cost_estimate=cost(2 * HALF * D * 3 * D, 4e6),
        name="project",
    )(stream, weights)


def attend_kernel(
    q_ref, ko_ref, vo_ref, kx_ref, vx_ref, qs_ref, kso_ref, ksx_ref, w_ref, x_ref, fsum_ref,
    norm_ref, ctx_ref, lse_ref, next_ref, sum_ref, fnew_ref, ctx_acc, lse_acc,
):
    pair = pl.program_id(0)
    q = q_ref[...] * jnp.asarray(SCALE, BF)
    keys_own = jnp.concatenate([ko_ref[...], kso_ref[...]], axis=1)
    keys_other = jnp.concatenate([kx_ref[...], ksx_ref[...]], axis=1)
    values_own, values_other = vo_ref[...], vx_ref[...]
    ones = jnp.ones((HALF, LANES), BF)
    none = jnp.zeros((), BF)
    lane = lax.broadcasted_iota(jnp.int32, (1, LANES), 1)
    context = jnp.zeros((HALF, LANES), F32)
    logs = jnp.where(pair == 0, jnp.zeros((HALF, LANES), F32), lse_acc[...])
    for which in range(2):
        mask = head_mask(which)
        query = jnp.concatenate([jnp.where(mask, q, none), qs_ref[...]], axis=1)
        score_own = mm_nt(query, keys_own)
        score_other = mm_nt(query, keys_other)
        peak = jnp.maximum(
            jnp.max(score_own, axis=1, keepdims=True), jnp.max(score_other, axis=1, keepdims=True)
        )
        own = jnp.exp(score_own - peak).astype(BF)
        other = jnp.exp(score_other - peak).astype(BF)
        total = mm(own, jnp.concatenate([jnp.where(mask, values_own, none), ones], axis=1)) + mm(
            other, jnp.concatenate([jnp.where(mask, values_other, none), ones], axis=1)
        )
        row_total = total[:, LANES:]
        context = context + total[:, :LANES] / row_total
        logs = jnp.where(lane == 2 * pair + which, peak + jnp.log(row_total), logs)
    lse_acc[...] = logs
    ctx_acc[pair] = context.astype(BF)
    ctx_ref[...] = context.astype(BF)

    @pl.when(pair == PAIRS - 1)
    def _():
        lse_ref[...] = lse_acc[...]
        full = jnp.concatenate([ctx_acc[k] for k in range(PAIRS)], axis=1)
        branch = mm(full, w_ref[0])
        summed = x_ref[...].astype(F32) + branch
        normal, _ = norm_parts(summed)
        moved = normal * norm_ref[0:1, :] + norm_ref[1:2, :]
        next_ref[...] = moved.astype(BF)
        sum_ref[...] = summed
        fnew_ref[...] = fsum_ref[...] + branch


def attend(stream, projected, other_kv, segs, weights, layer, norms, branch_sum):
    qseg, kseg_own, kseg_other = segs

    def column(offset):
        return pl.BlockSpec((HALF, LANES), lambda i: (0, offset + i))

    return pl.pallas_call(
        attend_kernel,
        grid=(PAIRS,),
        in_specs=[
            column(0), column(PAIRS), column(2 * PAIRS), column(0), column(PAIRS),
            whole(HALF, LANES), whole(HALF, LANES), whole(HALF, LANES),
            pl.BlockSpec((1, D, D), lambda i: (layer, 0, 3)),
            whole(HALF, D), whole(HALF, D), whole(2, D),
        ],
        out_specs=[
            column(0), whole(HALF, LANES), whole(HALF, D), whole(HALF, D), whole(HALF, D),
        ],
        out_shape=[
            shaped(HALF, D, BF), shaped(HALF, LANES, F32), shaped(HALF, D, BF),
            shaped(HALF, D, F32), shaped(HALF, D, F32),
        ],
        scratch_shapes=[pltpu.VMEM((PAIRS, HALF, LANES), BF), pltpu.VMEM((HALF, LANES), F32)],
        compiler_params=params(),
        cost_estimate=cost(8e9, 8e6, 4e6),
        name="attend",
    )(
        projected, projected, projected, other_kv, other_kv, qseg, kseg_own, kseg_other,
        weights, stream, branch_sum, norms,
    )


def gelu_parts(v):
    root = 0.7978845608028654
    squared = v * v
    inner = root * (v + 0.044715 * v * squared)
    t = jnp.tanh(inner)
    hidden = 0.5 * v * (1.0 + t)
    slope = 0.5 * (1.0 + t) + 0.5 * v * (1.0 - t * t) * (root * (1.0 + 3 * 0.044715 * squared))
    return hidden, slope


def feed_kernel(
    x_ref, w1_ref, w2_ref, fsum_ref, norm_ref, next_ref, sum_ref, fnew_ref, acc_ref
):
    step = pl.program_id(0)
    preact = mm(x_ref[...], w1_ref[0])
    hidden = gelu_parts(preact)[0].astype(BF)
    part = mm_nt(hidden, w2_ref[0])

    @pl.when(step == 0)
    def _():
        acc_ref[...] = part

    @pl.when(step > 0)
    def _():
        acc_ref[...] += part

    @pl.when(step == 3)
    def _():
        branch = acc_ref[...]
        summed = x_ref[...].astype(F32) + branch
        normal, _ = norm_parts(summed)
        moved = normal * norm_ref[0:1, :] + norm_ref[1:2, :]
        next_ref[...] = moved.astype(next_ref.dtype)
        sum_ref[...] = summed
        fnew_ref[...] = fsum_ref[...] + branch


def first_spec(layer):
    return pl.BlockSpec((1, D, D), lambda i: (layer - 1 + i // 2, 0, (4 + i) % 6))


def second_spec(layer):
    return pl.BlockSpec((1, D, D), lambda i: (layer, 0, 2 + i))


def feed(stream, weights, layer, norms, branch_sum, out_type):
    return pl.pallas_call(
        feed_kernel,
        grid=(4,),
        in_specs=[
            whole(HALF, D), first_spec(layer), second_spec(layer), whole(HALF, D), whole(2, D),
        ],
        out_specs=[whole(HALF, D), whole(HALF, D), whole(HALF, D)],
        out_shape=[shaped(HALF, D, out_type), shaped(HALF, D, F32), shaped(HALF, D, F32)],
        scratch_shapes=[pltpu.VMEM((HALF, D), F32)],
        compiler_params=params(),
        cost_estimate=cost(4 * HALF * D * 4 * D, 8e6, HALF * 4 * D),
        name="feed",
    )(stream, weights, weights, branch_sum, norms)


def finish_kernel(
    x_ref, fsum_ref, y_ref, cot_ref, live_ref, norm_ref, out_ref, c_ref, dy_ref, grad_ref
):
    summed = y_ref[...].astype(F32) + fsum_ref[...]
    normal, _ = norm_parts(summed)
    gain = norm_ref[0:1, :]
    out_ref[...] = (x_ref[...] + normal * gain + norm_ref[1:2, :]).astype(BF)
    cot = cot_ref[...].astype(F32) * live_ref[:, 0:1]
    c_ref[...] = cot
    grad, gain_grad, shift_grad = norm_back(summed, gain, cot)
    dy_ref[...] = grad
    grad_ref[0:1, :] = gain_grad
    grad_ref[1:2, :] = shift_grad


def finish(last, branch_sum, accum, cot, live, norms):
    return pl.pallas_call(
        finish_kernel,
        grid=(1,),
        in_specs=[
            whole(HALF, D), whole(HALF, D), whole(HALF, D), whole(HALF, D), whole(HALF, LANES),
            whole(2, D),
        ],
        out_specs=[whole(HALF, D), whole(HALF, D), whole(HALF, D), whole(2, D)],
        out_shape=[
            shaped(HALF, D, BF), shaped(HALF, D, F32), shaped(HALF, D, F32), shaped(2, D, F32),
        ],
        compiler_params=params(),
        cost_estimate=cost(1e7, 6e6),
        name="finish",
    )(last, branch_sum, accum, cot, live, norms)


def feed_back_kernel(
    x_ref, sum_ref, up_ref, dy_ref, w1_ref, w2_ref, norm_ref,
    dx_ref, dw1_ref, dw2_ref, grad_ref, acc_ref, df_ref, dft_ref, xt_ref,
):
    step = pl.program_id(0)

    @pl.when(step == 0)
    def _():
        grad, gain_grad, shift_grad = norm_back(
            sum_ref[...], norm_ref[0:1, :], up_ref[...].astype(F32)
        )
        grad_ref[0:1, :] = gain_grad
        grad_ref[1:2, :] = shift_grad
        acc_ref[...] = grad
        df = (grad + dy_ref[...]).astype(BF)
        df_ref[...] = df
        dft_ref[...] = df.T
        xt_ref[...] = x_ref[...].T

    preact = mm(x_ref[...], w1_ref[0])
    hidden, slope = gelu_parts(preact)
    dw2_ref[...] = mm(dft_ref[...], hidden.astype(BF)).astype(BF)
    hidden_grad = mm(df_ref[...], w2_ref[0])
    preact_grad = (hidden_grad * slope).astype(BF)
    dw1_ref[...] = mm(xt_ref[...], preact_grad).astype(BF)
    acc_ref[...] += mm_nt(preact_grad, w1_ref[0])

    @pl.when(step == 3)
    def _():
        dx_ref[...] = acc_ref[...].astype(BF)


def feed_back(stream, summed, upstream, dy, weights, layer, norms):
    return pl.pallas_call(
        feed_back_kernel,
        grid=(4,),
        in_specs=[
            whole(HALF, D), whole(HALF, D), whole(HALF, D), whole(HALF, D),
            first_spec(layer), second_spec(layer), whole(2, D),
        ],
        out_specs=[
            whole(HALF, D),
            pl.BlockSpec((D, D), lambda i: (0, i)),
            pl.BlockSpec((D, D), lambda i: (0, i)),
            whole(2, D),
        ],
        out_shape=[
            shaped(HALF, D, BF), shaped(D, 4 * D, BF), shaped(D, 4 * D, BF), shaped(2, D, F32),
        ],
        scratch_shapes=[
            pltpu.VMEM((HALF, D), F32), pltpu.VMEM((HALF, D), BF), pltpu.VMEM((D, HALF), BF),
            pltpu.VMEM((D, HALF), BF),
        ],
        compiler_params=params(),
        cost_estimate=cost(10 * HALF * D * 4 * D, 16e6, HALF * 4 * D),
        name="feed_back",
    )(stream, summed, upstream, dy, weights, weights, norms)


def outward_back_kernel(
    sum_ref, up_ref, dy_ref, ctx_ref, w_ref, norm_ref, dz_ref, dctx_ref, dwo_ref, delta_ref,
    grad_ref,
):
    grad, gain_grad, shift_grad = norm_back(sum_ref[...], norm_ref[0:1, :], up_ref[...].astype(F32))
    grad_ref[0:1, :] = gain_grad
    grad_ref[1:2, :] = shift_grad
    dz_ref[...] = grad
    df = (grad + dy_ref[...]).astype(BF)
    context = ctx_ref[...]
    dwo_ref[...] = mm_tn(context, df).astype(BF)
    context_grad = mm_nt(df, w_ref[0]).astype(BF)
    dctx_ref[...] = context_grad
    product = context.astype(F32) * context_grad.astype(F32)
    lane = lax.broadcasted_iota(jnp.int32, (1, LANES), 1)
    delta = jnp.zeros((HALF, LANES), F32)
    for head in range(HEADS):
        part = product[:, (head // 2) * LANES : (head // 2 + 1) * LANES]
        inner = jnp.sum(jnp.where(head_mask(head % 2), part, 0.0), axis=1, keepdims=True)
        delta = jnp.where(lane == head, inner, delta)
    delta_ref[...] = delta


def outward_back(summed, upstream, dy, context, weights, layer, norms):
    return pl.pallas_call(
        outward_back_kernel,
        grid=(1,),
        in_specs=[
            whole(HALF, D), whole(HALF, D), whole(HALF, D), whole(HALF, D),
            pl.BlockSpec((1, D, D), lambda i: (layer, 0, 3)), whole(2, D),
        ],
        out_specs=[
            whole(HALF, D), whole(HALF, D), whole(D, D), whole(HALF, LANES), whole(2, D),
        ],
        out_shape=[
            shaped(HALF, D, F32), shaped(HALF, D, BF), shaped(D, D, BF), shaped(HALF, LANES, F32),
            shaped(2, D, F32),
        ],
        compiler_params=params(),
        cost_estimate=cost(4 * HALF * D * D, 6e6),
        name="outward_back",
    )(summed, upstream, dy, context, weights, norms)


def scores_back_kernel(
    q_ref, k_ref, v_ref, dctx_ref, qs_ref, ks_ref, lse_ref, delta_ref, before_ref,
    dq_ref, dk_ref, dv_ref,
):
    pair = pl.program_id(0)
    none = jnp.zeros((), BF)
    lane = lax.broadcasted_iota(jnp.int32, (1, LANES), 1)
    q = q_ref[...] * jnp.asarray(SCALE, BF)
    k = k_ref[...]
    k_scaled = k * jnp.asarray(SCALE, BF)
    dctx = dctx_ref[...]
    extra = jnp.where((lane >= LANES - 3), jnp.ones((), BF), none)
    keys = jnp.concatenate([k, ks_ref[...] + extra], axis=1)
    values = jnp.concatenate([v_ref[...], jnp.broadcast_to(extra, (HALF, LANES))], axis=1)
    dq = before_ref[...]
    dk = jnp.zeros((HALF, LANES), F32)
    dv = jnp.zeros((HALF, LANES), F32)
    for which in range(2):
        mask = head_mask(which)
        here = lane == 2 * pair + which

        def lanes_of(table, base):
            column = -jnp.sum(jnp.where(here, table, 0.0), axis=1, keepdims=True)
            high, middle, low = three_way(column)
            base = jnp.where(lane == LANES - 3, high, base)
            base = jnp.where(lane == LANES - 2, middle, base)
            return jnp.where(lane == LANES - 1, low, base)

        query_part = jnp.where(mask, q, none)
        dctx_part = jnp.where(mask, dctx, none)
        query = jnp.concatenate([query_part, lanes_of(lse_ref[...], qs_ref[...])], axis=1)
        dcontext = jnp.concatenate(
            [dctx_part, lanes_of(delta_ref[...], jnp.zeros((HALF, LANES), BF))], axis=1
        )
        probability = jnp.exp(mm_nt(keys, query))
        score_grad = (probability * mm_nt(values, dcontext)).astype(BF)
        dv = dv + mm(probability.astype(BF), dctx_part)
        dk = dk + mm(score_grad, query_part)
        dq = dq + mm_tn(score_grad, jnp.where(mask, k_scaled, none))
    dq_ref[...] = dq
    dk_ref[...] = dk.astype(dk_ref.dtype)
    dv_ref[...] = dv.astype(dv_ref.dtype)


def scores_back(projected, keys, key_offset, dctx, qseg, kseg, lse, delta, before, out_type):
    def column(offset):
        return pl.BlockSpec((HALF, LANES), lambda i: (0, offset + i))

    return pl.pallas_call(
        scores_back_kernel,
        grid=(PAIRS,),
        in_specs=[
            column(0), column(key_offset), column(key_offset + PAIRS), column(0),
            whole(HALF, LANES), whole(HALF, LANES), whole(HALF, LANES), whole(HALF, LANES),
            column(0),
        ],
        out_specs=[column(0), column(0), column(0)],
        out_shape=[shaped(HALF, D, F32), shaped(HALF, D, out_type), shaped(HALF, D, out_type)],
        compiler_params=params(),
        cost_estimate=cost(8e9, 8e6, 2e6),
        name="scores_back",
    )(projected, keys, keys, dctx, qseg, kseg, lse, delta, before)


def project_back_kernel(
    x_ref, dq_ref, dk_ref, dv_ref, dkx_ref, dvx_ref, dz_ref, w_ref, dx_ref, dw_ref, acc_ref, xt_ref
):
    step = pl.program_id(0)

    @pl.when(step == 0)
    def _():
        xt_ref[...] = x_ref[...].T
        acc_ref[...] = dz_ref[...]

    def add(grad):
        dw_ref[...] = mm(xt_ref[...], grad).astype(BF)
        acc_ref[...] += mm_nt(grad, w_ref[0])

    @pl.when(step == 0)
    def _():
        add(dq_ref[...].astype(BF))

    @pl.when(step == 1)
    def _():
        add((dk_ref[...] + dkx_ref[...].astype(F32)).astype(BF))

    @pl.when(step == 2)
    def _():
        add((dv_ref[...] + dvx_ref[...].astype(F32)).astype(BF))
        dx_ref[...] = acc_ref[...].astype(BF)


def project_back(stream, dq, dk, dv, dk_other, dv_other, dz, weights, layer):
    return pl.pallas_call(
        project_back_kernel,
        grid=(3,),
        in_specs=[whole(HALF, D)] * 7 + [pl.BlockSpec((1, D, D), lambda i: (layer, 0, i))],
        out_specs=[whole(HALF, D), pl.BlockSpec((D, D), lambda i: (0, i))],
        out_shape=[shaped(HALF, D, BF), shaped(D, 3 * D, BF)],
        scratch_shapes=[pltpu.VMEM((HALF, D), F32), pltpu.VMEM((D, HALF), BF)],
        compiler_params=params(),
        cost_estimate=cost(4 * HALF * D * 3 * D, 10e6),
        name="project_back",
    )(stream, dq, dk, dv, dk_other, dv_other, dz, weights)


class Places:
    def __init__(self):
        self.ndp = lax.axis_size("dp")
        self.section = lax.axis_index("section")
        self.dp = lax.axis_index("dp")
        self.core = self.dp % 2

    def swap_core(self, block):
        return lax.ppermute(block, "dp", [(i, i ^ 1) for i in range(self.ndp)])

    def swap_section(self, block, step):
        return lax.ppermute(block, "section", [(i, i ^ step) for i in range(SECTIONS)])

    def send(self, block, route):
        pairs = []
        for s in range(SECTIONS):
            for d in range(self.ndp):
                to = route(s, d)
                if to is not None:
                    pairs.append((s * self.ndp + d, to[0] * self.ndp + to[1]))
        return lax.ppermute(block, ("section", "dp"), pairs)


def pick(stack, index):
    return lax.dynamic_index_in_dim(stack, index, 0, keepdims=False)


def tokens_in(places, block):
    pieces = block.reshape(4, HALF, D // SECTIONS)
    got = []
    for turn in range(4):

        def route(s, d, turn=turn):
            piece = s ^ turn
            return 2 * (d % 2) + piece // 2, d - d % 2 + piece % 2

        got.append(places.send(pick(pieces, places.section ^ turn), route))
    got = jnp.stack(got)
    mine = 2 * (places.section % 2) + places.core
    return jnp.concatenate([pick(got, mine ^ f) for f in range(SECTIONS)], axis=1)


def tokens_out(places, rows):
    features = jnp.stack(jnp.split(rows, SECTIONS, axis=1))
    mine = 2 * (places.section % 2) + places.core
    got = []
    for turn in range(4):

        def route(s, d, turn=turn):
            return (2 * (s % 2) + d % 2) ^ turn, d - d % 2 + s // 2

        got.append(places.send(pick(features, mine ^ turn), route))
    got = jnp.stack(got)
    return jnp.concatenate([pick(got, places.section ^ k) for k in range(4)], axis=0)


def weights_in(places, own):
    half = D // 2
    quarter = half // 2
    start = places.core * half
    mine = lax.dynamic_slice_in_dim(own, start, half, 0)
    from_x = places.swap_section(mine, 1)
    from_y = places.swap_section(mine, 2)
    diagonal = jnp.concatenate(
        [places.swap_section(from_x[:quarter], 2), places.swap_section(from_y[quarter:], 1)], axis=0
    )
    full = jnp.zeros((SECTIONS, D, 6 * D), BF)
    full = lax.dynamic_update_slice(full, own[None], (places.section, 0, 0))
    for step, piece in ((1, from_x), (2, from_y), (3, diagonal)):
        full = lax.dynamic_update_slice(full, piece[None], (places.section ^ step, start, 0))
        full = lax.dynamic_update_slice(
            full, places.swap_core(piece)[None], (places.section ^ step, half - start, 0)
        )
    return full


def reduce_columns(places, part, root, group):
    ndp = places.ndp
    blocks = part.reshape(D, ndp // 4, 2, 6 * D // ndp)
    keep = lax.dynamic_index_in_dim(blocks, places.core, 2, keepdims=False)
    give = lax.dynamic_index_in_dim(blocks, 1 - places.core, 2, keepdims=False)
    summed = keep + places.swap_core(give)
    half = D // 2

    def toward(block, step, second):
        if second:
            route = lambda s, d: (root, d) if s == root ^ step else None
        else:
            route = lambda s, d: (s ^ step, d) if (s ^ root) & step else None
        return block + places.send(block, route)

    upper = toward(toward(summed[:half], 1, False), 2, True)
    lower = toward(toward(summed[half:], 2, False), 1, True)
    summed = jnp.concatenate([upper, lower], axis=0)
    bit = 2
    while bit < ndp // 2:
        count = summed.shape[1]
        blocks = summed.reshape(D, count // 2, 2, summed.shape[2])
        mine = (places.dp // bit) % 2
        keep = lax.dynamic_index_in_dim(blocks, mine, 2, keepdims=False)
        give = lax.dynamic_index_in_dim(blocks, 1 - mine, 2, keepdims=False)
        route = lambda s, d, bit=bit: (s, d ^ bit) if s == root else None
        summed = keep + places.send(give, route)
        bit *= 2
    top = ndp // 2
    route = lambda s, d: (s, d ^ top) if s == root and (d // top) != group else None
    return (summed + places.send(summed, route)).reshape(D, 6 * D // ndp)


def on_device(
    stream_input,
    accum_input,
    section_weights,
    section_norms,
    final_norm,
    seq_lengths,
    out_cotangent,
):
    places = Places()
    section, core = places.section, places.core

    other_lengths = places.swap_core(seq_lengths)
    lengths = pick(jnp.where(core == section // 2, seq_lengths, other_lengths), section % 2)
    ending = jnp.cumsum(lengths, dtype=jnp.int32)

    def rows_of(which):
        spots = which * HALF + jnp.arange(HALF, dtype=jnp.int32)
        segment = jnp.sum(
            (spots[:, None] >= ending[None, :]).astype(jnp.int32), axis=1, dtype=jnp.int32
        )
        lane = jnp.arange(LANES, dtype=jnp.int32)
        hot = (segment[:, None] == lane[None, :]).astype(BF)
        alive = (spots < ending[-1]).astype(F32)
        return segment, hot, jnp.broadcast_to(alive[:, None], (HALF, LANES))

    segment_own, kseg_own, live = rows_of(core)
    _, kseg_other, _ = rows_of(1 - core)
    lane = jnp.arange(LANES, dtype=jnp.int32)
    qseg = jnp.where(
        (segment_own[:, None] != lane[None, :]) & (lane[None, :] < 32), -FAR, 0.0
    ).astype(BF)
    segs = (qseg, kseg_own, kseg_other)

    stream = tokens_in(places, stream_input)
    weights = weights_in(places, section_weights[0])
    small = jnp.concatenate([section_norms.reshape(2, D), final_norm.reshape(2, -1)], axis=1)
    small = lax.all_gather(small, "section", axis=0).astype(F32)
    norms = small[:, :, :D]
    final = jnp.concatenate([small[f, :, D:] for f in range(SECTIONS)], axis=1)
    accum = tokens_in(places, accum_input)
    cot = tokens_in(places, out_cotangent)

    branch_sum = jnp.zeros((HALF, D), F32)
    kept = []
    for layer in (0, 2):
        projected = project(stream, weights, layer)
        other_kv = places.swap_core(projected[:, D:])
        context, lse, middle, sum_a, branch_sum = attend(
            stream, projected, other_kv, segs, weights, layer, norms[layer], branch_sum
        )
        following, sum_f, branch_sum = feed(
            middle, weights, layer + 1, norms[layer + 1], branch_sum, BF if layer == 0 else F32
        )
        kept.append((stream, projected, other_kv, context, lse, sum_a, middle, sum_f))
        stream = following

    result, upstream, dy, final_grad = finish(stream, branch_sum, accum, cot, live, final)
    result_out = tokens_out(places, result)
    accum_out = tokens_out(places, dy.astype(BF))

    norm_grads = [None] * SECTIONS
    sums = {}
    for layer in (2, 0):
        entering, projected, other_kv, context, lse, sum_a, middle, sum_f = kept[layer // 2]
        upstream, dw1, dw2, norm_grads[layer + 1] = feed_back(
            middle, sum_f, upstream, dy, weights, layer + 1, norms[layer + 1]
        )
        odd = jnp.concatenate([dw1[:, 2 * D :], dw2], axis=1)
        sums[layer + 1, 0] = reduce_columns(places, odd[:, : 3 * D], layer + 1, 0)
        sums[layer + 1, 1] = reduce_columns(places, odd[:, 3 * D :], layer + 1, 1)
        dz, dctx, dwo, delta, norm_grads[layer] = outward_back(
            sum_a, upstream, dy, context, weights, layer, norms[layer]
        )
        sums[layer, 1] = reduce_columns(
            places, jnp.concatenate([dwo, dw1[:, : 2 * D]], axis=1), layer, 1
        )
        dq, dk_far, dv_far = scores_back(
            projected, other_kv, 0, dctx, qseg, kseg_other, lse, delta,
            jnp.zeros((HALF, D), F32), BF,
        )
        dk_other, dv_other = places.swap_core(dk_far), places.swap_core(dv_far)
        dq, dk, dv = scores_back(
            projected, projected, PAIRS, dctx, qseg, kseg_own, lse, delta, dq, F32
        )
        upstream, dqkv = project_back(
            entering, dq, dk, dv, dk_other, dv_other, dz, weights, layer
        )
        sums[layer, 0] = reduce_columns(places, dqkv, layer, 0)

    stream_out = tokens_out(places, upstream)
    small_grads = jnp.concatenate(norm_grads + [final_grad], axis=0)
    small_grads = lax.psum(small_grads, ("section", "dp"))
    norm_out = lax.dynamic_slice(
        small_grads, (2 * section, places.dp * (D // places.ndp)), (2, D // places.ndp)
    )
    width = D // SECTIONS
    final_out = lax.dynamic_slice(small_grads, (2 * SECTIONS, section * width), (2, width))

    group = places.dp // (places.ndp // 2)
    slab = jnp.zeros((D, 6 * D // places.ndp), BF)
    for (s, g), value in sums.items():
        slab = jnp.where((section == s) & (group == g), value, slab)

    return (
        result_out,
        stream_out.astype(F32),
        accum_out.astype(F32),
        slab.astype(F32)[None],
        norm_out[None],
        final_out,
    )


def solution(mesh):
    placed = (
        P("dp", "section"),
        P("dp", "section"),
        P("section", None, None),
        P("section", None, None),
        P(None, "section"),
        P("dp", None),
        P("dp", "section"),
    )
    return jax.shard_map(
        on_device,
        mesh=mesh,
        in_specs=placed,
        out_specs=(
            P("dp", "section"),
            P("dp", "section"),
            P("dp", "section"),
            P("section", None, "dp"),
            P("section", None, "dp"),
            P(None, "section"),
        ),
        check_vma=False,
    )
```

```python
import functools

import jax
import jax.numpy as jnp
from jax import lax
from jax.experimental import pallas as pl
from jax.experimental.pallas import tpu as pltpu
from jax.sharding import PartitionSpec as P

D = 512
HEADS = 8
HEAD = 64
PACK = 1024
HALF = PACK // 2
PAIRS = HEADS // 2
LANES = 2 * HEAD
SECTIONS = 4
FAR = 1e30
SCALE = HEAD ** (-0.5)
BF = jnp.bfloat16
F32 = jnp.float32
NT = (((1,), (1,)), ((), ()))
TN = (((0,), (0,)), ((), ()))


def mm(left, right):
    return jnp.dot(left, right, preferred_element_type=F32)


def mm_nt(left, right):
    return lax.dot_general(left, right, NT, preferred_element_type=F32)


def mm_tn(left, right):
    return lax.dot_general(left, right, TN, preferred_element_type=F32)


def params():
    return pltpu.CompilerParams(
        dimension_semantics=("arbitrary",), vmem_limit_bytes=48 * 1024 * 1024
    )


def shaped(rows, cols, dtype):
    return jax.ShapeDtypeStruct((rows, cols), dtype)


def whole(rows, cols):
    return pl.BlockSpec((rows, cols), lambda i: (0, 0))


def cost(flops, moved, transcendentals=0):
    return pl.CostEstimate(
        flops=int(flops), bytes_accessed=int(moved), transcendentals=int(transcendentals)
    )


def norm_parts(summed):
    average = jnp.mean(summed, axis=-1, keepdims=True)
    centered = summed - average
    spread = jnp.mean(centered * centered, axis=-1, keepdims=True)
    inverse = lax.rsqrt(spread + 1e-05)
    return centered * inverse, inverse


def norm_back(summed, gain, upstream):
    normal, inverse = norm_parts(summed)
    scaled = upstream * gain
    mean_one = jnp.mean(scaled, axis=-1, keepdims=True)
    mean_two = jnp.mean(scaled * normal, axis=-1, keepdims=True)
    grad = (scaled - mean_one - normal * mean_two) * inverse
    gain_grad = jnp.sum(upstream * normal, axis=0, keepdims=True)
    shift_grad = jnp.sum(upstream, axis=0, keepdims=True)
    return grad, gain_grad, shift_grad


def head_mask(which):
    lane = lax.broadcasted_iota(jnp.int32, (1, LANES), 1)
    return (lane // HEAD) == which


def three_way(column):
    high = column.astype(BF)
    rest = column - high.astype(F32)
    middle = rest.astype(BF)
    low = (rest - middle.astype(F32)).astype(BF)
    return high, middle, low


def project_kernel(x_ref, w_ref, q_ref, kv_ref):
    x = x_ref[...]
    q_ref[...] = mm(x, w_ref[0, :, :D]).astype(BF)
    keys = mm(x, w_ref[0, :, D : 2 * D]).astype(BF)
    values = mm(x, w_ref[0, :, 2 * D :]).astype(BF)
    for pair in range(PAIRS):
        lanes = slice(pair * LANES, (pair + 1) * LANES)
        kv_ref[pair, :, :LANES] = keys[:, lanes]
        kv_ref[pair, :, LANES:] = values[:, lanes]


def project(stream, near, layer):
    return pl.pallas_call(
        project_kernel,
        grid=(1,),
        in_specs=[
            whole(HALF, D),
            pl.BlockSpec((1, D, 3 * D), lambda i: (layer, 0, 0)),
        ],
        out_specs=[whole(HALF, D), pl.BlockSpec((PAIRS, HALF, 2 * LANES), lambda i: (0, 0, 0))],
        out_shape=[
            shaped(HALF, D, BF), jax.ShapeDtypeStruct((PAIRS, HALF, 2 * LANES), BF),
        ],
        compiler_params=params(),
        cost_estimate=cost(2 * HALF * D * 3 * D, 4e6),
        name="project",
    )(stream, near)


def attend_kernel(
    q_ref, own_ref, far_ref, qs_ref, kso_ref, ksx_ref, w_ref, x_ref, fsum_ref,
    norm_ref, ctx_ref, lse_ref, next_ref, sum_ref, fnew_ref, ctx_acc, lse_acc,
):
    pair = pl.program_id(0)
    q = q_ref[...] * jnp.asarray(SCALE, BF)
    keys_own = jnp.concatenate([own_ref[0, :, :LANES], kso_ref[...]], axis=1)
    keys_other = jnp.concatenate([far_ref[0, :, :LANES], ksx_ref[...]], axis=1)
    values_own, values_other = own_ref[0, :, LANES:], far_ref[0, :, LANES:]
    ones = jnp.ones((HALF, LANES), BF)
    none = jnp.zeros((), BF)
    lane = lax.broadcasted_iota(jnp.int32, (1, LANES), 1)
    context = jnp.zeros((HALF, LANES), F32)
    logs = jnp.where(pair == 0, jnp.zeros((HALF, LANES), F32), lse_acc[...])
    for which in range(2):
        mask = head_mask(which)
        query = jnp.concatenate([jnp.where(mask, q, none), qs_ref[...]], axis=1)
        score_own = mm_nt(query, keys_own)
        score_other = mm_nt(query, keys_other)
        peak = jnp.maximum(
            jnp.max(score_own, axis=1, keepdims=True), jnp.max(score_other, axis=1, keepdims=True)
        )
        own = jnp.exp(score_own - peak).astype(BF)
        other = jnp.exp(score_other - peak).astype(BF)
        total = mm(own, jnp.concatenate([jnp.where(mask, values_own, none), ones], axis=1)) + mm(
            other, jnp.concatenate([jnp.where(mask, values_other, none), ones], axis=1)
        )
        row_total = total[:, LANES:]
        context = context + total[:, :LANES] / row_total
        logs = jnp.where(lane == 2 * pair + which, peak + jnp.log(row_total), logs)
    lse_acc[...] = logs
    ctx_acc[pair] = context.astype(BF)
    ctx_ref[...] = context.astype(BF)

    @pl.when(pair == PAIRS - 1)
    def _():
        lse_ref[...] = lse_acc[...]
        full = jnp.concatenate([ctx_acc[k] for k in range(PAIRS)], axis=1)
        branch = mm(full, w_ref[0])
        summed = x_ref[...].astype(F32) + branch
        normal, _ = norm_parts(summed)
        moved = normal * norm_ref[0:1, :] + norm_ref[1:2, :]
        next_ref[...] = moved.astype(BF)
        sum_ref[...] = summed
        fnew_ref[...] = fsum_ref[...] + branch


def column():
    return pl.BlockSpec((HALF, LANES), lambda i: (0, i))


def pair_block():
    return pl.BlockSpec((1, HALF, 2 * LANES), lambda i: (i, 0, 0))


def attend(stream, queries, own_kv, far_kv, segs, near, layer, norms, branch_sum):
    qseg, kseg_own, kseg_other = segs
    return pl.pallas_call(
        attend_kernel,
        grid=(PAIRS,),
        in_specs=[
            column(), pair_block(), pair_block(),
            whole(HALF, LANES), whole(HALF, LANES), whole(HALF, LANES),
            pl.BlockSpec((1, D, D), lambda i: (layer, 0, 3)),
            whole(HALF, D), whole(HALF, D), whole(2, D),
        ],
        out_specs=[
            column(), whole(HALF, LANES), whole(HALF, D), whole(HALF, D), whole(HALF, D),
        ],
        out_shape=[
            shaped(HALF, D, BF), shaped(HALF, LANES, F32), shaped(HALF, D, BF),
            shaped(HALF, D, F32), shaped(HALF, D, F32),
        ],
        scratch_shapes=[pltpu.VMEM((PAIRS, HALF, LANES), BF), pltpu.VMEM((HALF, LANES), F32)],
        compiler_params=params(),
        cost_estimate=cost(8e9, 8e6, 4e6),
        name="attend",
    )(
        queries, own_kv, far_kv, qseg, kseg_own, kseg_other, near, stream, branch_sum, norms,
    )


def gelu_parts(v):
    root = 0.7978845608028654
    squared = v * v
    inner = root * (v + 0.044715 * v * squared)
    t = jnp.tanh(inner)
    hidden = 0.5 * v * (1.0 + t)
    slope = 0.5 * (1.0 + t) + 0.5 * v * (1.0 - t * t) * (root * (1.0 + 3 * 0.044715 * squared))
    return hidden, slope


def feed_specs(layer):
    return [
        pl.BlockSpec((1, D, D), lambda i: (layer - 1, 0, i)),
        pl.BlockSpec((1, D, D), lambda i: (layer, 0, 2 + i)),
        pl.BlockSpec((1, D, D), lambda i: (layer, 0, i)),
        pl.BlockSpec((1, D, D), lambda i: (layer, 0, i)),
    ]


def feed_kernel(
    x_ref, in_a_ref, out_a_ref, in_b_ref, out_b_ref, fsum_ref, norm_ref,
    next_ref, sum_ref, fnew_ref, acc_ref,
):
    step = pl.program_id(0)
    x = x_ref[...]
    hidden_a = gelu_parts(mm(x, in_a_ref[0]))[0].astype(BF)
    hidden_b = gelu_parts(mm(x, in_b_ref[0]))[0].astype(BF)
    part = mm_nt(hidden_a, out_a_ref[0]) + mm_nt(hidden_b, out_b_ref[0])

    @pl.when(step == 0)
    def _():
        acc_ref[...] = part

    @pl.when(step == 1)
    def _():
        branch = acc_ref[...] + part
        summed = x_ref[...].astype(F32) + branch
        normal, _ = norm_parts(summed)
        moved = normal * norm_ref[0:1, :] + norm_ref[1:2, :]
        next_ref[...] = moved.astype(next_ref.dtype)
        sum_ref[...] = summed
        fnew_ref[...] = fsum_ref[...] + branch


def feed(stream, near, late, layer, norms, branch_sum, out_type):
    return pl.pallas_call(
        feed_kernel,
        grid=(2,),
        in_specs=[whole(HALF, D), *feed_specs(layer), whole(HALF, D), whole(2, D)],
        out_specs=[whole(HALF, D), whole(HALF, D), whole(HALF, D)],
        out_shape=[shaped(HALF, D, out_type), shaped(HALF, D, F32), shaped(HALF, D, F32)],
        scratch_shapes=[pltpu.VMEM((HALF, D), F32)],
        compiler_params=params(),
        cost_estimate=cost(4 * HALF * D * 4 * D, 8e6, HALF * 4 * D),
        name="feed",
    )(stream, late, near, near, late, branch_sum, norms)


def finish_kernel(
    x_ref, fsum_ref, y_ref, cot_ref, live_ref, norm_ref, out_ref, low_ref, c_ref, dy_ref, grad_ref
):
    summed = y_ref[...].astype(F32) + fsum_ref[...]
    normal, _ = norm_parts(summed)
    gain = norm_ref[0:1, :]
    out_ref[...] = (x_ref[...] + normal * gain + norm_ref[1:2, :]).astype(BF)
    cot = cot_ref[...].astype(F32) * live_ref[:, 0:1]
    c_ref[...] = cot
    grad, gain_grad, shift_grad = norm_back(summed, gain, cot)
    dy_ref[...] = grad
    low_ref[...] = grad.astype(BF)
    grad_ref[0:1, :] = gain_grad
    grad_ref[1:2, :] = shift_grad


def finish(last, branch_sum, accum, cot, live, norms):
    return pl.pallas_call(
        finish_kernel,
        grid=(1,),
        in_specs=[
            whole(HALF, D), whole(HALF, D), whole(HALF, D), whole(HALF, D), whole(HALF, LANES),
            whole(2, D),
        ],
        out_specs=[whole(HALF, D)] * 4 + [whole(2, D)],
        out_shape=[
            shaped(HALF, D, BF), shaped(HALF, D, BF), shaped(HALF, D, F32), shaped(HALF, D, F32),
            shaped(2, D, F32),
        ],
        compiler_params=params(),
        cost_estimate=cost(1e7, 6e6),
        name="finish",
    )(last, branch_sum, accum, cot, live, norms)


def feed_back_kernel(
    x_ref, sum_ref, up_ref, dy_ref, in_a_ref, out_a_ref, in_b_ref, out_b_ref, norm_ref,
    dx_ref, odd_ref, even_ref, grad_ref, acc_ref, df_ref,
):
    step = pl.program_id(0)

    @pl.when(step == 0)
    def _():
        grad, gain_grad, shift_grad = norm_back(
            sum_ref[...], norm_ref[0:1, :], up_ref[...].astype(F32)
        )
        grad_ref[0:1, :] = gain_grad
        grad_ref[1:2, :] = shift_grad
        acc_ref[...] = grad
        df_ref[...] = (grad + dy_ref[...]).astype(BF)

    x = x_ref[...]
    df = df_ref[...]

    def chunk(inner, outer):
        hidden, slope = gelu_parts(mm(x, inner))
        outer_grad = mm_tn(hidden.astype(BF), df).astype(BF)
        preact_grad = (mm(df, outer) * slope).astype(BF)
        inner_grad = mm_tn(preact_grad, x).astype(BF)
        return inner_grad, outer_grad, mm_nt(preact_grad, inner)

    inner_grad, outer_grad, back_a = chunk(in_a_ref[0], out_a_ref[0])
    even_ref[...] = inner_grad
    odd_ref[1, 0] = outer_grad
    inner_grad, outer_grad, back_b = chunk(in_b_ref[0], out_b_ref[0])
    odd_ref[0, 0] = inner_grad
    odd_ref[2, 0] = outer_grad
    total = acc_ref[...] + (back_a + back_b)
    acc_ref[...] = total

    @pl.when(step == 1)
    def _():
        dx_ref[...] = total.astype(BF)


def feed_back(stream, summed, upstream, dy, near, late, layer, norms):
    dx, odd, even, grads = pl.pallas_call(
        feed_back_kernel,
        grid=(2,),
        in_specs=[
            whole(HALF, D), whole(HALF, D), whole(HALF, D), whole(HALF, D),
            *feed_specs(layer), whole(2, D),
        ],
        out_specs=[
            whole(HALF, D),
            pl.BlockSpec((3, 1, D, D), lambda i: (0, i, 0, 0)),
            pl.BlockSpec((D, D), lambda i: (i, 0)),
            whole(2, D),
        ],
        out_shape=[
            shaped(HALF, D, BF), jax.ShapeDtypeStruct((3, 2, D, D), BF), shaped(2 * D, D, BF),
            shaped(2, D, F32),
        ],
        scratch_shapes=[pltpu.VMEM((HALF, D), F32), pltpu.VMEM((HALF, D), BF)],
        compiler_params=params(),
        cost_estimate=cost(10 * HALF * D * 4 * D, 16e6, HALF * 4 * D),
        name="feed_back",
    )(stream, summed, upstream, dy, late, near, near, late, norms)
    return dx, odd.reshape(6 * D, D), even, grads


def outward_back_kernel(
    sum_ref, up_ref, dy_ref, ctx_ref, w_ref, norm_ref, dz_ref, dctx_ref, dwo_ref, delta_ref,
    grad_ref,
):
    grad, gain_grad, shift_grad = norm_back(sum_ref[...], norm_ref[0:1, :], up_ref[...].astype(F32))
    grad_ref[0:1, :] = gain_grad
    grad_ref[1:2, :] = shift_grad
    dz_ref[...] = grad
    df = (grad + dy_ref[...]).astype(BF)
    context = ctx_ref[...]
    dwo_ref[...] = mm_tn(df, context).astype(BF)
    context_grad = mm_nt(df, w_ref[0]).astype(BF)
    dctx_ref[...] = context_grad
    product = context.astype(F32) * context_grad.astype(F32)
    lane = lax.broadcasted_iota(jnp.int32, (1, LANES), 1)
    delta = jnp.zeros((HALF, LANES), F32)
    for head in range(HEADS):
        part = product[:, (head // 2) * LANES : (head // 2 + 1) * LANES]
        inner = jnp.sum(jnp.where(head_mask(head % 2), part, 0.0), axis=1, keepdims=True)
        delta = jnp.where(lane == head, inner, delta)
    delta_ref[...] = delta


def outward_back(summed, upstream, dy, context, near, layer, norms):
    return pl.pallas_call(
        outward_back_kernel,
        grid=(1,),
        in_specs=[
            whole(HALF, D), whole(HALF, D), whole(HALF, D), whole(HALF, D),
            pl.BlockSpec((1, D, D), lambda i: (layer, 0, 3)), whole(2, D),
        ],
        out_specs=[
            whole(HALF, D), whole(HALF, D), whole(D, D), whole(HALF, LANES), whole(2, D),
        ],
        out_shape=[
            shaped(HALF, D, F32), shaped(HALF, D, BF), shaped(D, D, BF), shaped(HALF, LANES, F32),
            shaped(2, D, F32),
        ],
        compiler_params=params(),
        cost_estimate=cost(4 * HALF * D * D, 6e6),
        name="outward_back",
    )(summed, upstream, dy, context, near, norms)


def scores_back_kernel(
    q_ref, kv_ref, dctx_ref, qs_ref, ks_ref, lse_ref, delta_ref, before_ref, dq_ref, dkv_ref
):
    pair = pl.program_id(0)
    none = jnp.zeros((), BF)
    lane = lax.broadcasted_iota(jnp.int32, (1, LANES), 1)
    q = q_ref[...] * jnp.asarray(SCALE, BF)
    k = kv_ref[0, :, :LANES]
    k_scaled = k * jnp.asarray(SCALE, BF)
    dctx = dctx_ref[...]
    extra = jnp.where((lane >= LANES - 3), jnp.ones((), BF), none)
    keys = jnp.concatenate([k, ks_ref[...] + extra], axis=1)
    values = jnp.concatenate(
        [kv_ref[0, :, LANES:], jnp.broadcast_to(extra, (HALF, LANES))], axis=1
    )
    dq = before_ref[...]
    dk = jnp.zeros((HALF, LANES), F32)
    dv = jnp.zeros((HALF, LANES), F32)
    for which in range(2):
        mask = head_mask(which)
        here = lane == 2 * pair + which

        def lanes_of(table, base):
            column = -jnp.sum(jnp.where(here, table, 0.0), axis=1, keepdims=True)
            high, middle, low = three_way(column)
            base = jnp.where(lane == LANES - 3, high, base)
            base = jnp.where(lane == LANES - 2, middle, base)
            return jnp.where(lane == LANES - 1, low, base)

        query_part = jnp.where(mask, q, none)
        dctx_part = jnp.where(mask, dctx, none)
        query = jnp.concatenate([query_part, lanes_of(lse_ref[...], qs_ref[...])], axis=1)
        dcontext = jnp.concatenate(
            [dctx_part, lanes_of(delta_ref[...], jnp.zeros((HALF, LANES), BF))], axis=1
        )
        probability = jnp.exp(mm_nt(keys, query))
        score_grad = (probability * mm_nt(values, dcontext)).astype(BF)
        dv = dv + mm(probability.astype(BF), dctx_part)
        dk = dk + mm(score_grad, query_part)
        dq = dq + mm_tn(score_grad, jnp.where(mask, k_scaled, none))
    dq_ref[...] = dq
    dkv_ref[0, :, :LANES] = dk.astype(dkv_ref.dtype)
    dkv_ref[0, :, LANES:] = dv.astype(dkv_ref.dtype)


def scores_back(queries, kv, dctx, qseg, kseg, lse, delta, before, out_type):
    return pl.pallas_call(
        scores_back_kernel,
        grid=(PAIRS,),
        in_specs=[
            column(), pair_block(), column(),
            whole(HALF, LANES), whole(HALF, LANES), whole(HALF, LANES), whole(HALF, LANES),
            column(),
        ],
        out_specs=[column(), pair_block()],
        out_shape=[
            shaped(HALF, D, F32), jax.ShapeDtypeStruct((PAIRS, HALF, 2 * LANES), out_type),
        ],
        compiler_params=params(),
        cost_estimate=cost(8e9, 8e6, 2e6),
        name="scores_back",
    )(queries, kv, dctx, qseg, kseg, lse, delta, before)


def project_back_kernel(
    x_ref, dq_ref, dkv_ref, far_ref, dz_ref, w_ref, dx_ref, dw_ref
):
    x = x_ref[...]
    parts = [(dkv_ref[k] + far_ref[k].astype(F32)).astype(BF) for k in range(PAIRS)]
    dk = jnp.concatenate([part[:, :LANES] for part in parts], axis=1)
    dv = jnp.concatenate([part[:, LANES:] for part in parts], axis=1)
    total = dz_ref[...]
    for place, grad in enumerate((dq_ref[...].astype(BF), dk, dv)):
        dw_ref[place * D : (place + 1) * D] = mm_tn(grad, x).astype(BF)
        total = total + mm_nt(grad, w_ref[0, :, place * D : (place + 1) * D])
    dx_ref[...] = total.astype(BF)


def project_back(stream, dq, dkv, far, dz, near, layer):
    pairs = pl.BlockSpec((PAIRS, HALF, 2 * LANES), lambda i: (0, 0, 0))
    return pl.pallas_call(
        project_back_kernel,
        grid=(1,),
        in_specs=[
            whole(HALF, D), whole(HALF, D), pairs, pairs, whole(HALF, D),
            pl.BlockSpec((1, D, 3 * D), lambda i: (layer, 0, 0)),
        ],
        out_specs=[whole(HALF, D), whole(3 * D, D)],
        out_shape=[shaped(HALF, D, BF), shaped(3 * D, D, BF)],
        compiler_params=params(),
        cost_estimate=cost(4 * HALF * D * 3 * D, 10e6),
        name="project_back",
    )(stream, dq, dkv, far, dz, near)


class Places:
    def __init__(self):
        self.ndp = lax.axis_size("dp")
        self.section = lax.axis_index("section")
        self.dp = lax.axis_index("dp")
        self.core = self.dp % 2

    def swap_dp(self, block, step):
        return lax.ppermute(block, "dp", [(i, i ^ step) for i in range(self.ndp)])

    def swap_core(self, block):
        return self.swap_dp(block, 1)

    def swap_section(self, block, step):
        return lax.ppermute(block, "section", [(i, i ^ step) for i in range(SECTIONS)])

    def send(self, block, route):
        pairs = []
        for s in range(SECTIONS):
            for d in range(self.ndp):
                to = route(s, d)
                pairs.append((s * self.ndp + d, to[0] * self.ndp + to[1]))
        return lax.ppermute(block, ("section", "dp"), pairs)


def pick(stack, index):
    return lax.dynamic_index_in_dim(stack, index, 0, keepdims=False)


def after(value, *earlier):
    return lax.optimization_barrier((value, *earlier))[0]


def tokens_in(places, block):
    several = block.shape[0]
    width = D // SECTIONS
    pieces = jnp.swapaxes(block.reshape(several, 4, HALF, width), 0, 1)
    got = []
    for turn in range(4):

        def route(s, d, turn=turn):
            piece = s ^ turn
            return 2 * (d % 2) + piece // 2, d - d % 2 + piece % 2

        got.append(places.send(pick(pieces, places.section ^ turn), route))
    got = jnp.stack(got)
    mine = 2 * (places.section % 2) + places.core
    return jnp.concatenate([pick(got, mine ^ f) for f in range(SECTIONS)], axis=2)


def tokens_out(places, rows):
    several = rows.shape[0]
    features = jnp.stack(jnp.split(rows, SECTIONS, axis=2))
    mine = 2 * (places.section % 2) + places.core
    got = []
    for turn in range(4):

        def route(s, d, turn=turn):
            return (2 * (s % 2) + d % 2) ^ turn, d - d % 2 + s // 2

        got.append(places.send(pick(features, mine ^ turn), route))
    got = jnp.stack(got)
    return jnp.concatenate([pick(got, places.section ^ k) for k in range(4)], axis=1)


def gather_start(places, mine):
    half = D // 4
    from_x = places.swap_section(mine, 1)
    from_y = places.swap_section(mine, 2)
    upper = places.swap_section(from_x[:half], 2)
    lower = places.swap_section(from_y[half:], 1)
    return from_x, from_y, upper, lower


def place_kernel(columns, spot_ref, own_ref, out_ref, sem):
    copy = pltpu.make_async_copy(own_ref.at[:, columns], out_ref.at[spot_ref[0]], sem)
    copy.start()
    copy.wait()


def place_own(places, own, columns):
    return pl.pallas_call(
        functools.partial(place_kernel, columns),
        in_specs=[
            pl.BlockSpec(memory_space=pltpu.SMEM), pl.BlockSpec(memory_space=pl.ANY),
        ],
        out_specs=pl.BlockSpec(memory_space=pl.ANY),
        out_shape=jax.ShapeDtypeStruct((SECTIONS, D, columns.stop - columns.start), BF),
        scratch_shapes=[pltpu.SemaphoreType.DMA],
        cost_estimate=cost(0, 4e6),
        name="place_own",
    )(places.section.reshape(1).astype(jnp.int32), own)


def gather_finish(places, full, pieces):
    half = D // 2
    from_x, from_y, upper, lower = pieces
    start = places.core * half

    def put(full, piece, step, offset):
        spot = places.section ^ step
        far = places.swap_core(piece)
        full = lax.dynamic_update_slice(full, piece[None], (spot, start + offset, 0))
        return lax.dynamic_update_slice(full, far[None], (spot, half - start + offset, 0))

    full = put(full, from_x[:half], 1, 0)
    full = put(full, from_y[:half], 2, 0)
    full = put(full, upper, 3, 0)
    return put(full, lower[: half // 2], 3, half // 2)


def norm_rows(places, norm_grads, final_grad):
    ndp = places.ndp
    cut = jnp.moveaxis(norm_grads.reshape(2, ndp, D // ndp), 1, 0).reshape(ndp, 2 * D // ndp)
    shared = jnp.broadcast_to(final_grad.reshape(1, -1), (ndp, 2 * D // SECTIONS))
    row = jnp.concatenate([cut, shared], axis=1)
    return jnp.pad(row[:, None], ((0, 0), (0, 15), (0, D - row.shape[1]))).astype(BF)


def core_sums(places, rows, extra):
    ndp = places.ndp
    blocks = rows.reshape(ndp // 2, 2, -1, D)
    extra = extra.reshape(ndp // 2, 2, -1, D)

    def of(parity):
        return jnp.concatenate(
            [
                lax.dynamic_index_in_dim(blocks, parity, 1, keepdims=False),
                lax.dynamic_index_in_dim(extra, parity, 1, keepdims=False),
            ],
            axis=1,
        )

    return of(places.core) + places.swap_core(of(1 - places.core))


def reduce_sections(places, sums):
    section = places.section
    cut = max(16, sums[0].shape[1] // 32 * 16)
    stack = jnp.stack(sums)
    near, over_x, over_y, far = (pick(stack, section ^ step) for step in range(4))
    got = places.swap_section(jnp.stack([over_x[:, :cut], far[:, :cut]]), 1)
    upper, upper_y = near[:, :cut] + got[0], over_y[:, :cut] + got[1]
    got = places.swap_section(jnp.stack([over_y[:, cut:], far[:, cut:]]), 2)
    lower, lower_x = near[:, cut:] + got[0], over_x[:, cut:] + got[1]
    upper = upper + places.swap_section(upper_y, 2)
    lower = lower + places.swap_section(lower_x, 1)
    blocks = jnp.concatenate([upper, lower], axis=1)
    total = blocks.shape[0]
    place = places.dp // 2
    if total <= 4:
        got = [pick(blocks, place)]
        for step in range(1, total):
            got.append(places.swap_dp(pick(blocks, place ^ step), 2 * step))
        got = jnp.stack(got)
        out = pick(got, place).astype(F32)
        for spot in range(1, total):
            out = out + pick(got, place ^ spot).astype(F32)
        return out
    bit = total // 2
    while bit:
        blocks = blocks.reshape(2, bit, *blocks.shape[1:])
        mine = (place // bit) % 2
        blocks = pick(blocks, mine) + places.swap_dp(pick(blocks, 1 - mine), 2 * bit)
        bit //= 2
    return blocks[0].astype(F32)


def on_device(
    stream_input,
    accum_input,
    section_weights,
    section_norms,
    final_norm,
    seq_lengths,
    out_cotangent,
):
    places = Places()
    section, core = places.section, places.core
    width = D // SECTIONS
    rows = D // 2

    stream = tokens_in(places, stream_input[None])[0]
    own = section_weights[0]
    small = jnp.concatenate(
        [section_norms[0, 0], section_norms[0, 1], final_norm[0], final_norm[1]], axis=0
    )
    small = jnp.pad(small[None], ((0, 15), (0, 4 * D - small.shape[0])))
    near_own, late_own = own[:, : 4 * D], own[:, 4 * D :]
    mine = lax.dynamic_slice(near_own, (core * rows, 0), (rows, 4 * D))
    near_pieces = gather_start(places, jnp.concatenate([mine, small], axis=0))
    late_mine = after(
        lax.dynamic_slice(late_own, (core * rows, 0), (rows, 2 * D)), near_pieces[0], near_pieces[1]
    )
    late_pieces = gather_start(places, late_mine)
    near = gather_finish(places, place_own(places, own, slice(0, 4 * D)), near_pieces)
    late = gather_finish(places, place_own(places, own, slice(4 * D, 6 * D)), late_pieces)
    tail = jnp.stack(
        [small, near_pieces[0][rows:], near_pieces[1][rows:], near_pieces[3][rows // 2 :]]
    )[:, 0].astype(F32)
    tail = jnp.stack([pick(tail, section ^ j) for j in range(SECTIONS)])
    norms = tail[:, : 2 * D].reshape(SECTIONS, 2, D)
    final = jnp.moveaxis(tail[:, 2 * D : 2 * D + 2 * width].reshape(SECTIONS, 2, width), 0, 1)
    final = final.reshape(2, D)

    other_lengths = places.swap_core(seq_lengths)
    lengths = pick(jnp.where(core == section // 2, seq_lengths, other_lengths), section % 2)
    ending = jnp.cumsum(lengths, dtype=jnp.int32)

    def rows_of(which):
        spots = which * HALF + jnp.arange(HALF, dtype=jnp.int32)
        segment = jnp.sum(
            (spots[:, None] >= ending[None, :]).astype(jnp.int32), axis=1, dtype=jnp.int32
        )
        lane = jnp.arange(LANES, dtype=jnp.int32)
        hot = (segment[:, None] == lane[None, :]).astype(BF)
        alive = (spots < ending[-1]).astype(F32)
        return segment, hot, jnp.broadcast_to(alive[:, None], (HALF, LANES))

    segment_own, kseg_own, live = rows_of(core)
    _, kseg_other, _ = rows_of(1 - core)
    lane = jnp.arange(LANES, dtype=jnp.int32)
    qseg = jnp.where(
        (segment_own[:, None] != lane[None, :]) & (lane[None, :] < 32), -FAR, 0.0
    ).astype(BF)
    segs = (qseg, kseg_own, kseg_other)

    both = after(jnp.stack([accum_input, out_cotangent]), late_pieces[2], late_pieces[3])
    accum, cot = tokens_in(places, both)

    branch_sum = jnp.zeros((HALF, D), F32)
    kept = []
    for layer in (0, 2):
        queries, own_kv = project(stream, near, layer)
        far_kv = places.swap_core(own_kv)
        context, lse, middle, sum_a, branch_sum = attend(
            stream, queries, own_kv, far_kv, segs, near, layer, norms[layer], branch_sum
        )
        following, sum_f, branch_sum = feed(
            middle, near, late, layer + 1, norms[layer + 1], branch_sum, BF if layer == 0 else F32
        )
        kept.append((stream, queries, own_kv, far_kv, context, lse, sum_a, middle, sum_f))
        stream = following

    result, dy_low, upstream, dy, final_grad = finish(stream, branch_sum, accum, cot, live, final)
    result_out, accum_out = tokens_out(places, jnp.stack([result, dy_low]))

    sums = [None] * SECTIONS

    def extra(layer, grads):
        return norm_rows(places, grads, final_grad[:, layer * width : (layer + 1) * width])

    for layer in (2, 0):
        entering, queries, own_kv, far_kv, context, lse, sum_a, middle, sum_f = kept[layer // 2]
        upstream, odd, even, grads = feed_back(
            middle, sum_f, upstream, dy, near, late, layer + 1, norms[layer + 1]
        )
        sums[layer + 1] = core_sums(places, odd, extra(layer + 1, grads))
        dz, dctx, dwo, delta, grads = outward_back(
            sum_a, upstream, dy, context, near, layer, norms[layer]
        )
        dq, dkv_far = scores_back(
            queries, far_kv, dctx, qseg, segs[2], lse, delta, jnp.zeros((HALF, D), F32), BF
        )
        from_far = places.swap_core(dkv_far)
        dq, dkv = scores_back(queries, own_kv, dctx, qseg, segs[1], lse, delta, dq, F32)
        upstream, dqkv = project_back(entering, dq, dkv, from_far, dz, near, layer)
        sums[layer] = core_sums(
            places, jnp.concatenate([dqkv, dwo, even], axis=0), extra(layer, grads)
        )

    reduced = reduce_sections(places, sums)
    block = 6 * D // places.ndp
    slab = reduced[:block].T
    small_out = reduced[block]
    cut = D // places.ndp
    norm_out = small_out[: 2 * cut].reshape(2, cut)
    final_out = small_out[2 * cut : 2 * cut + 2 * width].reshape(2, width)
    stream_out = tokens_out(places, upstream[None])[0]

    return (
        result_out,
        stream_out.astype(F32),
        accum_out.astype(F32),
        slab[None],
        norm_out[None],
        final_out,
    )


def solution(mesh):
    placed = (
        P("dp", "section"),
        P("dp", "section"),
        P("section", None, None),
        P("section", None, None),
        P(None, "section"),
        P("dp", None),
        P("dp", "section"),
    )
    return jax.shard_map(
        on_device,
        mesh=mesh,
        in_specs=placed,
        out_specs=(
            P("dp", "section"),
            P("dp", "section"),
            P("dp", "section"),
            P("section", None, "dp"),
            P("section", None, "dp"),
            P(None, "section"),
        ),
        check_vma=False,
    )
```

```python
import functools
import math

import jax
import jax.numpy as jnp
from jax import lax
from jax.experimental import pallas as pl
from jax.experimental.pallas import tpu as pltpu
from jax.sharding import PartitionSpec as P

D = 512
HEADS = 8
HEAD = 64
PACK = 1024
HALF = PACK // 2
PAIRS = HEADS // 2
LANES = 2 * HEAD
SECTIONS = 4
FAR = 1e30
SCALE = HEAD ** (-0.5)
BF = jnp.bfloat16
F32 = jnp.float32
NT = (((1,), (1,)), ((), ()))
TN = (((0,), (0,)), ((), ()))


def mm(left, right):
    return jnp.dot(left, right, preferred_element_type=F32)


def mm_nt(left, right):
    return lax.dot_general(left, right, NT, preferred_element_type=F32)


def mm_tn(left, right):
    return lax.dot_general(left, right, TN, preferred_element_type=F32)


def params():
    return pltpu.CompilerParams(
        dimension_semantics=("arbitrary",), vmem_limit_bytes=32 * 1024 * 1024
    )


def shaped(rows, cols, dtype):
    return jax.ShapeDtypeStruct((rows, cols), dtype)


def whole(rows, cols):
    return pl.BlockSpec((rows, cols), lambda i: (0, 0))


def cost(flops, moved, transcendentals=0):
    return pl.CostEstimate(
        flops=int(flops), bytes_accessed=int(moved), transcendentals=int(transcendentals)
    )


def gain_of(table_ref, layer):
    return table_ref[layer : layer + 1, :D]


def shift_of(table_ref, layer):
    return table_ref[layer : layer + 1, D : 2 * D]


def norm_parts(summed):
    average = jnp.mean(summed, axis=-1, keepdims=True)
    centered = summed - average
    spread = jnp.mean(centered * centered, axis=-1, keepdims=True)
    inverse = lax.rsqrt(spread + 1e-05)
    return centered * inverse, inverse


def norm_back(summed, gain, upstream):
    normal, inverse = norm_parts(summed)
    scaled = upstream * gain
    mean_one = jnp.mean(scaled, axis=-1, keepdims=True)
    mean_two = jnp.mean(scaled * normal, axis=-1, keepdims=True)
    grad = (scaled - mean_one - normal * mean_two) * inverse
    gain_grad = jnp.sum(upstream * normal, axis=0, keepdims=True)
    shift_grad = jnp.sum(upstream, axis=0, keepdims=True)
    return grad, gain_grad, shift_grad


def head_mask(which):
    lane = lax.broadcasted_iota(jnp.int32, (1, LANES), 1)
    return (lane // HEAD) == which


def three_way(column):
    high = column.astype(BF)
    rest = column - high.astype(F32)
    middle = rest.astype(BF)
    low = (rest - middle.astype(F32)).astype(BF)
    return high, middle, low


def project_kernel(x_ref, w_ref, q_ref, kv_ref):
    x = x_ref[...]
    q_ref[...] = mm(x, w_ref[0, :, :D]).astype(BF)
    keys = mm(x, w_ref[0, :, D : 2 * D]).astype(BF)
    values = mm(x, w_ref[0, :, 2 * D :]).astype(BF)
    for pair in range(PAIRS):
        lanes = slice(pair * LANES, (pair + 1) * LANES)
        kv_ref[pair, :, :LANES] = keys[:, lanes]
        kv_ref[pair, :, LANES:] = values[:, lanes]


def project(stream, near, layer):
    return pl.pallas_call(
        project_kernel,
        grid=(1,),
        in_specs=[
            whole(HALF, D),
            pl.BlockSpec((1, D, 3 * D), lambda i: (layer, 0, 0)),
        ],
        out_specs=[whole(HALF, D), pl.BlockSpec((PAIRS, HALF, 2 * LANES), lambda i: (0, 0, 0))],
        out_shape=[
            shaped(HALF, D, BF), jax.ShapeDtypeStruct((PAIRS, HALF, 2 * LANES), BF),
        ],
        compiler_params=params(),
        cost_estimate=cost(2 * HALF * D * 3 * D, 4e6),
        name="project",
    )(stream, near)


def attend_kernel(
    layer, q_ref, own_ref, far_ref, qs_ref, kso_ref, ksx_ref, w_ref, x_ref, fsum_ref,
    norm_ref, ctx_ref, lse_ref, next_ref, sum_ref, fnew_ref, ctx_acc, lse_acc,
):
    pair = pl.program_id(0)
    q = q_ref[...] * jnp.asarray(SCALE, BF)
    keys_own = jnp.concatenate([own_ref[0, :, :LANES], kso_ref[...]], axis=1)
    keys_other = jnp.concatenate([far_ref[0, :, :LANES], ksx_ref[...]], axis=1)
    values_own, values_other = own_ref[0, :, LANES:], far_ref[0, :, LANES:]
    ones = jnp.ones((HALF, LANES), BF)
    none = jnp.zeros((), BF)
    lane = lax.broadcasted_iota(jnp.int32, (1, LANES), 1)
    context = jnp.zeros((HALF, LANES), F32)
    logs = jnp.where(pair == 0, jnp.zeros((HALF, LANES), F32), lse_acc[...])
    for which in range(2):
        mask = head_mask(which)
        query = jnp.concatenate([jnp.where(mask, q, none), qs_ref[...]], axis=1)
        score_own = mm_nt(query, keys_own)
        score_other = mm_nt(query, keys_other)
        peak = jnp.maximum(
            jnp.max(score_own, axis=1, keepdims=True), jnp.max(score_other, axis=1, keepdims=True)
        )
        own = jnp.exp(score_own - peak).astype(BF)
        other = jnp.exp(score_other - peak).astype(BF)
        total = mm(own, jnp.concatenate([jnp.where(mask, values_own, none), ones], axis=1)) + mm(
            other, jnp.concatenate([jnp.where(mask, values_other, none), ones], axis=1)
        )
        row_total = total[:, LANES:]
        context = context + total[:, :LANES] / row_total
        logs = jnp.where(lane == 2 * pair + which, peak + jnp.log(row_total), logs)
    lse_acc[...] = logs
    ctx_acc[pair] = context.astype(BF)
    ctx_ref[...] = context.astype(BF)

    @pl.when(pair == PAIRS - 1)
    def _():
        lse_ref[...] = lse_acc[...]
        full = jnp.concatenate([ctx_acc[k] for k in range(PAIRS)], axis=1)
        branch = mm(full, w_ref[0])
        summed = x_ref[...].astype(F32) + branch
        normal, _ = norm_parts(summed)
        moved = normal * gain_of(norm_ref, layer) + shift_of(norm_ref, layer)
        next_ref[...] = moved.astype(BF)
        sum_ref[...] = summed
        fnew_ref[...] = fsum_ref[...] + branch


def column():
    return pl.BlockSpec((HALF, LANES), lambda i: (0, i))


def pair_block():
    return pl.BlockSpec((1, HALF, 2 * LANES), lambda i: (i, 0, 0))


def attend(stream, queries, own_kv, far_kv, segs, near, layer, norms, branch_sum):
    qseg, kseg_own, kseg_other = segs
    return pl.pallas_call(
        functools.partial(attend_kernel, layer),
        grid=(PAIRS,),
        in_specs=[
            column(), pair_block(), pair_block(),
            whole(HALF, LANES), whole(HALF, LANES), whole(HALF, LANES),
            pl.BlockSpec((1, D, D), lambda i: (layer, 0, 3)),
            whole(HALF, D), whole(HALF, D), whole(SECTIONS, 4 * D),
        ],
        out_specs=[
            column(), whole(HALF, LANES), whole(HALF, D), whole(HALF, D), whole(HALF, D),
        ],
        out_shape=[
            shaped(HALF, D, BF), shaped(HALF, LANES, F32), shaped(HALF, D, BF),
            shaped(HALF, D, F32), shaped(HALF, D, F32),
        ],
        scratch_shapes=[pltpu.VMEM((PAIRS, HALF, LANES), BF), pltpu.VMEM((HALF, LANES), F32)],
        compiler_params=params(),
        cost_estimate=cost(8e9, 8e6, 4e6),
        name="attend",
    )(
        queries, own_kv, far_kv, qseg, kseg_own, kseg_other, near, stream, branch_sum, norms,
    )


def gelu_parts(v):
    root = 0.7978845608028654
    squared = v * v
    inner = root * (v + 0.044715 * v * squared)
    t = jnp.tanh(inner)
    hidden = 0.5 * v * (1.0 + t)
    slope = 0.5 * (1.0 + t) + 0.5 * v * (1.0 - t * t) * (root * (1.0 + 3 * 0.044715 * squared))
    return hidden, slope


def feed_specs(layer):
    return [
        pl.BlockSpec((1, D, D), lambda i: (layer - 1, 0, i)),
        pl.BlockSpec((1, D, D), lambda i: (layer, 0, 2 + i)),
        pl.BlockSpec((1, D, D), lambda i: (layer, 0, i)),
        pl.BlockSpec((1, D, D), lambda i: (layer, 0, i)),
    ]


def feed_kernel(
    layer, x_ref, in_a_ref, out_a_ref, in_b_ref, out_b_ref, fsum_ref, norm_ref,
    next_ref, sum_ref, fnew_ref, acc_ref,
):
    step = pl.program_id(0)
    x = x_ref[...]
    hidden_a = gelu_parts(mm(x, in_a_ref[0]))[0].astype(BF)
    hidden_b = gelu_parts(mm(x, in_b_ref[0]))[0].astype(BF)
    part = mm_nt(hidden_a, out_a_ref[0]) + mm_nt(hidden_b, out_b_ref[0])

    @pl.when(step == 0)
    def _():
        acc_ref[...] = part

    @pl.when(step == 1)
    def _():
        branch = acc_ref[...] + part
        summed = x_ref[...].astype(F32) + branch
        normal, _ = norm_parts(summed)
        moved = normal * gain_of(norm_ref, layer) + shift_of(norm_ref, layer)
        next_ref[...] = moved.astype(next_ref.dtype)
        sum_ref[...] = summed
        fnew_ref[...] = fsum_ref[...] + branch


def feed(stream, near, late, layer, norms, branch_sum, out_type):
    return pl.pallas_call(
        functools.partial(feed_kernel, layer),
        grid=(2,),
        in_specs=[whole(HALF, D), *feed_specs(layer), whole(HALF, D), whole(SECTIONS, 4 * D)],
        out_specs=[whole(HALF, D), whole(HALF, D), whole(HALF, D)],
        out_shape=[shaped(HALF, D, out_type), shaped(HALF, D, F32), shaped(HALF, D, F32)],
        scratch_shapes=[pltpu.VMEM((HALF, D), F32)],
        compiler_params=params(),
        cost_estimate=cost(4 * HALF * D * 4 * D, 8e6, HALF * 4 * D),
        name="feed",
    )(stream, late, near, near, late, branch_sum, norms)


def finish_kernel(
    x_ref, fsum_ref, y_ref, cot_ref, live_ref, norm_ref, out_ref, low_ref, c_ref, dy_ref, grad_ref
):
    summed = y_ref[...].astype(F32) + fsum_ref[...]
    normal, _ = norm_parts(summed)
    width = D // SECTIONS
    gain, shift = (
        jnp.concatenate(
            [
                norm_ref[k : k + 1, 2 * D + part * width : 2 * D + (part + 1) * width]
                for k in range(SECTIONS)
            ],
            axis=1,
        )
        for part in range(2)
    )
    out_ref[...] = (x_ref[...] + normal * gain + shift).astype(BF)
    cot = cot_ref[...].astype(F32) * live_ref[:, 0:1]
    c_ref[...] = cot
    grad, gain_grad, shift_grad = norm_back(summed, gain, cot)
    dy_ref[...] = grad
    low_ref[...] = grad.astype(BF)
    grad_ref[0:1, :] = gain_grad
    grad_ref[1:2, :] = shift_grad


def finish(last, branch_sum, accum, cot, live, norms):
    return pl.pallas_call(
        finish_kernel,
        grid=(1,),
        in_specs=[
            whole(HALF, D), whole(HALF, D), whole(HALF, D), whole(HALF, D), whole(HALF, LANES),
            whole(SECTIONS, 4 * D),
        ],
        out_specs=[whole(HALF, D)] * 4 + [whole(2, D)],
        out_shape=[
            shaped(HALF, D, BF), shaped(HALF, D, BF), shaped(HALF, D, F32), shaped(HALF, D, F32),
            shaped(2, D, F32),
        ],
        compiler_params=params(),
        cost_estimate=cost(1e7, 6e6),
        name="finish",
    )(last, branch_sum, accum, cot, live, norms)


def split_rows(core, blk, row, value, keep_ref, give_ref):
    step = math.gcd(D, blk)
    for k in range(value.shape[0] // step):
        part = value[k * step : (k + 1) * step]
        first = row + k * step
        block, offset = first // blk, first % blk
        if not isinstance(first, int):
            offset = pl.multiple_of(offset, step)

        @pl.when(block % 2 == core)
        def _():
            keep_ref[block // 2, pl.ds(offset, step), :] = part

        @pl.when(block % 2 != core)
        def _():
            give_ref[block // 2, pl.ds(offset, step), :] = part


def side_rows(grads, final_grads, keep_ref, give_ref):
    extra = jnp.concatenate([grads, final_grads, jnp.zeros((12, D), F32)], axis=0).astype(BF)
    blk = keep_ref.shape[1] - 16
    for block in range(keep_ref.shape[0]):
        keep_ref[block, blk:, :] = extra
        give_ref[block, blk:, :] = extra


def split_shapes(count, blk):
    spec = pl.BlockSpec((count, blk + 16, D), lambda i: (0, 0, 0))
    return [spec] * 2, [jax.ShapeDtypeStruct((count, blk + 16, D), BF)] * 2


SCALAR = pl.BlockSpec(memory_space=pltpu.SMEM)


def feed_back_kernel(
    layer, core_ref, x_ref, sum_ref, up_ref, dy_ref, in_a_ref, out_a_ref, in_b_ref, out_b_ref,
    norm_ref, final_ref, dx_ref, even_ref, keep_ref, give_ref, acc_ref, df_ref,
):
    step = pl.program_id(0)
    core = core_ref[0]
    blk = keep_ref.shape[1] - 16

    @pl.when(step == 0)
    def _():
        grad, gain_grad, shift_grad = norm_back(
            sum_ref[...], gain_of(norm_ref, layer), up_ref[...].astype(F32)
        )
        side_rows(
            jnp.concatenate([gain_grad, shift_grad], axis=0), final_ref[...], keep_ref, give_ref
        )
        acc_ref[...] = grad
        df_ref[...] = (grad + dy_ref[...]).astype(BF)

    x = x_ref[...]
    df = df_ref[...]

    def chunk(inner, outer):
        hidden, slope = gelu_parts(mm(x, inner))
        outer_grad = mm_tn(hidden.astype(BF), df).astype(BF)
        preact_grad = (mm(df, outer) * slope).astype(BF)
        inner_grad = mm_tn(preact_grad, x).astype(BF)
        return inner_grad, outer_grad, mm_nt(preact_grad, inner)

    inner_grad, outer_grad, back_a = chunk(in_a_ref[0], out_a_ref[0])
    even_ref[...] = inner_grad
    split_rows(core, blk, (2 + step) * D, outer_grad, keep_ref, give_ref)
    inner_grad, outer_grad, back_b = chunk(in_b_ref[0], out_b_ref[0])
    split_rows(core, blk, step * D, inner_grad, keep_ref, give_ref)
    split_rows(core, blk, (4 + step) * D, outer_grad, keep_ref, give_ref)
    total = acc_ref[...] + (back_a + back_b)
    acc_ref[...] = total

    @pl.when(step == 1)
    def _():
        dx_ref[...] = total.astype(BF)


def feed_back(places, stream, summed, upstream, dy, near, late, layer, norms, final_grads):
    specs, shapes = split_shapes(places.ndp // 2, places.blk)
    return pl.pallas_call(
        functools.partial(feed_back_kernel, layer),
        grid=(2,),
        in_specs=[
            SCALAR, whole(HALF, D), whole(HALF, D), whole(HALF, D), whole(HALF, D),
            *feed_specs(layer), whole(SECTIONS, 4 * D), whole(2, D),
        ],
        out_specs=[whole(HALF, D), pl.BlockSpec((D, D), lambda i: (i, 0)), *specs],
        out_shape=[shaped(HALF, D, BF), shaped(2 * D, D, BF), *shapes],
        scratch_shapes=[pltpu.VMEM((HALF, D), F32), pltpu.VMEM((HALF, D), BF)],
        compiler_params=params(),
        cost_estimate=cost(10 * HALF * D * 4 * D, 16e6, HALF * 4 * D),
        name="feed_back",
    )(
        places.core_scalar, stream, summed, upstream, dy, late, near, near, late, norms,
        final_grads,
    )


def outward_back_kernel(
    layer, core_ref, sum_ref, up_ref, dy_ref, ctx_ref, w_ref, norm_ref, final_ref, even_ref,
    dz_ref, dctx_ref, delta_ref, grad_ref, keep_ref, give_ref,
):
    core = core_ref[0]
    blk = keep_ref.shape[1] - 16
    grad, gain_grad, shift_grad = norm_back(
        sum_ref[...], gain_of(norm_ref, layer), up_ref[...].astype(F32)
    )
    grads = jnp.concatenate([gain_grad, shift_grad], axis=0)
    grad_ref[...] = grads
    side_rows(grads, final_ref[...], keep_ref, give_ref)
    dz_ref[...] = grad
    df = (grad + dy_ref[...]).astype(BF)
    context = ctx_ref[...]
    split_rows(core, blk, 0, mm_tn(df, context).astype(BF), keep_ref, give_ref)
    split_rows(core, blk, D, even_ref[...], keep_ref, give_ref)
    context_grad = mm_nt(df, w_ref[0]).astype(BF)
    dctx_ref[...] = context_grad
    product = context.astype(F32) * context_grad.astype(F32)
    lane = lax.broadcasted_iota(jnp.int32, (1, LANES), 1)
    delta = jnp.zeros((HALF, LANES), F32)
    for head in range(HEADS):
        part = product[:, (head // 2) * LANES : (head // 2 + 1) * LANES]
        inner = jnp.sum(jnp.where(head_mask(head % 2), part, 0.0), axis=1, keepdims=True)
        delta = jnp.where(lane == head, inner, delta)
    delta_ref[...] = delta


def outward_back(places, summed, upstream, dy, context, near, layer, norms, final_grads, even):
    specs, shapes = split_shapes(places.ndp // 4, places.blk)
    return pl.pallas_call(
        functools.partial(outward_back_kernel, layer),
        grid=(1,),
        in_specs=[
            SCALAR, whole(HALF, D), whole(HALF, D), whole(HALF, D), whole(HALF, D),
            pl.BlockSpec((1, D, D), lambda i: (layer, 0, 3)), whole(SECTIONS, 4 * D), whole(2, D),
            whole(2 * D, D),
        ],
        out_specs=[
            whole(HALF, D), whole(HALF, D), whole(HALF, LANES), whole(2, D), *specs,
        ],
        out_shape=[
            shaped(HALF, D, F32), shaped(HALF, D, BF), shaped(HALF, LANES, F32),
            shaped(2, D, F32), *shapes,
        ],
        compiler_params=params(),
        cost_estimate=cost(4 * HALF * D * D, 6e6),
        name="outward_back",
    )(
        places.core_scalar, summed, upstream, dy, context, near, norms, final_grads, even,
    )


def scores_back_kernel(
    q_ref, kv_ref, dctx_ref, qs_ref, ks_ref, lse_ref, delta_ref, before_ref, dq_ref, dkv_ref
):
    pair = pl.program_id(0)
    none = jnp.zeros((), BF)
    lane = lax.broadcasted_iota(jnp.int32, (1, LANES), 1)
    q = q_ref[...] * jnp.asarray(SCALE, BF)
    k = kv_ref[0, :, :LANES]
    k_scaled = k * jnp.asarray(SCALE, BF)
    dctx = dctx_ref[...]
    extra = jnp.where((lane >= LANES - 3), jnp.ones((), BF), none)
    keys = jnp.concatenate([k, ks_ref[...] + extra], axis=1)
    values = jnp.concatenate(
        [kv_ref[0, :, LANES:], jnp.broadcast_to(extra, (HALF, LANES))], axis=1
    )
    dq = before_ref[...]
    dk = jnp.zeros((HALF, LANES), F32)
    dv = jnp.zeros((HALF, LANES), F32)
    for which in range(2):
        mask = head_mask(which)
        here = lane == 2 * pair + which

        def lanes_of(table, base):
            column = -jnp.sum(jnp.where(here, table, 0.0), axis=1, keepdims=True)
            high, middle, low = three_way(column)
            base = jnp.where(lane == LANES - 3, high, base)
            base = jnp.where(lane == LANES - 2, middle, base)
            return jnp.where(lane == LANES - 1, low, base)

        query_part = jnp.where(mask, q, none)
        dctx_part = jnp.where(mask, dctx, none)
        query = jnp.concatenate([query_part, lanes_of(lse_ref[...], qs_ref[...])], axis=1)
        dcontext = jnp.concatenate(
            [dctx_part, lanes_of(delta_ref[...], jnp.zeros((HALF, LANES), BF))], axis=1
        )
        probability = jnp.exp(mm_nt(keys, query))
        score_grad = (probability * mm_nt(values, dcontext)).astype(BF)
        dv = dv + mm(probability.astype(BF), dctx_part)
        dk = dk + mm(score_grad, query_part)
        dq = dq + mm_tn(score_grad, jnp.where(mask, k_scaled, none))
    dq_ref[...] = dq
    dkv_ref[0, :, :LANES] = dk.astype(dkv_ref.dtype)
    dkv_ref[0, :, LANES:] = dv.astype(dkv_ref.dtype)


def scores_back(queries, kv, dctx, qseg, kseg, lse, delta, before, out_type):
    return pl.pallas_call(
        scores_back_kernel,
        grid=(PAIRS,),
        in_specs=[
            column(), pair_block(), column(),
            whole(HALF, LANES), whole(HALF, LANES), whole(HALF, LANES), whole(HALF, LANES),
            column(),
        ],
        out_specs=[column(), pair_block()],
        out_shape=[
            shaped(HALF, D, F32), jax.ShapeDtypeStruct((PAIRS, HALF, 2 * LANES), out_type),
        ],
        compiler_params=params(),
        cost_estimate=cost(8e9, 8e6, 2e6),
        name="scores_back",
    )(queries, kv, dctx, qseg, kseg, lse, delta, before)


def project_back_kernel(
    core_ref, x_ref, dq_ref, dkv_ref, far_ref, dz_ref, w_ref, grad_ref, final_ref,
    dx_ref, keep_ref, give_ref,
):
    core = core_ref[0]
    blk = keep_ref.shape[1] - 16
    side_rows(grad_ref[...], final_ref[...], keep_ref, give_ref)
    x = x_ref[...]
    parts = [(dkv_ref[k] + far_ref[k].astype(F32)).astype(BF) for k in range(PAIRS)]
    dk = jnp.concatenate([part[:, :LANES] for part in parts], axis=1)
    dv = jnp.concatenate([part[:, LANES:] for part in parts], axis=1)
    total = dz_ref[...]
    for place, grad in enumerate((dq_ref[...].astype(BF), dk, dv)):
        split_rows(core, blk, place * D, mm_tn(grad, x).astype(BF), keep_ref, give_ref)
        total = total + mm_nt(grad, w_ref[0, :, place * D : (place + 1) * D])
    dx_ref[...] = total.astype(BF)


def project_back(places, stream, dq, dkv, far, dz, near, layer, grads, final_grads):
    specs, shapes = split_shapes(places.ndp // 4, places.blk)
    pairs = pl.BlockSpec((PAIRS, HALF, 2 * LANES), lambda i: (0, 0, 0))
    return pl.pallas_call(
        project_back_kernel,
        grid=(1,),
        in_specs=[
            SCALAR, whole(HALF, D), whole(HALF, D), pairs, pairs, whole(HALF, D),
            pl.BlockSpec((1, D, 3 * D), lambda i: (layer, 0, 0)), whole(2, D), whole(2, D),
        ],
        out_specs=[whole(HALF, D), *specs],
        out_shape=[shaped(HALF, D, BF), *shapes],
        compiler_params=params(),
        cost_estimate=cost(4 * HALF * D * 3 * D, 10e6),
        name="project_back",
    )(places.core_scalar, stream, dq, dkv, far, dz, near, grads, final_grads)


class Places:
    def __init__(self):
        self.ndp = lax.axis_size("dp")
        self.section = lax.axis_index("section")
        self.dp = lax.axis_index("dp")
        self.core = self.dp % 2
        self.core_scalar = self.core.reshape(1).astype(jnp.int32)
        self.blk = 6 * D // self.ndp

    def swap_dp(self, block, step):
        return lax.ppermute(block, "dp", [(i, i ^ step) for i in range(self.ndp)])

    def swap_core(self, block):
        return self.swap_dp(block, 1)

    def swap_section(self, block, step):
        return lax.ppermute(block, "section", [(i, i ^ step) for i in range(SECTIONS)])

    def send(self, block, route):
        pairs = []
        for s in range(SECTIONS):
            for d in range(self.ndp):
                to = route(s, d)
                pairs.append((s * self.ndp + d, to[0] * self.ndp + to[1]))
        return lax.ppermute(block, ("section", "dp"), pairs)


def pick(stack, index):
    return lax.dynamic_index_in_dim(stack, index, 0, keepdims=False)


def after(value, *earlier):
    return lax.optimization_barrier((value, *earlier))[0]


def tokens_in(places, block):
    several = block.shape[0]
    width = D // SECTIONS
    pieces = jnp.swapaxes(block.reshape(several, 4, HALF, width), 0, 1)
    got = []
    for turn in range(4):

        def route(s, d, turn=turn):
            piece = s ^ turn
            return 2 * (d % 2) + piece // 2, d - d % 2 + piece % 2

        got.append(places.send(pick(pieces, places.section ^ turn), route))
    got = jnp.stack(got)
    mine = 2 * (places.section % 2) + places.core
    return jnp.concatenate([pick(got, mine ^ f) for f in range(SECTIONS)], axis=2)


def tokens_out(places, rows):
    several = rows.shape[0]
    features = jnp.stack(jnp.split(rows, SECTIONS, axis=2))
    mine = 2 * (places.section % 2) + places.core
    got = []
    for turn in range(4):

        def route(s, d, turn=turn):
            return (2 * (s % 2) + d % 2) ^ turn, d - d % 2 + s // 2

        got.append(places.send(pick(features, mine ^ turn), route))
    got = jnp.stack(got)
    return jnp.concatenate([pick(got, places.section ^ k) for k in range(4)], axis=1)


def gather_start(places, mine):
    half = D // 4
    from_x = places.swap_section(mine, 1)
    from_y = places.swap_section(mine, 2)
    upper = places.swap_section(from_x[:half], 2)
    lower = places.swap_section(from_y[half:], 1)
    return from_x, from_y, upper, lower


def place_kernel(spot_ref, own_ref, out_ref):
    out_ref[0] = own_ref[...]


def place_own(places, own, first, blocks):
    return pl.pallas_call(
        place_kernel,
        grid_spec=pltpu.PrefetchScalarGridSpec(
            num_scalar_prefetch=1,
            grid=(blocks,),
            in_specs=[pl.BlockSpec((D, D), lambda i, spot: (0, first + i))],
            out_specs=pl.BlockSpec((1, D, D), lambda i, spot: (spot[0], 0, i)),
        ),
        out_shape=jax.ShapeDtypeStruct((SECTIONS, D, blocks * D), BF),
        cost_estimate=cost(0, 4e6),
        name="place_own",
    )(places.section.reshape(1).astype(jnp.int32), own)


def gather_finish(places, full, pieces):
    half = D // 2
    from_x, from_y, upper, lower = pieces
    start = places.core * half

    def put(full, piece, step, offset):
        spot = places.section ^ step
        far = places.swap_core(piece)
        full = lax.dynamic_update_slice(full, piece[None], (spot, start + offset, 0))
        return lax.dynamic_update_slice(full, far[None], (spot, half - start + offset, 0))

    full = put(full, from_x[:half], 1, 0)
    full = put(full, from_y[:half], 2, 0)
    full = put(full, upper, 3, 0)
    return put(full, lower[: half // 2], 3, half // 2)


class Reduction:
    def __init__(self, places):
        self.places = places
        self.cut = max(16, (places.blk + 16) // 32 * 16)
        self.even_x = places.section % 2 == 0
        self.even_y = places.section // 2 == 0

    def cores(self, keep, give):
        return keep + self.places.swap_core(give)

    def plane_one(self, sums):
        zero = jnp.zeros_like(sums[0])
        first = jnp.concatenate([zero, sums[0]], axis=0)
        low = [part[:, : self.cut] for part in (first, *sums[1:])]
        high = [part[:, self.cut :] for part in (first, *sums[1:])]
        even, odd = jnp.stack([low[0], low[2]]), jnp.stack([low[1], low[3]])
        self.upper = jnp.where(self.even_x, even, odd) + self.places.swap_section(
            jnp.where(self.even_x, odd, even), 1
        )
        even, odd = jnp.stack([high[0], high[1]]), jnp.stack([high[2], high[3]])
        self.lower = jnp.where(self.even_y, even, odd) + self.places.swap_section(
            jnp.where(self.even_y, odd, even), 2
        )

    def plane_two(self, last):
        places = self.places
        half = last.shape[0]
        upper, lower = last[:, : self.cut], last[:, self.cut :]
        upper = upper + places.swap_section(upper, 1)
        lower = lower + places.swap_section(lower, 2)

        def joined(part, late, whose):
            first = jnp.where(whose, late, part[0, :half])
            return jnp.concatenate([first, part[0, half:]], axis=0), part[1]

        up = joined(self.upper, upper, self.even_x)
        down = joined(self.lower, lower, self.even_y)
        upper = jnp.where(self.even_y, up[0], up[1]) + places.swap_section(
            jnp.where(self.even_y, up[1], up[0]), 2
        )
        lower = jnp.where(self.even_x, down[0], down[1]) + places.swap_section(
            jnp.where(self.even_x, down[1], down[0]), 1
        )
        return jnp.concatenate([upper, lower], axis=1)

    def depth(self, blocks):
        places = self.places
        total = blocks.shape[0]
        place = places.dp // 2
        if total <= 4:
            got = [pick(blocks, place)]
            for step in range(1, total):
                got.append(places.swap_dp(pick(blocks, place ^ step), 2 * step))
            got = jnp.stack(got)
            out = pick(got, place).astype(F32)
            for spot in range(1, total):
                out = out + pick(got, place ^ spot).astype(F32)
            return out
        bit = total // 2
        while bit:
            blocks = blocks.reshape(2, bit, *blocks.shape[1:])
            mine = (place // bit) % 2
            blocks = pick(blocks, mine) + places.swap_dp(pick(blocks, 1 - mine), 2 * bit)
            bit //= 2
        return blocks[0].astype(F32)


def on_device(
    stream_input,
    accum_input,
    section_weights,
    section_norms,
    final_norm,
    seq_lengths,
    out_cotangent,
):
    places = Places()
    section, core = places.section, places.core
    width = D // SECTIONS
    rows = D // 2

    stream = tokens_in(places, stream_input[None])[0]
    own = section_weights[0]
    small = jnp.concatenate(
        [section_norms[0, 0], section_norms[0, 1], final_norm[0], final_norm[1]], axis=0
    )
    small = jnp.pad(small[None], ((0, 15), (0, 4 * D - small.shape[0])))
    near_own, late_own = own[:, : 4 * D], own[:, 4 * D :]
    mine = lax.dynamic_slice(near_own, (core * rows, 0), (rows, 4 * D))
    near_pieces = gather_start(places, jnp.concatenate([mine, small], axis=0))
    late_mine = after(
        lax.dynamic_slice(late_own, (core * rows, 0), (rows, 2 * D)), near_pieces[0], near_pieces[1]
    )
    late_pieces = gather_start(places, late_mine)
    near = gather_finish(places, place_own(places, own, 0, 4), near_pieces)
    late = gather_finish(places, place_own(places, own, 4, 2), late_pieces)
    tail = jnp.stack(
        [small, near_pieces[0][rows:], near_pieces[1][rows:], near_pieces[3][rows // 2 :]]
    )[:, 0].astype(F32)
    norms = jnp.stack([pick(tail, section ^ j) for j in range(SECTIONS)])

    other_lengths = places.swap_core(seq_lengths)
    lengths = pick(jnp.where(core == section // 2, seq_lengths, other_lengths), section % 2)
    ending = jnp.cumsum(lengths, dtype=jnp.int32)

    def rows_of(which):
        spots = which * HALF + jnp.arange(HALF, dtype=jnp.int32)
        segment = jnp.sum(
            (spots[:, None] >= ending[None, :]).astype(jnp.int32), axis=1, dtype=jnp.int32
        )
        lane = jnp.arange(LANES, dtype=jnp.int32)
        hot = (segment[:, None] == lane[None, :]).astype(BF)
        alive = (spots < ending[-1]).astype(F32)
        return segment, hot, jnp.broadcast_to(alive[:, None], (HALF, LANES))

    segment_own, kseg_own, live = rows_of(core)
    _, kseg_other, _ = rows_of(1 - core)
    lane = jnp.arange(LANES, dtype=jnp.int32)
    qseg = jnp.where(
        (segment_own[:, None] != lane[None, :]) & (lane[None, :] < 32), -FAR, 0.0
    ).astype(BF)
    segs = (qseg, kseg_own, kseg_other)

    both = after(jnp.stack([accum_input, out_cotangent]), late_pieces[2], late_pieces[3])
    accum, cot = tokens_in(places, both)

    branch_sum = jnp.zeros((HALF, D), F32)
    kept = []
    for layer in (0, 2):
        queries, own_kv = project(stream, near, layer)
        far_kv = places.swap_core(own_kv)
        context, lse, middle, sum_a, branch_sum = attend(
            stream, queries, own_kv, far_kv, segs, near, layer, norms, branch_sum
        )
        following, sum_f, branch_sum = feed(
            middle, near, late, layer + 1, norms, branch_sum, BF if layer == 0 else F32
        )
        kept.append((stream, queries, own_kv, far_kv, context, lse, sum_a, middle, sum_f))
        stream = following

    result, dy_low, upstream, dy, final_grad = finish(
        stream, branch_sum, accum, cot, live, norms
    )
    result_out, accum_out = tokens_out(places, jnp.stack([result, dy_low]))

    sums = [None] * SECTIONS
    reduction = Reduction(places)
    for layer in (2, 0):
        entering, queries, own_kv, far_kv, context, lse, sum_a, middle, sum_f = kept[layer // 2]
        upstream, inner, keep, give = feed_back(
            places, middle, sum_f, upstream, dy, near, late, layer + 1, norms, final_grad
        )
        if layer:
            upstream = after(upstream, result_out, accum_out)
        sums[layer + 1] = reduction.cores(keep, give)
        dz, dctx, delta, grads, keep, give = outward_back(
            places, sum_a, upstream, dy, context, near, layer, norms, final_grad, inner
        )
        later_half = reduction.cores(keep, give)
        if not layer:
            sums[layer] = later_half
            reduction.plane_one(sums)
        dq, dkv_far = scores_back(
            queries, far_kv, dctx, qseg, segs[2], lse, delta, jnp.zeros((HALF, D), F32), BF
        )
        from_far = places.swap_core(dkv_far)
        dq, dkv = scores_back(queries, own_kv, dctx, qseg, segs[1], lse, delta, dq, F32)
        upstream, keep, give = project_back(
            places, entering, dq, dkv, from_far, dz, near, layer, grads, final_grad
        )
        first_half = reduction.cores(keep, give)
        if layer:
            sums[layer] = jnp.concatenate([first_half, later_half], axis=0)
    blocks = reduction.plane_two(first_half)
    reduced = reduction.depth(blocks)
    stream_out = tokens_out(places, after(upstream[None], blocks))[0]
    slab = reduced[: places.blk].T
    small_out = reduced[places.blk :]
    cut = D // places.ndp
    norm_out = lax.dynamic_slice(small_out, (0, places.dp * cut), (2, cut))
    final_out = lax.dynamic_slice(small_out, (2, section * width), (2, width))

    return (
        result_out,
        stream_out.astype(F32),
        accum_out.astype(F32),
        slab[None],
        norm_out[None],
        final_out,
    )


def solution(mesh):
    placed = (
        P("dp", "section"),
        P("dp", "section"),
        P("section", None, None),
        P("section", None, None),
        P(None, "section"),
        P("dp", None),
        P("dp", "section"),
    )
    return jax.shard_map(
        on_device,
        mesh=mesh,
        in_specs=placed,
        out_specs=(
            P("dp", "section"),
            P("dp", "section"),
            P("dp", "section"),
            P("section", None, "dp"),
            P("section", None, "dp"),
            P(None, "section"),
        ),
        check_vma=False,
    )
```

```python
import functools
import math

import jax
import jax.numpy as jnp
from jax import lax
from jax.experimental import pallas as pl
from jax.experimental.pallas import tpu as pltpu
from jax.sharding import PartitionSpec as P

D = 512
HEADS = 8
HEAD = 64
PACK = 1024
HALF = PACK // 2
PAIRS = HEADS // 2
LANES = 2 * HEAD
SECTIONS = 4
FAR = 1e30
SCALE = HEAD ** (-0.5)
BF = jnp.bfloat16
F32 = jnp.float32
NT = (((1,), (1,)), ((), ()))
TN = (((0,), (0,)), ((), ()))


def mm(left, right):
    return jnp.dot(left, right, preferred_element_type=F32)


def mm_nt(left, right):
    return lax.dot_general(left, right, NT, preferred_element_type=F32)


def mm_tn(left, right):
    return lax.dot_general(left, right, TN, preferred_element_type=F32)


def params(megabytes=16):
    return pltpu.CompilerParams(
        dimension_semantics=("arbitrary",), vmem_limit_bytes=megabytes * 1024 * 1024
    )


def shaped(rows, cols, dtype):
    return jax.ShapeDtypeStruct((rows, cols), dtype)


def whole(rows, cols):
    return pl.BlockSpec((rows, cols), lambda i: (0, 0))


SCALAR = pl.BlockSpec(memory_space=pltpu.SMEM)


def cost(flops, moved, transcendentals=0):
    return pl.CostEstimate(
        flops=int(flops), bytes_accessed=int(moved), transcendentals=int(transcendentals)
    )


def gain_of(table_ref, layer):
    return table_ref[layer : layer + 1, :D]


def shift_of(table_ref, layer):
    return table_ref[layer : layer + 1, D : 2 * D]


def norm_parts(summed):
    average = jnp.mean(summed, axis=-1, keepdims=True)
    centered = summed - average
    spread = jnp.mean(centered * centered, axis=-1, keepdims=True)
    inverse = lax.rsqrt(spread + 1e-05)
    return centered * inverse, inverse


def norm_back(summed, gain, upstream):
    normal, inverse = norm_parts(summed)
    scaled = upstream * gain
    mean_one = jnp.mean(scaled, axis=-1, keepdims=True)
    mean_two = jnp.mean(scaled * normal, axis=-1, keepdims=True)
    grad = (scaled - mean_one - normal * mean_two) * inverse
    gain_grad = jnp.sum(upstream * normal, axis=0, keepdims=True)
    shift_grad = jnp.sum(upstream, axis=0, keepdims=True)
    return grad, gain_grad, shift_grad


def head_mask(which):
    lane = lax.broadcasted_iota(jnp.int32, (1, LANES), 1)
    return (lane // HEAD) == which


def three_way(column):
    high = column.astype(BF)
    rest = column - high.astype(F32)
    middle = rest.astype(BF)
    low = (rest - middle.astype(F32)).astype(BF)
    return high, middle, low


GROUP = 6


def fetch(where_ref, layer, own_ref, piece_refs, own_first, first, width, target, sem):
    section, core = where_ref[0], where_ref[1]
    half = D // 2
    step = section ^ layer
    mine_rows = pl.ds(pl.multiple_of(core * half, half), half)
    far_rows = pl.ds(pl.multiple_of((1 - core) * half, half), half)

    @pl.when(step == 0)
    def _():
        pltpu.make_async_copy(own_ref.at[:, pl.ds(own_first, width)], target, sem).start()

    for number, (partner, far_number) in enumerate(((1 + core, 1), (2 - core, 0), (3, 2))):

        @pl.when(step == partner)
        def _():
            part = (pl.ds(0, half), pl.ds(first, width))
            mine, far = piece_refs[number].at[part], piece_refs[3 + far_number].at[part]
            pltpu.make_async_copy(mine, target.at[mine_rows], sem).start()
            pltpu.make_async_copy(far, target.at[far_rows], sem).start()


def arrived(own_ref, width, target, sem):
    pltpu.make_async_copy(own_ref.at[:, pl.ds(0, width)], target, sem).wait()


def weight_specs(groups):
    return [pl.BlockSpec(memory_space=pl.ANY)] * (1 + GROUP * groups)


def project_kernel(layer, where_ref, x_ref, own_ref, *refs):
    near, (q_ref, kv_ref, weight_ref, sems) = refs[:GROUP], refs[GROUP:]
    for part in range(3):
        fetch(
            where_ref, layer, own_ref, near, part * D, part * D, D, weight_ref.at[part],
            sems.at[part],
        )
    x = x_ref[...]

    def times(part):
        arrived(own_ref, D, weight_ref.at[part], sems.at[part])
        return mm(x, weight_ref[part]).astype(BF)

    q_ref[...] = times(0)
    keys, values = times(1), times(2)
    for pair in range(PAIRS):
        lanes = slice(pair * LANES, (pair + 1) * LANES)
        kv_ref[pair, :, :LANES] = keys[:, lanes]
        kv_ref[pair, :, LANES:] = values[:, lanes]


def project(places, stream, own, near, layer):
    return pl.pallas_call(
        functools.partial(project_kernel, layer),
        grid=(1,),
        in_specs=[SCALAR, whole(HALF, D), *weight_specs(1)],
        out_specs=[whole(HALF, D), pl.BlockSpec((PAIRS, HALF, 2 * LANES), lambda i: (0, 0, 0))],
        out_shape=[
            shaped(HALF, D, BF), jax.ShapeDtypeStruct((PAIRS, HALF, 2 * LANES), BF),
        ],
        scratch_shapes=[pltpu.VMEM((3, D, D), BF), pltpu.SemaphoreType.DMA((3,))],
        compiler_params=params(),
        cost_estimate=cost(2 * HALF * D * 3 * D, 4e6),
        name="project",
    )(places.where, stream, own, *near)


def attend_kernel(
    layer, where_ref, q_ref, own_ref, far_ref, qs_ref, kso_ref, ksx_ref, x_ref, fsum_ref,
    norm_ref, weights_ref, *refs,
):
    near, (
        ctx_ref, lse_ref, next_ref, sum_ref, fnew_ref, ctx_acc, lse_acc, weight_ref, sem,
    ) = refs[:GROUP], refs[GROUP:]
    pair = pl.program_id(0)

    @pl.when(pair == 0)
    def _():
        fetch(where_ref, layer, weights_ref, near, 3 * D, 3 * D, D, weight_ref, sem)

    q = q_ref[...] * jnp.asarray(SCALE, BF)
    keys_own = jnp.concatenate([own_ref[0, :, :LANES], kso_ref[...]], axis=1)
    keys_other = jnp.concatenate([far_ref[0, :, :LANES], ksx_ref[...]], axis=1)
    values_own, values_other = own_ref[0, :, LANES:], far_ref[0, :, LANES:]
    ones = jnp.ones((HALF, LANES), BF)
    none = jnp.zeros((), BF)
    lane = lax.broadcasted_iota(jnp.int32, (1, LANES), 1)
    context = jnp.zeros((HALF, LANES), F32)
    logs = jnp.where(pair == 0, jnp.zeros((HALF, LANES), F32), lse_acc[...])
    for which in range(2):
        mask = head_mask(which)
        query = jnp.concatenate([jnp.where(mask, q, none), qs_ref[...]], axis=1)
        score_own = mm_nt(query, keys_own)
        score_other = mm_nt(query, keys_other)
        peak = jnp.maximum(
            jnp.max(score_own, axis=1, keepdims=True), jnp.max(score_other, axis=1, keepdims=True)
        )
        own = jnp.exp(score_own - peak).astype(BF)
        other = jnp.exp(score_other - peak).astype(BF)
        total = mm(own, jnp.concatenate([jnp.where(mask, values_own, none), ones], axis=1)) + mm(
            other, jnp.concatenate([jnp.where(mask, values_other, none), ones], axis=1)
        )
        row_total = total[:, LANES:]
        context = context + total[:, :LANES] / row_total
        logs = jnp.where(lane == 2 * pair + which, peak + jnp.log(row_total), logs)
    lse_acc[...] = logs
    ctx_acc[pair] = context.astype(BF)
    ctx_ref[...] = context.astype(BF)

    @pl.when(pair == PAIRS - 1)
    def _():
        lse_ref[...] = lse_acc[...]
        full = jnp.concatenate([ctx_acc[k] for k in range(PAIRS)], axis=1)
        arrived(weights_ref, D, weight_ref, sem)
        branch = mm(full, weight_ref[...])
        summed = x_ref[...].astype(F32) + branch
        normal, _ = norm_parts(summed)
        moved = normal * gain_of(norm_ref, layer) + shift_of(norm_ref, layer)
        next_ref[...] = moved.astype(BF)
        sum_ref[...] = summed
        fnew_ref[...] = fsum_ref[...] + branch


def column():
    return pl.BlockSpec((HALF, LANES), lambda i: (0, i))


def pair_block():
    return pl.BlockSpec((1, HALF, 2 * LANES), lambda i: (i, 0, 0))


def attend(
    places, stream, queries, own_kv, far_kv, segs, own, near, layer, norms, branch_sum
):
    qseg, kseg_own, kseg_other = segs
    return pl.pallas_call(
        functools.partial(attend_kernel, layer),
        grid=(PAIRS,),
        in_specs=[
            SCALAR, column(), pair_block(), pair_block(),
            whole(HALF, LANES), whole(HALF, LANES), whole(HALF, LANES),
            whole(HALF, D), whole(HALF, D), whole(SECTIONS, 4 * D), *weight_specs(1),
        ],
        out_specs=[
            column(), whole(HALF, LANES), whole(HALF, D), whole(HALF, D), whole(HALF, D),
        ],
        out_shape=[
            shaped(HALF, D, BF), shaped(HALF, LANES, F32), shaped(HALF, D, BF),
            shaped(HALF, D, F32), shaped(HALF, D, F32),
        ],
        scratch_shapes=[
            pltpu.VMEM((PAIRS, HALF, LANES), BF), pltpu.VMEM((HALF, LANES), F32),
            pltpu.VMEM((D, D), BF), pltpu.SemaphoreType.DMA,
        ],
        compiler_params=params(),
        cost_estimate=cost(8e9, 8e6, 4e6),
        name="attend",
    )(
        places.where, queries, own_kv, far_kv, qseg, kseg_own, kseg_other, stream, branch_sum,
        norms, own, *near,
    )


def gelu_parts(v):
    root = 0.7978845608028654
    squared = v * v
    inner = root * (v + 0.044715 * v * squared)
    t = jnp.tanh(inner)
    hidden = 0.5 * v * (1.0 + t)
    slope = 0.5 * (1.0 + t) + 0.5 * v * (1.0 - t * t) * (root * (1.0 + 3 * 0.044715 * squared))
    return hidden, slope


def feed_fetch(layer, where_ref, own_ref, refs, weight_ref, sems):
    near, late = refs[:GROUP], refs[GROUP:]
    for step in range(2):
        for number, (whose, pieces, own_first, first) in enumerate(
            (
                (layer - 1, late, 4 * D, 0),
                (layer, near, 2 * D, 2 * D),
                (layer, near, 0, 0),
                (layer, late, 4 * D, 0),
            )
        ):
            fetch(
                where_ref, whose, own_ref, pieces, own_first + step * D, first + step * D, D,
                weight_ref.at[step, number], sems.at[step, number],
            )


FEED_SCRATCH = [pltpu.VMEM((2, 4, D, D), BF), pltpu.SemaphoreType.DMA((2, 4))]


def feed_kernel(layer, where_ref, x_ref, fsum_ref, norm_ref, own_ref, *refs):
    pieces, (next_ref, sum_ref, fnew_ref, acc_ref, weight_ref, sems) = (
        refs[: 2 * GROUP], refs[2 * GROUP :],
    )
    step = pl.program_id(0)

    @pl.when(step == 0)
    def _():
        feed_fetch(layer, where_ref, own_ref, pieces, weight_ref, sems)

    def weight(number):
        arrived(own_ref, D, weight_ref.at[step, number], sems.at[step, number])
        return weight_ref[step, number]

    x = x_ref[...]
    hidden = gelu_parts(mm(x, weight(0)))[0].astype(BF)
    part = mm_nt(hidden, weight(1))
    hidden = gelu_parts(mm(x, weight(2)))[0].astype(BF)
    part = part + mm_nt(hidden, weight(3))

    @pl.when(step == 0)
    def _():
        acc_ref[...] = part

    @pl.when(step == 1)
    def _():
        branch = acc_ref[...] + part
        summed = x_ref[...].astype(F32) + branch
        normal, _ = norm_parts(summed)
        moved = normal * gain_of(norm_ref, layer) + shift_of(norm_ref, layer)
        next_ref[...] = moved.astype(next_ref.dtype)
        sum_ref[...] = summed
        fnew_ref[...] = fsum_ref[...] + branch


def feed(places, stream, own, near, late, layer, norms, branch_sum, out_type):
    return pl.pallas_call(
        functools.partial(feed_kernel, layer),
        grid=(2,),
        in_specs=[
            SCALAR, whole(HALF, D), whole(HALF, D), whole(SECTIONS, 4 * D), *weight_specs(2),
        ],
        out_specs=[whole(HALF, D), whole(HALF, D), whole(HALF, D)],
        out_shape=[shaped(HALF, D, out_type), shaped(HALF, D, F32), shaped(HALF, D, F32)],
        scratch_shapes=[pltpu.VMEM((HALF, D), F32), *FEED_SCRATCH],
        compiler_params=params(20),
        cost_estimate=cost(4 * HALF * D * 4 * D, 8e6, HALF * 4 * D),
        name="feed",
    )(places.where, stream, branch_sum, norms, own, *near, *late)


def finish_kernel(
    mine_ref, x_ref, fsum_ref, a_ref, b_ref, e_ref, d_ref, live_ref, norm_ref,
    out_ref, low_ref, c_ref, dy_ref, grad_ref,
):
    pieces = in_order([ref[...] for ref in (a_ref, b_ref, e_ref, d_ref)], mine_ref[0])
    accum, cot = (jnp.concatenate([piece[k] for piece in pieces], axis=1) for k in range(2))
    summed = accum.astype(F32) + fsum_ref[...]
    normal, _ = norm_parts(summed)
    width = D // SECTIONS
    gain, shift = (
        jnp.concatenate(
            [
                norm_ref[k : k + 1, 2 * D + part * width : 2 * D + (part + 1) * width]
                for k in range(SECTIONS)
            ],
            axis=1,
        )
        for part in range(2)
    )
    out_ref[...] = (x_ref[...] + normal * gain + shift).astype(BF)
    cot = cot.astype(F32) * live_ref[:, 0:1]
    c_ref[...] = cot
    grad, gain_grad, shift_grad = norm_back(summed, gain, cot)
    dy_ref[...] = grad
    low_ref[...] = grad.astype(BF)
    grad_ref[0:1, :] = gain_grad
    grad_ref[1:2, :] = shift_grad


def finish(places, last, branch_sum, pieces, live, norms):
    piece = pl.BlockSpec((2, HALF, D // SECTIONS), lambda i: (0, 0, 0))
    return pl.pallas_call(
        finish_kernel,
        grid=(1,),
        in_specs=[
            SCALAR, whole(HALF, D), whole(HALF, D), *[piece] * 4, whole(HALF, LANES),
            whole(SECTIONS, 4 * D),
        ],
        out_specs=[whole(HALF, D)] * 4 + [whole(2, D)],
        out_shape=[
            shaped(HALF, D, BF), shaped(HALF, D, BF), shaped(HALF, D, F32), shaped(HALF, D, F32),
            shaped(2, D, F32),
        ],
        compiler_params=params(),
        cost_estimate=cost(1e7, 6e6),
        name="finish",
    )(places.mine.reshape(1).astype(jnp.int32), last, branch_sum, *pieces, live, norms)


def split_rows(core, blk, row, value, keep_ref, give_ref):
    step = math.gcd(D, blk)
    for k in range(value.shape[0] // step):
        part = value[k * step : (k + 1) * step]
        first = row + k * step
        block, offset = first // blk, first % blk
        if not isinstance(first, int):
            offset = pl.multiple_of(offset, step)

        @pl.when(block % 2 == core)
        def _():
            keep_ref[block // 2, pl.ds(offset, step), :] = part

        @pl.when(block % 2 != core)
        def _():
            give_ref[block // 2, pl.ds(offset, step), :] = part


def side_rows(grads, final_grads, keep_ref, give_ref):
    extra = jnp.concatenate([grads, final_grads, jnp.zeros((12, D), F32)], axis=0).astype(BF)
    blk = keep_ref.shape[1] - 16
    for block in range(keep_ref.shape[0]):
        keep_ref[block, blk:, :] = extra
        give_ref[block, blk:, :] = extra


def split_shapes(count, blk):
    spec = pl.BlockSpec((count, blk + 16, D), lambda i: (0, 0, 0))
    return [spec] * 2, [jax.ShapeDtypeStruct((count, blk + 16, D), BF)] * 2


def feed_back_kernel(
    layer, where_ref, x_ref, sum_ref, up_ref, dy_ref, norm_ref, final_ref, own_ref, *refs
):
    pieces, (
        dx_ref, even_ref, keep_ref, give_ref, acc_ref, df_ref, weight_ref, sems,
    ) = refs[: 2 * GROUP], refs[2 * GROUP :]
    step = pl.program_id(0)
    core = where_ref[1]
    blk = keep_ref.shape[1] - 16

    def weight(number):
        arrived(own_ref, D, weight_ref.at[step, number], sems.at[step, number])
        return weight_ref[step, number]

    @pl.when(step == 0)
    def _():
        feed_fetch(layer, where_ref, own_ref, pieces, weight_ref, sems)
        grad, gain_grad, shift_grad = norm_back(
            sum_ref[...], gain_of(norm_ref, layer), up_ref[...].astype(F32)
        )
        side_rows(
            jnp.concatenate([gain_grad, shift_grad], axis=0), final_ref[...], keep_ref, give_ref
        )
        acc_ref[...] = grad
        df_ref[...] = (grad + dy_ref[...]).astype(BF)

    x = x_ref[...]
    df = df_ref[...]

    def chunk(inner, outer):
        hidden, slope = gelu_parts(mm(x, inner))
        outer_grad = mm_tn(hidden.astype(BF), df).astype(BF)
        preact_grad = (mm(df, outer) * slope).astype(BF)
        inner_grad = mm_tn(preact_grad, x).astype(BF)
        return inner_grad, outer_grad, mm_nt(preact_grad, inner)

    inner_grad, outer_grad, back_a = chunk(weight(0), weight(1))
    even_ref[...] = inner_grad
    split_rows(core, blk, (2 + step) * D, outer_grad, keep_ref, give_ref)
    inner_grad, outer_grad, back_b = chunk(weight(2), weight(3))
    split_rows(core, blk, step * D, inner_grad, keep_ref, give_ref)
    split_rows(core, blk, (4 + step) * D, outer_grad, keep_ref, give_ref)
    total = acc_ref[...] + (back_a + back_b)
    acc_ref[...] = total

    @pl.when(step == 1)
    def _():
        dx_ref[...] = total.astype(BF)


def feed_back(places, stream, summed, upstream, dy, own, near, late, layer, norms, final_grads):
    specs, shapes = split_shapes(places.ndp // 2, places.blk)
    return pl.pallas_call(
        functools.partial(feed_back_kernel, layer),
        grid=(2,),
        in_specs=[
            SCALAR, whole(HALF, D), whole(HALF, D), whole(HALF, D), whole(HALF, D),
            whole(SECTIONS, 4 * D), whole(2, D), *weight_specs(2),
        ],
        out_specs=[whole(HALF, D), pl.BlockSpec((D, D), lambda i: (i, 0)), *specs],
        out_shape=[shaped(HALF, D, BF), shaped(2 * D, D, BF), *shapes],
        scratch_shapes=[pltpu.VMEM((HALF, D), F32), pltpu.VMEM((HALF, D), BF), *FEED_SCRATCH],
        compiler_params=params(26),
        cost_estimate=cost(10 * HALF * D * 4 * D, 16e6, HALF * 4 * D),
        name="feed_back",
    )(
        places.where, stream, summed, upstream, dy, norms, final_grads, own, *near, *late,
    )


def outward_back_kernel(
    layer, where_ref, sum_ref, up_ref, dy_ref, ctx_ref, norm_ref, final_ref, even_ref, own_ref,
    *refs,
):
    near, (
        dz_ref, dctx_ref, delta_ref, grad_ref, keep_ref, give_ref, weight_ref, sem,
    ) = refs[:GROUP], refs[GROUP:]
    fetch(where_ref, layer, own_ref, near, 3 * D, 3 * D, D, weight_ref, sem)
    core = where_ref[1]
    blk = keep_ref.shape[1] - 16
    grad, gain_grad, shift_grad = norm_back(
        sum_ref[...], gain_of(norm_ref, layer), up_ref[...].astype(F32)
    )
    grads = jnp.concatenate([gain_grad, shift_grad], axis=0)
    grad_ref[...] = grads
    side_rows(grads, final_ref[...], keep_ref, give_ref)
    dz_ref[...] = grad
    df = (grad + dy_ref[...]).astype(BF)
    context = ctx_ref[...]
    split_rows(core, blk, 0, mm_tn(df, context).astype(BF), keep_ref, give_ref)
    split_rows(core, blk, D, even_ref[...], keep_ref, give_ref)
    arrived(own_ref, D, weight_ref, sem)
    context_grad = mm_nt(df, weight_ref[...]).astype(BF)
    dctx_ref[...] = context_grad
    product = context.astype(F32) * context_grad.astype(F32)
    lane = lax.broadcasted_iota(jnp.int32, (1, LANES), 1)
    delta = jnp.zeros((HALF, LANES), F32)
    for head in range(HEADS):
        part = product[:, (head // 2) * LANES : (head // 2 + 1) * LANES]
        inner = jnp.sum(jnp.where(head_mask(head % 2), part, 0.0), axis=1, keepdims=True)
        delta = jnp.where(lane == head, inner, delta)
    delta_ref[...] = delta


def outward_back(
    places, summed, upstream, dy, context, own, near, layer, norms, final_grads, even
):
    specs, shapes = split_shapes(places.ndp // 4, places.blk)
    return pl.pallas_call(
        functools.partial(outward_back_kernel, layer),
        grid=(1,),
        in_specs=[
            SCALAR, whole(HALF, D), whole(HALF, D), whole(HALF, D), whole(HALF, D),
            whole(SECTIONS, 4 * D), whole(2, D), whole(2 * D, D), *weight_specs(1),
        ],
        out_specs=[
            whole(HALF, D), whole(HALF, D), whole(HALF, LANES), whole(2, D), *specs,
        ],
        out_shape=[
            shaped(HALF, D, F32), shaped(HALF, D, BF), shaped(HALF, LANES, F32),
            shaped(2, D, F32), *shapes,
        ],
        scratch_shapes=[pltpu.VMEM((D, D), BF), pltpu.SemaphoreType.DMA],
        compiler_params=params(20),
        cost_estimate=cost(4 * HALF * D * D, 6e6),
        name="outward_back",
    )(
        places.where, summed, upstream, dy, context, norms, final_grads, even, own, *near,
    )


def scores_back_kernel(
    q_ref, kv_ref, dctx_ref, qs_ref, ks_ref, lse_ref, delta_ref, before_ref, dq_ref, dkv_ref
):
    pair = pl.program_id(0)
    none = jnp.zeros((), BF)
    lane = lax.broadcasted_iota(jnp.int32, (1, LANES), 1)
    q = q_ref[...] * jnp.asarray(SCALE, BF)
    k = kv_ref[0, :, :LANES]
    k_scaled = k * jnp.asarray(SCALE, BF)
    dctx = dctx_ref[...]
    extra = jnp.where((lane >= LANES - 3), jnp.ones((), BF), none)
    keys = jnp.concatenate([k, ks_ref[...] + extra], axis=1)
    values = jnp.concatenate(
        [kv_ref[0, :, LANES:], jnp.broadcast_to(extra, (HALF, LANES))], axis=1
    )
    dq = before_ref[...]
    dk = jnp.zeros((HALF, LANES), F32)
    dv = jnp.zeros((HALF, LANES), F32)
    for which in range(2):
        mask = head_mask(which)
        here = lane == 2 * pair + which

        def lanes_of(table, base):
            column = -jnp.sum(jnp.where(here, table, 0.0), axis=1, keepdims=True)
            high, middle, low = three_way(column)
            base = jnp.where(lane == LANES - 3, high, base)
            base = jnp.where(lane == LANES - 2, middle, base)
            return jnp.where(lane == LANES - 1, low, base)

        query_part = jnp.where(mask, q, none)
        dctx_part = jnp.where(mask, dctx, none)
        query = jnp.concatenate([query_part, lanes_of(lse_ref[...], qs_ref[...])], axis=1)
        dcontext = jnp.concatenate(
            [dctx_part, lanes_of(delta_ref[...], jnp.zeros((HALF, LANES), BF))], axis=1
        )
        probability = jnp.exp(mm_nt(keys, query))
        score_grad = (probability * mm_nt(values, dcontext)).astype(BF)
        dv = dv + mm(probability.astype(BF), dctx_part)
        dk = dk + mm(score_grad, query_part)
        dq = dq + mm_tn(score_grad, jnp.where(mask, k_scaled, none))
    dq_ref[...] = dq
    dkv_ref[0, :, :LANES] = dk.astype(dkv_ref.dtype)
    dkv_ref[0, :, LANES:] = dv.astype(dkv_ref.dtype)


def scores_back(queries, kv, dctx, qseg, kseg, lse, delta, before, out_type):
    return pl.pallas_call(
        scores_back_kernel,
        grid=(PAIRS,),
        in_specs=[
            column(), pair_block(), column(),
            whole(HALF, LANES), whole(HALF, LANES), whole(HALF, LANES), whole(HALF, LANES),
            column(),
        ],
        out_specs=[column(), pair_block()],
        out_shape=[
            shaped(HALF, D, F32), jax.ShapeDtypeStruct((PAIRS, HALF, 2 * LANES), out_type),
        ],
        compiler_params=params(),
        cost_estimate=cost(8e9, 8e6, 2e6),
        name="scores_back",
    )(queries, kv, dctx, qseg, kseg, lse, delta, before)


def project_back_kernel(
    layer, where_ref, x_ref, dq_ref, dkv_ref, far_ref, dz_ref, grad_ref, final_ref, own_ref, *refs
):
    near, (dx_ref, keep_ref, give_ref, weight_ref, sems) = refs[:GROUP], refs[GROUP:]
    for part in range(3):
        fetch(
            where_ref, layer, own_ref, near, part * D, part * D, D, weight_ref.at[part],
            sems.at[part],
        )
    core = where_ref[1]
    blk = keep_ref.shape[1] - 16
    side_rows(grad_ref[...], final_ref[...], keep_ref, give_ref)
    x = x_ref[...]
    parts = [(dkv_ref[k] + far_ref[k].astype(F32)).astype(BF) for k in range(PAIRS)]
    dk = jnp.concatenate([part[:, :LANES] for part in parts], axis=1)
    dv = jnp.concatenate([part[:, LANES:] for part in parts], axis=1)
    total = dz_ref[...]
    for place, grad in enumerate((dq_ref[...].astype(BF), dk, dv)):
        split_rows(core, blk, place * D, mm_tn(grad, x).astype(BF), keep_ref, give_ref)
        arrived(own_ref, D, weight_ref.at[place], sems.at[place])
        total = total + mm_nt(grad, weight_ref[place])
    dx_ref[...] = total.astype(BF)


def project_back(places, stream, dq, dkv, far, dz, own, near, layer, grads, final_grads):
    specs, shapes = split_shapes(places.ndp // 4, places.blk)
    pairs = pl.BlockSpec((PAIRS, HALF, 2 * LANES), lambda i: (0, 0, 0))
    return pl.pallas_call(
        functools.partial(project_back_kernel, layer),
        grid=(1,),
        in_specs=[
            SCALAR, whole(HALF, D), whole(HALF, D), pairs, pairs, whole(HALF, D),
            whole(2, D), whole(2, D), *weight_specs(1),
        ],
        out_specs=[whole(HALF, D), *specs],
        out_shape=[shaped(HALF, D, BF), *shapes],
        scratch_shapes=[pltpu.VMEM((3, D, D), BF), pltpu.SemaphoreType.DMA((3,))],
        compiler_params=params(20),
        cost_estimate=cost(4 * HALF * D * 3 * D, 10e6),
        name="project_back",
    )(places.where, stream, dq, dkv, far, dz, grads, final_grads, own, *near)


class Places:
    def __init__(self):
        self.ndp = lax.axis_size("dp")
        self.section = lax.axis_index("section")
        self.dp = lax.axis_index("dp")
        self.core = self.dp % 2
        self.where = jnp.stack([self.section, self.core]).astype(jnp.int32)
        self.blk = 6 * D // self.ndp
        self.mine = 2 * (self.section % 2) + self.core
        bits = (self.section % 2 == 1, self.section // 2 == 1)
        self.is_first = self.core == 0
        self.first_bit = jnp.where(self.is_first, bits[0], bits[1])
        self.second_bit = jnp.where(self.is_first, bits[1], bits[0])

    def swap_dp(self, block, step):
        return lax.ppermute(block, "dp", [(i, i ^ step) for i in range(self.ndp)])

    def swap_core(self, block):
        return self.swap_dp(block, 1)

    def swap_plane(self, block, turn):
        return self.send(block, lambda s, d: (s ^ (1 + (d + turn) % 2), d))

    def send(self, block, route):
        pairs = []
        for s in range(SECTIONS):
            for d in range(self.ndp):
                to = route(s, d)
                pairs.append((s * self.ndp + d, to[0] * self.ndp + to[1]))
        return lax.ppermute(block, ("section", "dp"), pairs)


def pick(stack, index):
    return lax.dynamic_index_in_dim(stack, index, 0, keepdims=False)


ANYWHERE = pl.BlockSpec(memory_space=pl.ANY)


def gate_kernel(*refs):
    del refs


def gate(value, *earlier):
    return pl.pallas_call(
        gate_kernel,
        in_specs=[ANYWHERE] * (1 + len(earlier)),
        out_specs=ANYWHERE,
        out_shape=jax.ShapeDtypeStruct(value.shape, value.dtype),
        input_output_aliases={0: 0},
        cost_estimate=cost(0, 0),
        name="gate",
    )(value, *earlier)


def token_pieces(places, block):
    several = block.shape[0]
    pieces = jnp.swapaxes(block.reshape(several, 4, HALF, D // SECTIONS), 0, 1)
    got = []
    for turn in range(4):

        def route(s, d, turn=turn):
            piece = s ^ turn
            return 2 * (d % 2) + piece // 2, d - d % 2 + piece % 2

        got.append(places.send(pick(pieces, places.section ^ turn), route))
    return got


def in_order(pieces, mine):
    one, two = mine % 2 == 1, mine // 2 == 1
    a, b, c, d = pieces
    a, b, c, d = (
        jnp.where(one, b, a), jnp.where(one, a, b), jnp.where(one, d, c), jnp.where(one, c, d)
    )
    return (
        jnp.where(two, c, a), jnp.where(two, d, b), jnp.where(two, a, c), jnp.where(two, b, d)
    )


def deal_kernel(mine_ref, a_ref, b_ref, c_ref, later_ref, *out_refs):
    width = D // SECTIONS
    for k, ref in enumerate((a_ref, b_ref, c_ref)):
        rows = ref[...]
        features = [rows[:, f * width : (f + 1) * width] for f in range(SECTIONS)]
        for out_ref, piece in zip(out_refs, in_order(features, mine_ref[0]), strict=True):
            out_ref[k] = piece


def tokens_out(places, rows, later):
    width = D // SECTIONS
    features = pl.pallas_call(
        deal_kernel,
        grid=(1,),
        in_specs=[SCALAR, *[whole(HALF, D)] * 3, pl.BlockSpec(memory_space=pl.ANY)],
        out_specs=[pl.BlockSpec((3, HALF, width), lambda i: (0, 0, 0))] * SECTIONS,
        out_shape=[jax.ShapeDtypeStruct((3, HALF, width), BF)] * SECTIONS,
        compiler_params=params(),
        cost_estimate=cost(0, 4e6),
        name="deal",
    )(places.mine.reshape(1).astype(jnp.int32), *rows, later)
    got = []
    for turn in range(4):

        def route(s, d, turn=turn):
            return (2 * (s % 2) + d % 2) ^ turn, d - d % 2 + s // 2

        got.append(places.send(features[turn], route))
    return got


def undeal_kernel(section_ref, a_ref, b_ref, c_ref, d_ref, later_ref, x_ref, y_ref, z_ref):
    refs = (a_ref, b_ref, c_ref, d_ref)
    for k, out_ref in enumerate((x_ref, y_ref, z_ref)):
        pieces = in_order([ref[k] for ref in refs], section_ref[0])
        for number, piece in enumerate(pieces):
            out_ref[number * HALF : (number + 1) * HALF] = piece.astype(out_ref.dtype)


def tokens_placed(places, pieces, types, later):
    width = D // SECTIONS
    return pl.pallas_call(
        undeal_kernel,
        grid=(1,),
        in_specs=[SCALAR, *[pl.BlockSpec((3, HALF, width), lambda i: (0, 0, 0))] * 4, ANYWHERE],
        out_specs=[whole(4 * HALF, width)] * 3,
        out_shape=[shaped(4 * HALF, width, kind) for kind in types],
        compiler_params=params(),
        cost_estimate=cost(0, 4e6),
        name="undeal",
    )(places.section.reshape(1).astype(jnp.int32), *pieces, later)


def gather_start(places, mine, *earlier):
    one = places.swap_plane(mine, 0)
    two = places.swap_plane(mine, 1)
    return one, two, places.swap_plane(gate(one, *earlier) if earlier else one, 1)


def gather_finish(places, pieces):
    return (*pieces, *(places.swap_core(piece) for piece in pieces))


class Reduction:
    def __init__(self, places):
        self.places = places

    def cores(self, keep, give):
        return keep, self.places.swap_core(give)

    def plane_one(self, sums):
        places = self.places
        which = 2 * places.first_bit.astype(jnp.int32) + places.core

        def of(section, parts):
            blocks = [kept + got for kept, got in parts[section]]
            if section == 0:
                blocks = [jnp.zeros_like(blocks[0])] + blocks
            return jnp.concatenate(blocks, axis=0) if len(blocks) > 1 else blocks[0]

        def rows(bit, core):
            return ((0, 2 - core), (1 + core, 3))[bit]

        def sending(bit, core):
            return lambda parts: jnp.stack([of(k, parts) for k in rows(1 - bit, core)])

        def holding(bit, core):
            return lambda parts: jnp.stack([of(k, parts) for k in rows(bit, core)])

        cases = [(bit, core) for bit in range(2) for core in range(2)]
        self.got = places.swap_plane(
            lax.switch(which, [sending(*case) for case in cases], sums), 0
        )
        self.hold = lambda sums: lax.switch(which, [holding(*case) for case in cases], sums)
        self.sums = sums

    def plane_two(self, kept, got):
        places = self.places
        half = kept.shape[0]
        last = kept + got
        last = last + places.swap_plane(last, 0)
        rest = self.sums[0][0]
        held = self.hold([[(gate(rest[0], got), rest[1])], *self.sums[1:]])
        second = places.second_bit.astype(jnp.int32)

        def of(number):
            blocks = pick(held, number) + pick(self.got, number)
            late = jnp.logical_and(number == 0, jnp.logical_not(places.first_bit))
            return jnp.concatenate([jnp.where(late, last, blocks[:half]), blocks[half:]], axis=0)

        return of(second) + places.swap_plane(of(1 - second), 1)

    def shared(self, rows):
        return jnp.where(self.places.is_first, rows, self.places.swap_core(rows))

    def depth(self, blocks):
        places = self.places
        place = places.dp // 2
        if blocks.shape[0] == 4:
            near, far = place % 2, place // 2
            mine = jnp.where(places.is_first, near, 2 * far)
            theirs = jnp.where(places.is_first, 1 - near, 2 - 2 * far)
            step = 2 - places.core

            def two(first):
                return jnp.stack([pick(blocks, first), pick(blocks, first + step)])

            blocks = two(mine) + places.send(two(theirs), lambda s, d: (s, d ^ (2 + 2 * (d % 2))))
            mine = jnp.where(places.is_first, far, near)
            got = places.send(pick(blocks, 1 - mine), lambda s, d: (s, d ^ (4 - 2 * (d % 2))))
            return pick(blocks, mine).astype(F32) + got.astype(F32), blocks
        bit = 1
        while blocks.shape[0] > 1:
            pairs = blocks.reshape(-1, 2, *blocks.shape[1:])
            mine = (place // bit) % 2
            keep = lax.dynamic_index_in_dim(pairs, mine, 1, keepdims=False)
            give = lax.dynamic_index_in_dim(pairs, 1 - mine, 1, keepdims=False)
            blocks = keep + places.swap_dp(give, 2 * bit)
            bit *= 2
        return blocks[0].astype(F32), blocks


def on_device(
    stream_input,
    accum_input,
    section_weights,
    section_norms,
    final_norm,
    seq_lengths,
    out_cotangent,
):
    places = Places()
    section, core = places.section, places.core
    width = D // SECTIONS
    rows = D // 2

    own = section_weights[0]
    pieces = token_pieces(places, stream_input[None])
    near_pieces = gather_start(
        places, lax.dynamic_slice(own, (core * rows, 0), (rows, 4 * D)), *pieces
    )
    small = jnp.stack(
        [section_norms.reshape(2 * D), jnp.pad(final_norm.reshape(2 * width), (0, 2 * D - 2 * width))]
    )
    late_mine = jnp.concatenate(
        [
            lax.dynamic_slice(own, (core * rows, 4 * D), (rows, 2 * D)),
            jnp.pad(small, ((0, 14), (0, 0))),
        ],
        axis=0,
    )
    late_pieces = gather_start(places, gate(late_mine, near_pieces[2]))
    near = gather_finish(places, near_pieces)
    late = gather_finish(places, late_pieces)
    stream = jnp.concatenate(in_order([piece[0] for piece in pieces], places.mine), axis=1)
    one, two, three = (piece[rows : rows + 2] for piece in late_pieces)
    table = in_order(
        (small, jnp.where(core == 0, one, two), jnp.where(core == 0, two, one), three), section
    )
    norms = jnp.stack(table).reshape(SECTIONS, 4 * D).astype(F32)

    other_lengths = places.swap_core(seq_lengths)
    lengths = pick(jnp.where(core == section // 2, seq_lengths, other_lengths), section % 2)
    ending = jnp.cumsum(lengths, dtype=jnp.int32)

    def rows_of(which):
        spots = which * HALF + jnp.arange(HALF, dtype=jnp.int32)
        segment = jnp.sum(
            (spots[:, None] >= ending[None, :]).astype(jnp.int32), axis=1, dtype=jnp.int32
        )
        lane = jnp.arange(LANES, dtype=jnp.int32)
        hot = (segment[:, None] == lane[None, :]).astype(BF)
        alive = (spots < ending[-1]).astype(F32)
        return segment, hot, jnp.broadcast_to(alive[:, None], (HALF, LANES))

    segment_own, kseg_own, live = rows_of(core)
    _, kseg_other, _ = rows_of(1 - core)
    lane = jnp.arange(LANES, dtype=jnp.int32)
    qseg = jnp.where(
        (segment_own[:, None] != lane[None, :]) & (lane[None, :] < 32), -FAR, 0.0
    ).astype(BF)
    segs = (qseg, kseg_own, kseg_other)

    both = token_pieces(places, jnp.stack([accum_input, out_cotangent]))

    branch_sum = jnp.zeros((HALF, D), F32)
    kept = []
    for layer in (0, 2):
        queries, own_kv = project(places, stream, own, near, layer)
        far_kv = places.swap_core(own_kv)
        context, lse, middle, sum_a, branch_sum = attend(
            places, stream, queries, own_kv, far_kv, segs, own, near, layer, norms, branch_sum
        )
        following, sum_f, branch_sum = feed(
            places, middle, own, near, late, layer + 1, norms, branch_sum,
            BF if layer == 0 else F32,
        )
        kept.append((stream, queries, own_kv, far_kv, context, lse, sum_a, middle, sum_f))
        stream = following

    result, dy_low, upstream, dy, final_grad = finish(
        places, stream, branch_sum, both, live, norms
    )

    sums = [None] * SECTIONS
    reduction = Reduction(places)
    for layer in (2, 0):
        entering, queries, own_kv, far_kv, context, lse, sum_a, middle, sum_f = kept[layer // 2]
        upstream, inner, keep, give = feed_back(
            places, middle, sum_f, upstream, dy, own, near, late, layer + 1, norms, final_grad
        )
        sums[layer + 1] = [reduction.cores(keep, give)]
        dz, dctx, delta, grads, keep, give = outward_back(
            places, sum_a, upstream, dy, context, own, near, layer, norms, final_grad, inner
        )
        later_half = reduction.cores(keep, give)
        if not layer:
            sums[layer] = [later_half]
            reduction.plane_one(sums)
        dq, dkv_far = scores_back(
            queries, far_kv, dctx, qseg, segs[2], lse, delta, jnp.zeros((HALF, D), F32), BF
        )
        from_far = places.swap_core(dkv_far)
        dq, dkv = scores_back(queries, own_kv, dctx, qseg, segs[1], lse, delta, dq, F32)
        upstream, keep, give = project_back(
            places, entering, dq, dkv, from_far, dz, own, near, layer, grads, final_grad
        )
        first_half = reduction.cores(keep, give)
        if layer:
            sums[layer] = [first_half, later_half]
    blocks = reduction.plane_two(*first_half)
    reduced, early = reduction.depth(blocks)
    shared = reduction.shared(reduced[places.blk :])
    stream_out, result_out, accum_out = tokens_placed(
        places, tokens_out(places, (upstream, result, dy_low), blocks), (F32, BF, F32), early
    )
    slab = reduced[: places.blk].T
    cut = D // places.ndp
    norm_out = lax.dynamic_slice(reduced, (places.blk, places.dp * cut), (2, cut))
    final_out = lax.dynamic_slice(shared, (2, section * width), (2, width))

    return (
        result_out,
        stream_out,
        accum_out,
        slab[None],
        norm_out[None],
        final_out,
    )


def solution(mesh):
    placed = (
        P("dp", "section"),
        P("dp", "section"),
        P("section", None, None),
        P("section", None, None),
        P(None, "section"),
        P("dp", None),
        P("dp", "section"),
    )
    return jax.shard_map(
        on_device,
        mesh=mesh,
        in_specs=placed,
        out_specs=(
            P("dp", "section"),
            P("dp", "section"),
            P("dp", "section"),
            P("section", None, "dp"),
            P("section", None, "dp"),
            P(None, "section"),
        ),
        check_vma=False,
    )
```

```python
import functools
import math

import jax
import jax.numpy as jnp
from jax import lax
from jax.experimental import pallas as pl
from jax.experimental.pallas import tpu as pltpu
from jax.sharding import PartitionSpec as P

D = 512
HEADS = 8
HEAD = 64
PACK = 1024
HALF = PACK // 2
PAIRS = HEADS // 2
LANES = 2 * HEAD
SECTIONS = 4
FAR = 1e30
SCALE = HEAD ** (-0.5)
BF = jnp.bfloat16
F32 = jnp.float32
NT = (((1,), (1,)), ((), ()))
TN = (((0,), (0,)), ((), ()))


def mm(left, right):
    return jnp.dot(left, right, preferred_element_type=F32)


def mm_nt(left, right):
    return lax.dot_general(left, right, NT, preferred_element_type=F32)


def mm_tn(left, right):
    return lax.dot_general(left, right, TN, preferred_element_type=F32)


def params(megabytes=16):
    return pltpu.CompilerParams(
        dimension_semantics=("arbitrary",), vmem_limit_bytes=megabytes * 1024 * 1024
    )


def shaped(rows, cols, dtype):
    return jax.ShapeDtypeStruct((rows, cols), dtype)


def in_hbm(array):
    return pltpu.with_memory_space_constraint(array, pltpu.HBM)


def whole(rows, cols):
    return pl.BlockSpec((rows, cols), lambda i: (0, 0))


SCALAR = pl.BlockSpec(memory_space=pltpu.SMEM)


def cost(flops, moved, transcendentals=0):
    return pl.CostEstimate(
        flops=int(flops), bytes_accessed=int(moved), transcendentals=int(transcendentals)
    )


def gain_of(table_ref, layer):
    return table_ref[layer : layer + 1, :D]


def shift_of(table_ref, layer):
    return table_ref[layer : layer + 1, D : 2 * D]


def norm_parts(summed):
    average = jnp.mean(summed, axis=-1, keepdims=True)
    centered = summed - average
    spread = jnp.mean(centered * centered, axis=-1, keepdims=True)
    inverse = lax.rsqrt(spread + 1e-05)
    return centered * inverse, inverse


def norm_forward(summed, table_ref, layer):
    normal, _ = norm_parts(summed)
    return normal * gain_of(table_ref, layer) + shift_of(table_ref, layer)


def norm_back(summed, gain, upstream):
    normal, inverse = norm_parts(summed)
    scaled = upstream * gain
    mean_one = jnp.mean(scaled, axis=-1, keepdims=True)
    mean_two = jnp.mean(scaled * normal, axis=-1, keepdims=True)
    grad = (scaled - mean_one - normal * mean_two) * inverse
    gain_grad = jnp.sum(upstream * normal, axis=0, keepdims=True)
    shift_grad = jnp.sum(upstream, axis=0, keepdims=True)
    return grad, gain_grad, shift_grad


def head_mask(which):
    lane = lax.broadcasted_iota(jnp.int32, (1, LANES), 1)
    return (lane // HEAD) == which


def three_way(column):
    high = column.astype(BF)
    rest = column - high.astype(F32)
    middle = rest.astype(BF)
    low = (rest - middle.astype(F32)).astype(BF)
    return high, middle, low


GROUP = 6


def fetch(where_ref, layer, own_ref, piece_refs, own_first, first, width, target, sem):
    section, core = where_ref[0], where_ref[1]
    half = D // 2
    step = section ^ layer
    mine_rows = pl.ds(pl.multiple_of(core * half, half), half)
    far_rows = pl.ds(pl.multiple_of((1 - core) * half, half), half)

    @pl.when(step == 0)
    def _():
        pltpu.make_async_copy(own_ref.at[:, pl.ds(own_first, width)], target, sem).start()

    for number, (partner, far_number) in enumerate(((1 + core, 1), (2 - core, 0), (3, 2))):

        @pl.when(step == partner)
        def _():
            part = (pl.ds(0, half), pl.ds(first, width))
            mine, far = piece_refs[number].at[part], piece_refs[3 + far_number].at[part]
            pltpu.make_async_copy(mine, target.at[mine_rows], sem).start()
            pltpu.make_async_copy(far, target.at[far_rows], sem).start()


def arrived(own_ref, width, target, sem):
    pltpu.make_async_copy(own_ref.at[:, pl.ds(0, width)], target, sem).wait()


def weight_specs(groups):
    return [pl.BlockSpec(memory_space=pl.ANY)] * (1 + GROUP * groups)


def column_of(pair):
    return pl.ds(pl.multiple_of(pair * LANES, LANES), LANES)


def fetch_projection(layer, where_ref, own_ref, near, weight_ref, sems):
    for part in range(3):
        fetch(
            where_ref, layer, own_ref, near, part * D, part * D, D, weight_ref.at[part],
            sems.at[part],
        )


def fetch_outward(layer, where_ref, own_ref, near, weight_ref, sem):
    fetch(where_ref, layer, own_ref, near, 3 * D, 3 * D, D, weight_ref, sem)


def fetch_feed(layer, where_ref, own_ref, near, late, weight_ref, sems):
    for chunk in range(4):
        turn = chunk % 2
        if chunk < 2:
            inner = (layer - 1, late, (4 + turn) * D, turn * D)
            outer = (layer, near, (2 + turn) * D, (2 + turn) * D)
        else:
            inner = (layer, near, turn * D, turn * D)
            outer = (layer, late, (4 + turn) * D, turn * D)
        for number, (whose, pieces, own_first, first) in enumerate((inner, outer)):
            fetch(
                where_ref, whose, own_ref, pieces, own_first, first, D,
                weight_ref.at[chunk, number], sems.at[chunk, number],
            )


PROJECTION = [pltpu.VMEM((3, D, D), BF), pltpu.SemaphoreType.DMA((3,))]
OUTWARD = [pltpu.VMEM((D, D), BF), pltpu.SemaphoreType.DMA]
FEED = [pltpu.VMEM((4, 2, D, D), BF), pltpu.SemaphoreType.DMA((4, 2))]


def put_projection(own_ref, x, q_ref, kv_ref, weight_ref, sems):
    def times(part):
        arrived(own_ref, D, weight_ref.at[part], sems.at[part])
        return mm(x, weight_ref[part]).astype(BF)

    q_ref[...] = times(0)
    keys, values = times(1), times(2)
    for pair in range(PAIRS):
        lanes = slice(pair * LANES, (pair + 1) * LANES)
        kv_ref[pair, :, :LANES] = keys[:, lanes]
        kv_ref[pair, :, LANES:] = values[:, lanes]


def put_attention(q_ref, own_ref, far_ref, qs_ref, kso_ref, ksx_ref, ctx_ref, lse_ref):
    none = jnp.zeros((), BF)
    lane = lax.broadcasted_iota(jnp.int32, (1, LANES), 1)
    ones = jnp.ones((HALF, LANES), BF)
    lse_ref[...] = jnp.zeros((HALF, LANES), F32)

    @pl.loop(0, PAIRS)
    def _(pair):
        q = q_ref[:, column_of(pair)] * jnp.asarray(SCALE, BF)
        keys_own = jnp.concatenate([own_ref[pair, :, :LANES], kso_ref[...]], axis=1)
        keys_other = jnp.concatenate([far_ref[pair, :, :LANES], ksx_ref[...]], axis=1)
        values_own, values_other = own_ref[pair, :, LANES:], far_ref[pair, :, LANES:]
        context = jnp.zeros((HALF, LANES), F32)
        logs = lse_ref[...]
        for which in range(2):
            mask = head_mask(which)
            query = jnp.concatenate([jnp.where(mask, q, none), qs_ref[...]], axis=1)
            score_own = mm_nt(query, keys_own)
            score_other = mm_nt(query, keys_other)
            peak = jnp.maximum(
                jnp.max(score_own, axis=1, keepdims=True),
                jnp.max(score_other, axis=1, keepdims=True),
            )
            own = jnp.exp(score_own - peak).astype(BF)
            other = jnp.exp(score_other - peak).astype(BF)
            total = mm(
                own, jnp.concatenate([jnp.where(mask, values_own, none), ones], axis=1)
            ) + mm(other, jnp.concatenate([jnp.where(mask, values_other, none), ones], axis=1))
            row_total = total[:, LANES:]
            context = context + total[:, :LANES] / row_total
            logs = jnp.where(lane == 2 * pair + which, peak + jnp.log(row_total), logs)
        lse_ref[...] = logs
        ctx_ref[:, column_of(pair)] = context.astype(BF)


def gelu_parts(v):
    root = 0.7978845608028654
    squared = v * v
    inner = root * (v + 0.044715 * v * squared)
    t = jnp.tanh(inner)
    hidden = 0.5 * v * (1.0 + t)
    slope = 0.5 * (1.0 + t) + 0.5 * v * (1.0 - t * t) * (root * (1.0 + 3 * 0.044715 * squared))
    return hidden, slope


def feed_weight(own_ref, weight_ref, sems, chunk, number):
    arrived(own_ref, D, weight_ref.at[chunk, number], sems.at[chunk, number])
    return weight_ref[chunk, number]


def split_rows(core, blk, row, value, keep_ref, give_ref):
    step = math.gcd(D, blk)
    for k in range(value.shape[0] // step):
        part = value[k * step : (k + 1) * step]
        first = row + k * step
        block, offset = first // blk, first % blk

        @pl.when(block % 2 == core)
        def _():
            keep_ref[block // 2, offset : offset + step, :] = part

        @pl.when(block % 2 != core)
        def _():
            give_ref[block // 2, offset : offset + step, :] = part


def side_rows(grads, final_grads, keep_ref, give_ref):
    extra = jnp.concatenate([grads, final_grads, jnp.zeros((12, D), F32)], axis=0).astype(BF)
    blk = keep_ref.shape[1] - 16
    for block in range(keep_ref.shape[0]):
        keep_ref[block, blk:, :] = extra
        give_ref[block, blk:, :] = extra


def split_shapes(count, blk):
    return [full(count, blk + 16, D)] * 2, [pltpu.HBM((count, blk + 16, D), BF)] * 2


def put_outward_back(
    summed, upstream, dy, context, gain, weight_of, dctx_ref, delta_ref, grad_ref, rest_ref
):
    grad, gain_grad, shift_grad = norm_back(summed, gain, upstream)
    grad_ref[...] = jnp.concatenate([gain_grad, shift_grad], axis=0)
    df = (grad + dy).astype(BF)
    rest_ref[:D] = mm_tn(df, context).astype(BF)
    context_grad = mm_nt(df, weight_of()).astype(BF)
    dctx_ref[...] = context_grad
    product = context.astype(F32) * context_grad.astype(F32)
    lane = lax.broadcasted_iota(jnp.int32, (1, LANES), 1)
    delta = jnp.zeros((HALF, LANES), F32)
    for head in range(HEADS):
        part = product[:, (head // 2) * LANES : (head // 2 + 1) * LANES]
        inner = jnp.sum(jnp.where(head_mask(head % 2), part, 0.0), axis=1, keepdims=True)
        delta = jnp.where(lane == head, inner, delta)
    delta_ref[...] = delta
    return grad


def put_feed_back(
    core, x, hidden_of, df, grad, weight_of, rest_ref, keep_ref, give_ref
):
    blk = keep_ref.shape[1] - 16
    total = grad
    for chunk in range(4):
        inner, outer = weight_of(chunk, 0), weight_of(chunk, 1)
        hidden, slope = hidden_of(chunk, inner)
        split_rows(core, blk, (2 + chunk) * D, mm_tn(hidden, df).astype(BF), keep_ref, give_ref)
        preact_grad = (mm(df, outer) * slope).astype(BF)
        inner_grad = mm_tn(preact_grad, x).astype(BF)
        if chunk < 2:
            rest_ref[(1 + chunk) * D : (2 + chunk) * D] = inner_grad
        else:
            split_rows(core, blk, (chunk - 2) * D, inner_grad, keep_ref, give_ref)
        total = total + mm_nt(preact_grad, inner)
    return total


def put_project_back(
    core, x, dq_ref, dkv_ref, far_ref, dz, grads, final_grads, rest_ref, weight_of, keep_ref,
    give_ref,
):
    blk = keep_ref.shape[1] - 16
    side_rows(grads, final_grads, keep_ref, give_ref)
    split_rows(core, blk, 3 * D, rest_ref[...], keep_ref, give_ref)
    parts = [(dkv_ref[k].astype(F32) + far_ref[k].astype(F32)).astype(BF) for k in range(PAIRS)]
    dk = jnp.concatenate([part[:, :LANES] for part in parts], axis=1)
    dv = jnp.concatenate([part[:, LANES:] for part in parts], axis=1)
    total = dz
    for place, grad in enumerate((dq_ref[...].astype(BF), dk, dv)):
        split_rows(core, blk, place * D, mm_tn(grad, x).astype(BF), keep_ref, give_ref)
        total = total + mm_nt(grad, weight_of(place))
    return total


def full(*shape):
    return pl.BlockSpec(shape, lambda i: (0,) * len(shape), pipeline_mode=pl.Buffered(1))


KV = (PAIRS, HALF, 2 * LANES)
TABLE = (SECTIONS, 4 * D)


def project_kernel(layer, where_ref, x_ref, own_ref, *refs):
    near, (q_ref, kv_ref, weight_ref, sems) = refs[:GROUP], refs[GROUP:]
    fetch_projection(layer, where_ref, own_ref, near, weight_ref, sems)
    put_projection(own_ref, x_ref[...], q_ref, kv_ref, weight_ref, sems)


def project(places, stream, own, near, layer):
    return pl.pallas_call(
        functools.partial(project_kernel, layer),
        grid=(1,),
        in_specs=[SCALAR, full(HALF, D), *weight_specs(1)],
        out_specs=[full(HALF, D), full(*KV)],
        out_shape=[shaped(HALF, D, BF), jax.ShapeDtypeStruct(KV, BF)],
        scratch_shapes=PROJECTION,
        compiler_params=params(),
        cost_estimate=cost(2 * HALF * D * 3 * D, 4e6),
        name="project",
    )(places.where, stream, *map(in_hbm, (own, *near)))


def layer_kernel(
    layer, where_ref, q_ref, own_kv_ref, far_kv_ref, qs_ref, kso_ref, ksx_ref, x_ref, norm_ref,
    own_ref, *refs,
):
    near, late, refs = refs[:GROUP], refs[GROUP : 2 * GROUP], refs[2 * GROUP :]
    (
        ctx_ref, lse_ref, middle_ref, sum_a_ref, sum_f_ref, branch_ref, next_ref, q_next_ref,
        kv_next_ref, outward_ref, outward_sem, feed_ref, feed_sems, project_ref, project_sems,
    ) = refs
    fetch_outward(layer, where_ref, own_ref, near, outward_ref, outward_sem)
    fetch_feed(layer + 1, where_ref, own_ref, near, late, feed_ref, feed_sems)
    fetch_projection(layer + 2, where_ref, own_ref, near, project_ref, project_sems)
    put_attention(
        q_ref, own_kv_ref, far_kv_ref, qs_ref, kso_ref, ksx_ref, ctx_ref, lse_ref
    )
    arrived(own_ref, D, outward_ref, outward_sem)
    branch = mm(ctx_ref[...], outward_ref[...])
    summed = x_ref[...].astype(F32) + branch
    sum_a_ref[...] = summed
    middle = norm_forward(summed, norm_ref, layer).astype(BF)
    middle_ref[...] = middle
    total = jnp.zeros((HALF, D), F32)
    for chunk in range(4):
        inner = feed_weight(own_ref, feed_ref, feed_sems, chunk, 0)
        hidden = gelu_parts(mm(middle, inner))[0].astype(BF)
        total = total + mm_nt(hidden, feed_weight(own_ref, feed_ref, feed_sems, chunk, 1))
    summed = middle.astype(F32) + total
    sum_f_ref[...] = summed
    branch_ref[...] = branch + total
    following = norm_forward(summed, norm_ref, layer + 1).astype(BF)
    next_ref[...] = following
    put_projection(own_ref, following, q_next_ref, kv_next_ref, project_ref, project_sems)


def first_layer(places, stream, queries, own_kv, far_kv, segs, own, near, late, norms):
    return pl.pallas_call(
        functools.partial(layer_kernel, 0),
        grid=(1,),
        in_specs=[
            SCALAR, full(HALF, D), full(*KV), full(*KV), *[full(HALF, LANES)] * 3, full(HALF, D),
            full(*TABLE), *weight_specs(2),
        ],
        out_specs=[
            full(HALF, D), full(HALF, LANES), *[full(HALF, D)] * 6, full(*KV),
        ],
        out_shape=[
            shaped(HALF, D, BF), shaped(HALF, LANES, F32), shaped(HALF, D, BF),
            shaped(HALF, D, F32), shaped(HALF, D, F32), shaped(HALF, D, F32), shaped(HALF, D, BF),
            shaped(HALF, D, BF), jax.ShapeDtypeStruct(KV, BF),
        ],
        scratch_shapes=[*OUTWARD, *FEED, *PROJECTION],
        compiler_params=params(30),
        cost_estimate=cost(14e9, 20e6, 4e6),
        name="first_layer",
    )(
        places.where, queries, own_kv, far_kv, *segs, stream, norms, *map(in_hbm, (own, *near, *late))
    )


def attend_kernel(
    layer, where_ref, q_ref, own_kv_ref, far_kv_ref, qs_ref, kso_ref, ksx_ref, x_ref, norm_ref,
    own_ref, *refs,
):
    near, refs = refs[:GROUP], refs[GROUP:]
    ctx_ref, lse_ref, middle_ref, sum_ref, outward_ref, outward_sem = refs
    fetch_outward(layer, where_ref, own_ref, near, outward_ref, outward_sem)
    put_attention(
        q_ref, own_kv_ref, far_kv_ref, qs_ref, kso_ref, ksx_ref, ctx_ref, lse_ref
    )
    arrived(own_ref, D, outward_ref, outward_sem)
    summed = x_ref[...].astype(F32) + mm(ctx_ref[...], outward_ref[...])
    sum_ref[...] = summed
    middle_ref[...] = norm_forward(summed, norm_ref, layer).astype(BF)


def second_attention(places, stream, queries, own_kv, far_kv, segs, own, near, norms):
    return pl.pallas_call(
        functools.partial(attend_kernel, 2),
        grid=(1,),
        in_specs=[
            SCALAR, full(HALF, D), full(*KV), full(*KV), *[full(HALF, LANES)] * 3, full(HALF, D),
            full(*TABLE), *weight_specs(1),
        ],
        out_specs=[full(HALF, D), full(HALF, LANES), full(HALF, D), full(HALF, D)],
        out_shape=[
            shaped(HALF, D, BF), shaped(HALF, LANES, F32), shaped(HALF, D, BF),
            shaped(HALF, D, F32),
        ],
        scratch_shapes=OUTWARD,
        compiler_params=params(),
        cost_estimate=cost(9e9, 10e6, 4e6),
        name="second_attention",
    )(places.where, queries, own_kv, far_kv, *segs, stream, norms, *map(in_hbm, (own, *near)))


def turn_kernel(
    layer, where_ref, middle_ref, x_ref, sum_ref, ctx_ref, norm_ref, branch_ref,
    a_ref, b_ref, c_ref, d_ref, live_ref, own_ref, *refs,
):
    near, late, refs = refs[:GROUP], refs[GROUP : 2 * GROUP], refs[2 * GROUP :]
    (
        result_ref, low_ref, dy_ref, final_ref, dz_ref, dctx_ref, delta_ref, grad_ref,
        feed_keep, feed_give, rest_ref,
        hidden_ref, slope_ref, outward_ref, outward_sem, feed_ref, feed_sems,
    ) = refs
    core, mine = where_ref[1], where_ref[2]
    fetch_feed(layer + 1, where_ref, own_ref, near, late, feed_ref, feed_sems)
    fetch_outward(layer, where_ref, own_ref, near, outward_ref, outward_sem)
    middle, sum_a = middle_ref[...], sum_ref[...]
    branch = sum_a - x_ref[...].astype(F32)
    total = jnp.zeros((HALF, D), F32)
    for chunk in range(4):
        inner = feed_weight(own_ref, feed_ref, feed_sems, chunk, 0)
        hidden, slope = gelu_parts(mm(middle, inner))
        hidden = hidden.astype(BF)
        hidden_ref[chunk] = hidden
        slope_ref[chunk] = slope
        total = total + mm_nt(hidden, feed_weight(own_ref, feed_ref, feed_sems, chunk, 1))
    sum_f = middle.astype(F32) + total
    last = norm_forward(sum_f, norm_ref, layer + 1)

    pieces = in_order([ref[...] for ref in (a_ref, b_ref, c_ref, d_ref)], mine)
    accum, cot = (jnp.concatenate([piece[k] for piece in pieces], axis=1) for k in range(2))
    summed = accum.astype(F32) + (branch_ref[...] + (branch + total))
    normal, _ = norm_parts(summed)
    width = D // SECTIONS
    gain, shift = (
        jnp.concatenate(
            [
                norm_ref[k : k + 1, 2 * D + part * width : 2 * D + (part + 1) * width]
                for k in range(SECTIONS)
            ],
            axis=1,
        )
        for part in range(2)
    )
    result_ref[...] = (last + normal * gain + shift).astype(BF)
    cot = cot.astype(F32) * live_ref[:, 0:1]
    dy, gain_grad, shift_grad = norm_back(summed, gain, cot)
    dy_ref[...] = dy
    low_ref[...] = dy.astype(BF)
    final_grads = jnp.concatenate([gain_grad, shift_grad], axis=0)
    final_ref[...] = final_grads

    grad, gain_grad, shift_grad = norm_back(sum_f, gain_of(norm_ref, layer + 1), cot)
    side_rows(
        jnp.concatenate([gain_grad, shift_grad], axis=0), final_grads, feed_keep, feed_give
    )
    upstream = put_feed_back(
        core, middle, lambda chunk, inner: (hidden_ref[chunk], slope_ref[chunk]),
        (grad + dy).astype(BF), grad, lambda chunk, number: feed_ref[chunk, number],
        rest_ref, feed_keep, feed_give,
    )
    arrived(own_ref, D, outward_ref, outward_sem)
    dz_ref[...] = put_outward_back(
        sum_a, upstream.astype(BF).astype(F32), dy, ctx_ref[...], gain_of(norm_ref, layer),
        lambda: outward_ref[...], dctx_ref, delta_ref, grad_ref, rest_ref,
    )


def turn(places, middle, stream, sum_a, context, own, near, late, norms, branch_sum, pieces, live):
    specs, shapes = split_shapes(places.ndp // 2, places.blk)
    return pl.pallas_call(
        functools.partial(turn_kernel, 2),
        grid=(1,),
        in_specs=[
            SCALAR, *[full(HALF, D)] * 4, full(*TABLE), full(HALF, D),
            *[full(2, HALF, D // SECTIONS)] * 4, full(HALF, LANES), *weight_specs(2),
        ],
        out_specs=[
            *[full(HALF, D)] * 3, full(2, D), full(HALF, D), full(HALF, D),
            full(HALF, LANES), full(2, D), *specs, full(3 * D, D),
        ],
        out_shape=[
            shaped(HALF, D, BF), shaped(HALF, D, BF),
            shaped(HALF, D, F32), shaped(2, D, F32), shaped(HALF, D, F32), shaped(HALF, D, BF),
            shaped(HALF, LANES, F32), shaped(2, D, F32), *shapes, shaped(3 * D, D, BF),
        ],
        scratch_shapes=[
            pltpu.VMEM((4, HALF, D), BF), pltpu.VMEM((4, HALF, D), F32), *OUTWARD, *FEED,
        ],
        compiler_params=params(40),
        cost_estimate=cost(16e9, 30e6, 2e6),
        name="turn",
    )(
        places.where, middle, stream, sum_a, context, norms, branch_sum, *pieces, live, *map(in_hbm, (own, *near, *late)),
    )


def column():
    return pl.BlockSpec((HALF, LANES), lambda i: (0, i))


def pair_block():
    return pl.BlockSpec((1, HALF, 2 * LANES), lambda i: (i, 0, 0))


def scores_back_kernel(
    q_ref, kv_ref, dctx_ref, qs_ref, ks_ref, lse_ref, delta_ref, before_ref, dq_ref, dkv_ref
):
    pair = pl.program_id(0)
    none = jnp.zeros((), BF)
    lane = lax.broadcasted_iota(jnp.int32, (1, LANES), 1)
    q = q_ref[...] * jnp.asarray(SCALE, BF)
    k = kv_ref[0, :, :LANES]
    k_scaled = k * jnp.asarray(SCALE, BF)
    dctx = dctx_ref[...]
    extra = jnp.where((lane >= LANES - 3), jnp.ones((), BF), none)
    keys = jnp.concatenate([k, ks_ref[...] + extra], axis=1)
    values = jnp.concatenate(
        [kv_ref[0, :, LANES:], jnp.broadcast_to(extra, (HALF, LANES))], axis=1
    )
    dq = before_ref[...]
    dk = jnp.zeros((HALF, LANES), F32)
    dv = jnp.zeros((HALF, LANES), F32)
    for which in range(2):
        mask = head_mask(which)
        here = lane == 2 * pair + which

        def lanes_of(table, base):
            column = -jnp.sum(jnp.where(here, table, 0.0), axis=1, keepdims=True)
            high, middle, low = three_way(column)
            base = jnp.where(lane == LANES - 3, high, base)
            base = jnp.where(lane == LANES - 2, middle, base)
            return jnp.where(lane == LANES - 1, low, base)

        query_part = jnp.where(mask, q, none)
        dctx_part = jnp.where(mask, dctx, none)
        query = jnp.concatenate([query_part, lanes_of(lse_ref[...], qs_ref[...])], axis=1)
        dcontext = jnp.concatenate(
            [dctx_part, lanes_of(delta_ref[...], jnp.zeros((HALF, LANES), BF))], axis=1
        )
        probability = jnp.exp(mm_nt(keys, query))
        score_grad = (probability * mm_nt(values, dcontext)).astype(BF)
        dv = dv + mm(probability.astype(BF), dctx_part)
        dk = dk + mm(score_grad, query_part)
        dq = dq + mm_tn(score_grad, jnp.where(mask, k_scaled, none))
    dq_ref[...] = dq
    dkv_ref[0, :, :LANES] = dk.astype(dkv_ref.dtype)
    dkv_ref[0, :, LANES:] = dv.astype(dkv_ref.dtype)


def scores_back(queries, kv, dctx, qseg, kseg, lse, delta, before, out_type):
    return pl.pallas_call(
        scores_back_kernel,
        grid=(PAIRS,),
        in_specs=[
            column(), pair_block(), column(),
            whole(HALF, LANES), whole(HALF, LANES), whole(HALF, LANES), whole(HALF, LANES),
            column(),
        ],
        out_specs=[column(), pair_block()],
        out_shape=[
            shaped(HALF, D, F32), jax.ShapeDtypeStruct((PAIRS, HALF, 2 * LANES), out_type),
        ],
        compiler_params=params(),
        cost_estimate=cost(8e9, 8e6, 2e6),
        name="scores_back",
    )(queries, kv, dctx, qseg, kseg, lse, delta, before)


def middle_kernel(
    layer, where_ref, x_ref, dq_ref, dkv_ref, far_ref, dz_ref, dy_ref, grad_ref, final_ref,
    before_ref, middle_ref, sum_f_ref, sum_a_ref, ctx_ref, norm_ref, own_ref, *refs,
):
    near, late, refs = refs[:GROUP], refs[GROUP : 2 * GROUP], refs[2 * GROUP :]
    (
        dz_out, dctx_ref, delta_ref, grad_out, project_keep, project_give, feed_keep, feed_give,
        rest_ref,
        project_ref, project_sems, feed_ref, feed_sems, outward_ref, outward_sem,
    ) = refs
    core = where_ref[1]
    fetch_projection(layer, where_ref, own_ref, near, project_ref, project_sems)
    fetch_feed(layer - 1, where_ref, own_ref, near, late, feed_ref, feed_sems)
    fetch_outward(layer - 2, where_ref, own_ref, near, outward_ref, outward_sem)
    final_grads = final_ref[...]

    def project_weight(place):
        arrived(own_ref, D, project_ref.at[place], project_sems.at[place])
        return project_ref[place]

    def outward_weight():
        arrived(own_ref, D, outward_ref, outward_sem)
        return outward_ref[...]

    upstream = put_project_back(
        core, x_ref[...], dq_ref, dkv_ref, far_ref, dz_ref[...], grad_ref[...], final_grads,
        before_ref, project_weight, project_keep, project_give,
    ).astype(BF).astype(F32)
    dy = dy_ref[...]
    grad, gain_grad, shift_grad = norm_back(
        sum_f_ref[...], gain_of(norm_ref, layer - 1), upstream
    )
    side_rows(
        jnp.concatenate([gain_grad, shift_grad], axis=0), final_grads, feed_keep, feed_give
    )
    middle = middle_ref[...]

    def hidden_of(chunk, inner):
        hidden, slope = gelu_parts(mm(middle, inner))
        return hidden.astype(BF), slope

    upstream = put_feed_back(
        core, middle, hidden_of, (grad + dy).astype(BF), grad,
        functools.partial(feed_weight, own_ref, feed_ref, feed_sems), rest_ref, feed_keep, feed_give,
    ).astype(BF).astype(F32)
    dz_out[...] = put_outward_back(
        sum_a_ref[...], upstream, dy, ctx_ref[...], gain_of(norm_ref, layer - 2),
        outward_weight, dctx_ref, delta_ref, grad_out, rest_ref,
    )


def between(
    places, stream, dq, dkv, far, dz, dy, grads, final_grads, rest, kept, own, near, late, norms
):
    context, _, middle, sum_a, sum_f = kept
    specs, shapes = split_shapes(places.ndp // 2, places.blk)
    return pl.pallas_call(
        functools.partial(middle_kernel, 2),
        grid=(1,),
        in_specs=[
            SCALAR, full(HALF, D), full(HALF, D), full(*KV), full(*KV), full(HALF, D),
            full(HALF, D), full(2, D), full(2, D), full(3 * D, D), *[full(HALF, D)] * 4,
            full(*TABLE), *weight_specs(2),
        ],
        out_specs=[
            full(HALF, D), full(HALF, D), full(HALF, LANES), full(2, D), *specs, *specs,
            full(3 * D, D),
        ],
        out_shape=[
            shaped(HALF, D, F32), shaped(HALF, D, BF), shaped(HALF, LANES, F32),
            shaped(2, D, F32), *shapes, *shapes, shaped(3 * D, D, BF),
        ],
        scratch_shapes=[*PROJECTION, *FEED, *OUTWARD],
        compiler_params=params(44),
        cost_estimate=cost(20e9, 30e6, 2e6),
        name="between",
    )(
        places.where, stream, dq, dkv, far, dz, dy, grads, final_grads, rest, middle, sum_f,
        sum_a, context, norms, *map(in_hbm, (own, *near, *late)),
    )


def project_back_kernel(
    layer, where_ref, x_ref, dq_ref, dkv_ref, far_ref, dz_ref, grad_ref, final_ref, rest_ref,
    own_ref, *refs,
):
    near, (dx_ref, keep_ref, give_ref, weight_ref, sems) = refs[:GROUP], refs[GROUP:]
    fetch_projection(layer, where_ref, own_ref, near, weight_ref, sems)

    def weight_of(place):
        arrived(own_ref, D, weight_ref.at[place], sems.at[place])
        return weight_ref[place]

    dx_ref[...] = put_project_back(
        where_ref[1], x_ref[...], dq_ref, dkv_ref, far_ref, dz_ref[...], grad_ref[...],
        final_ref[...], rest_ref, weight_of, keep_ref, give_ref,
    ).astype(BF)


def project_back(places, stream, dq, dkv, far, dz, own, near, layer, grads, final_grads, rest):
    specs, shapes = split_shapes(places.ndp // 2, places.blk)
    return pl.pallas_call(
        functools.partial(project_back_kernel, layer),
        grid=(1,),
        in_specs=[
            SCALAR, full(HALF, D), full(HALF, D), full(*KV), full(*KV), full(HALF, D),
            full(2, D), full(2, D), full(3 * D, D), *weight_specs(1),
        ],
        out_specs=[full(HALF, D), *specs],
        out_shape=[shaped(HALF, D, BF), *shapes],
        scratch_shapes=PROJECTION,
        compiler_params=params(20),
        cost_estimate=cost(4 * HALF * D * 3 * D, 10e6),
        name="project_back",
    )(places.where, stream, dq, dkv, far, dz, grads, final_grads, rest, *map(in_hbm, (own, *near)))


class Places:
    def __init__(self):
        self.ndp = lax.axis_size("dp")
        self.section = lax.axis_index("section")
        self.dp = lax.axis_index("dp")
        self.core = self.dp % 2
        self.blk = 6 * D // self.ndp
        self.mine = 2 * (self.section % 2) + self.core
        self.where = jnp.stack([self.section, self.core, self.mine]).astype(jnp.int32)
        bits = (self.section % 2 == 1, self.section // 2 == 1)
        self.is_first = self.core == 0
        self.first_bit = jnp.where(self.is_first, bits[0], bits[1])
        self.second_bit = jnp.where(self.is_first, bits[1], bits[0])

    def swap_dp(self, block, step):
        return lax.ppermute(block, "dp", [(i, i ^ step) for i in range(self.ndp)])

    def swap_core(self, block):
        return self.swap_dp(block, 1)

    def swap_plane(self, block, turn):
        return self.send(block, lambda s, d: (s ^ (1 + (d + turn) % 2), d))

    def send(self, block, route):
        pairs = []
        for s in range(SECTIONS):
            for d in range(self.ndp):
                to = route(s, d)
                pairs.append((s * self.ndp + d, to[0] * self.ndp + to[1]))
        return lax.ppermute(block, ("section", "dp"), pairs)


def pick(stack, index):
    return lax.dynamic_index_in_dim(stack, index, 0, keepdims=False)


ANYWHERE = pl.BlockSpec(memory_space=pl.ANY)


def sequence_kernel(where_ref, own_ref, far_ref, qseg_ref, own_seg_ref, far_seg_ref, live_ref):
    section, core = where_ref[0], where_ref[1]
    here = core == section // 2
    row = section % 2
    lane = lax.broadcasted_iota(jnp.int32, (HALF, LANES), 1)
    spot = lax.broadcasted_iota(jnp.int32, (HALF, LANES), 0)
    own = jnp.zeros((HALF, LANES), jnp.int32)
    far = jnp.zeros((HALF, LANES), jnp.int32)
    ending = jnp.int32(0)
    for k in range(own_ref.shape[1]):
        ending = ending + jnp.where(here, own_ref[row, k], far_ref[row, k])
        own = own + (spot + core * HALF >= ending).astype(jnp.int32)
        far = far + (spot + (1 - core) * HALF >= ending).astype(jnp.int32)
    own_seg_ref[...] = jnp.where(own == lane, 1.0, 0.0).astype(BF)
    far_seg_ref[...] = jnp.where(far == lane, 1.0, 0.0).astype(BF)
    qseg_ref[...] = jnp.where((own != lane) & (lane < 32), -FAR, 0.0).astype(BF)
    live_ref[...] = jnp.where(spot + core * HALF < ending, 1.0, 0.0)


def sequences(places, lengths):
    return pl.pallas_call(
        sequence_kernel,
        grid=(1,),
        in_specs=[SCALAR] * 3,
        out_specs=[whole(HALF, LANES)] * 4,
        out_shape=[shaped(HALF, LANES, BF)] * 3 + [shaped(HALF, LANES, F32)],
        compiler_params=params(),
        cost_estimate=cost(1e6, 1e6),
        name="sequences",
    )(places.where, lengths, places.swap_core(lengths))


def gate_kernel(*refs):
    del refs


def gate(value, *earlier):
    return pl.pallas_call(
        gate_kernel,
        in_specs=[ANYWHERE] * (1 + len(earlier)),
        out_specs=ANYWHERE,
        out_shape=jax.ShapeDtypeStruct(value.shape, value.dtype),
        input_output_aliases={0: 0},
        cost_estimate=cost(0, 0),
        name="gate",
    )(value, *earlier)


def token_pieces(places, block):
    several = block.shape[0]
    pieces = jnp.swapaxes(block.reshape(several, 4, HALF, D // SECTIONS), 0, 1)
    got = []
    for turn in range(4):

        def route(s, d, turn=turn):
            piece = s ^ turn
            return 2 * (d % 2) + piece // 2, d - d % 2 + piece % 2

        got.append(places.send(pick(pieces, places.section ^ turn), route))
    return got


def in_order(pieces, mine):
    one, two = mine % 2 == 1, mine // 2 == 1
    a, b, c, d = pieces
    a, b, c, d = (
        jnp.where(one, b, a), jnp.where(one, a, b), jnp.where(one, d, c), jnp.where(one, c, d)
    )
    return (
        jnp.where(two, c, a), jnp.where(two, d, b), jnp.where(two, a, c), jnp.where(two, b, d)
    )


def deal_kernel(mine_ref, a_ref, b_ref, c_ref, later_ref, *out_refs):
    width = D // SECTIONS
    for k, ref in enumerate((a_ref, b_ref, c_ref)):
        rows = ref[...]
        features = [rows[:, f * width : (f + 1) * width] for f in range(SECTIONS)]
        for out_ref, piece in zip(out_refs, in_order(features, mine_ref[0]), strict=True):
            out_ref[k] = piece


def tokens_out(places, rows, later):
    width = D // SECTIONS
    features = pl.pallas_call(
        deal_kernel,
        grid=(1,),
        in_specs=[SCALAR, *[whole(HALF, D)] * 3, pl.BlockSpec(memory_space=pl.ANY)],
        out_specs=[pl.BlockSpec((3, HALF, width), lambda i: (0, 0, 0))] * SECTIONS,
        out_shape=[jax.ShapeDtypeStruct((3, HALF, width), BF)] * SECTIONS,
        compiler_params=params(),
        cost_estimate=cost(0, 4e6),
        name="deal",
    )(places.mine.reshape(1).astype(jnp.int32), *rows, later)
    got = []
    for turn in range(4):

        def route(s, d, turn=turn):
            return (2 * (s % 2) + d % 2) ^ turn, d - d % 2 + s // 2

        got.append(places.send(features[turn], route))
    return got


def undeal_kernel(section_ref, a_ref, b_ref, c_ref, d_ref, later_ref, x_ref, y_ref, z_ref):
    refs = (a_ref, b_ref, c_ref, d_ref)
    for k, out_ref in enumerate((x_ref, y_ref, z_ref)):
        pieces = in_order([ref[k] for ref in refs], section_ref[0])
        for number, piece in enumerate(pieces):
            out_ref[number * HALF : (number + 1) * HALF] = piece.astype(out_ref.dtype)


def tokens_placed(places, pieces, types, later):
    width = D // SECTIONS
    return pl.pallas_call(
        undeal_kernel,
        grid=(1,),
        in_specs=[SCALAR, *[pl.BlockSpec((3, HALF, width), lambda i: (0, 0, 0))] * 4, ANYWHERE],
        out_specs=[whole(4 * HALF, width)] * 3,
        out_shape=[shaped(4 * HALF, width, kind) for kind in types],
        compiler_params=params(),
        cost_estimate=cost(0, 4e6),
        name="undeal",
    )(places.section.reshape(1).astype(jnp.int32), *pieces, later)


def gather_start(places, mine, *earlier):
    one = places.swap_plane(mine, 0)
    two = places.swap_plane(mine, 1)
    if earlier:
        one = gate(one, *earlier)
    return one, two, places.swap_plane(one, 1)


def gather_finish(places, pieces):
    return (*pieces, *(places.swap_core(piece) for piece in pieces))


def chosen_kernel(counts, starts, which_ref, *refs):
    total = sum(counts)
    arrays, (out_ref, held_ref, sems) = refs[:total], refs[total:]

    def rows_of(number):
        return arrays[number].at[:, pl.ds(starts[number], out_ref.shape[1])]

    first = 0
    for place, count in enumerate(counts):
        for number in range(count):

            @pl.when(which_ref[place] == number)
            def _():
                pltpu.make_async_copy(
                    rows_of(first + number), held_ref.at[place], sems.at[place]
                ).start()

        first += count
    for place in range(len(counts)):
        pltpu.make_async_copy(rows_of(0), held_ref.at[place], sems.at[place]).wait()
    for block in range(out_ref.shape[0]):
        value = held_ref[0, block].astype(F32)
        for place in range(1, len(counts)):
            value = value + held_ref[place, block].astype(F32)
        out_ref[block] = value.astype(BF)


def chosen_sum(which, groups, first, rows):
    arrays = [array for group in groups for array in group]
    shape = (arrays[0].shape[0], rows, D)
    counts = tuple(len(group) for group in groups)
    starts = tuple(0 if array.shape[1] == rows else first for array in arrays)
    return pl.pallas_call(
        functools.partial(chosen_kernel, counts, starts),
        grid=(1,),
        in_specs=[SCALAR, *[ANYWHERE] * sum(counts)],
        out_specs=full(*shape),
        out_shape=jax.ShapeDtypeStruct(shape, BF),
        scratch_shapes=[
            pltpu.VMEM((len(counts), *shape), BF), pltpu.SemaphoreType.DMA((len(counts),)),
        ],
        compiler_params=params(),
        cost_estimate=cost(1e6, 5e6),
        name="chosen_sum",
    )(
        jnp.stack([w.astype(jnp.int32) for w in which]), *[in_hbm(array) for array in arrays],
    )


class Reduction:
    def __init__(self, places):
        self.places = places
        rows = places.blk + 16
        cut = rows // 32 * 16
        self.ranges = ((0, cut), (cut, rows - cut))

    def cores(self, keep, give):
        return keep, self.places.swap_core(give)

    def total(self, which, *sections):
        groups = tuple(zip(*sections, strict=True))
        return [
            self.places.swap_plane(chosen_sum((which, which), groups, *rows), 0)
            for rows in self.ranges
        ]

    def send_early(self, one, two, three):
        places = self.places
        self.sections = (one, two, three)
        low, first = jnp.logical_not(places.first_bit), places.is_first
        which = jnp.where(low, 2, jnp.where(first, 1, 0))
        self.early = self.total(which, one, two, three)

    def plane(self, zero):
        places = self.places
        one, two, three = self.sections
        low, first = jnp.logical_not(places.first_bit), places.is_first
        which = jnp.where(low, jnp.where(first, 1, 2), 0)
        late = self.total(which, zero, one, two)
        keeps, gots = zip(zero, one, two, three, strict=True)
        other = places.section ^ jnp.where(first, 2, 1)
        sums = []
        for early_part, late_part, rows in zip(self.early, late, self.ranges, strict=True):

            def held(section, arrived=(early_part, late_part), rows=rows):
                is_late = (section == 0) | ((section == 1) & first) | ((section == 2) & (~first))
                return chosen_sum((section, section, is_late), (keeps, gots, arrived), *rows)

            got = places.swap_plane(held(other), 1)
            sums.append(held(places.section) + got)
        return sums

    def shared(self, rows):
        return jnp.where(self.places.is_first, rows, self.places.swap_core(rows))

    def depth(self, blocks, beside):
        places = self.places
        place = places.dp // 2
        if blocks.shape[0] == 4:
            near, far = place % 2, place // 2
            mine = jnp.where(places.is_first, near, 2 * far)
            theirs = jnp.where(places.is_first, 1 - near, 2 - 2 * far)
            step = 2 - places.core

            def two(first):
                return jnp.stack([pick(blocks, first), pick(blocks, first + step)])

            blocks = two(mine) + places.send(two(theirs), lambda s, d: (s, d ^ (2 + 2 * (d % 2))))
            mine = jnp.where(places.is_first, far, near)
            got = places.send(
                gate(pick(blocks, 1 - mine), beside), lambda s, d: (s, d ^ (4 - 2 * (d % 2)))
            )
            return pick(blocks, mine).astype(F32) + got.astype(F32), blocks
        bit = 1
        while blocks.shape[0] > 1:
            pairs = blocks.reshape(-1, 2, *blocks.shape[1:])
            mine = (place // bit) % 2
            keep = lax.dynamic_index_in_dim(pairs, mine, 1, keepdims=False)
            give = lax.dynamic_index_in_dim(pairs, 1 - mine, 1, keepdims=False)
            blocks = keep + places.swap_dp(give, 2 * bit)
            bit *= 2
        return blocks[0].astype(F32), blocks


def on_device(
    stream_input,
    accum_input,
    section_weights,
    section_norms,
    final_norm,
    seq_lengths,
    out_cotangent,
):
    places = Places()
    section, core = places.section, places.core
    width = D // SECTIONS
    rows = D // 2

    own = section_weights[0]
    pieces = token_pieces(places, stream_input[None])
    near_pieces = gather_start(
        places, lax.dynamic_slice(own, (core * rows, 0), (rows, 4 * D)), *pieces
    )
    small = jnp.stack(
        [section_norms.reshape(2 * D), jnp.pad(final_norm.reshape(2 * width), (0, 2 * D - 2 * width))]
    )
    late_mine = jnp.concatenate(
        [
            lax.dynamic_slice(own, (core * rows, 4 * D), (rows, 2 * D)),
            jnp.pad(small, ((0, 14), (0, 0))),
        ],
        axis=0,
    )
    late_pieces = gather_start(places, gate(late_mine, *near_pieces[:2]))
    near = gather_finish(places, near_pieces)
    late = gather_finish(places, late_pieces)
    stream = jnp.concatenate(in_order([piece[0] for piece in pieces], places.mine), axis=1)
    one, two, three = (piece[rows : rows + 2] for piece in late_pieces)
    table = in_order(
        (small, jnp.where(core == 0, one, two), jnp.where(core == 0, two, one), three), section
    )
    norms = jnp.stack(table).reshape(SECTIONS, 4 * D).astype(F32)

    *segs, live = sequences(places, seq_lengths)
    qseg = segs[0]
    both = token_pieces(places, jnp.stack([accum_input, out_cotangent]))

    queries, own_kv = project(places, stream, own, near, 0)
    far_kv = places.swap_core(own_kv)
    *kept, branch_sum, turning, queries_two, own_kv_two = first_layer(
        places, stream, queries, own_kv, far_kv, segs, own, near, late, norms
    )
    far_kv_two = places.swap_core(own_kv_two)
    context, lse, middle, sum_a = second_attention(
        places, turning, queries_two, own_kv_two, far_kv_two, segs, own, near, norms
    )
    (
        result, dy_low, dy, final_grad, dz, dctx, delta, grads, keep_f, give_f, rest,
    ) = turn(
        places, middle, turning, sum_a, context, own, near, late, norms, branch_sum, both, live
    )

    reduction = Reduction(places)
    zero = jnp.zeros((HALF, D), F32)

    def scores(queries, own_kv, far_kv, dctx, lse, delta):
        dq, dkv_far = scores_back(queries, far_kv, dctx, qseg, segs[2], lse, delta, zero, BF)
        from_far = places.swap_core(dkv_far)
        dq, dkv = scores_back(queries, own_kv, dctx, qseg, segs[1], lse, delta, dq, BF)
        return dq, dkv, from_far

    third = reduction.cores(keep_f, give_f)
    dq, dkv, from_far = scores(queries_two, own_kv_two, far_kv_two, dctx, lse, delta)
    dz, dctx, delta, grads_first, keep_p, give_p, keep_f, give_f, rest = between(
        places, turning, dq, dkv, from_far, dz, dy, grads, final_grad, rest, kept, own, near,
        late, norms,
    )
    reduction.send_early(reduction.cores(keep_f, give_f), reduction.cores(keep_p, give_p), third)
    dq, dkv, from_far = scores(queries, own_kv, far_kv, dctx, kept[1], delta)
    upstream, keep, give = project_back(
        places, stream, dq, dkv, from_far, dz, own, near, 0, grads_first, final_grad, rest
    )
    blocks = reduction.plane(reduction.cores(keep, give))
    leaving = tokens_out(places, (upstream, result, dy_low), blocks[0])
    reduced, early = zip(*(reduction.depth(part, leaving[0]) for part in blocks), strict=True)
    reduced = jnp.concatenate(reduced, axis=0)
    shared = reduction.shared(reduced[places.blk :])
    stream_out, result_out, accum_out = tokens_placed(places, leaving, (F32, BF, F32), early[1])
    slab = reduced[: places.blk].T
    cut = D // places.ndp
    norm_out = lax.dynamic_slice(reduced, (places.blk, places.dp * cut), (2, cut))
    final_out = lax.dynamic_slice(shared, (2, section * width), (2, width))

    return (
        result_out,
        stream_out,
        accum_out,
        slab[None],
        norm_out[None],
        final_out,
    )


def solution(mesh):
    placed = (
        P("dp", "section"),
        P("dp", "section"),
        P("section", None, None),
        P("section", None, None),
        P(None, "section"),
        P("dp", None),
        P("dp", "section"),
    )
    return jax.shard_map(
        on_device,
        mesh=mesh,
        in_specs=placed,
        out_specs=(
            P("dp", "section"),
            P("dp", "section"),
            P("dp", "section"),
            P("section", None, "dp"),
            P("section", None, "dp"),
            P(None, "section"),
        ),
        check_vma=False,
    )
```

```python
import functools
import math

import jax
import jax.numpy as jnp
from jax import lax
from jax.experimental import pallas as pl
from jax.experimental.pallas import tpu as pltpu
from jax.sharding import PartitionSpec as P

D = 512
HEADS = 8
HEAD = 64
PACK = 1024
HALF = PACK // 2
PAIRS = HEADS // 2
LANES = 2 * HEAD
SECTIONS = 4
FAR = 1e30
SCALE = HEAD ** (-0.5)
BF = jnp.bfloat16
F32 = jnp.float32
NT = (((1,), (1,)), ((), ()))
TN = (((0,), (0,)), ((), ()))


def mm(left, right):
    return jnp.dot(left, right, preferred_element_type=F32)


def mm_nt(left, right):
    return lax.dot_general(left, right, NT, preferred_element_type=F32)


def mm_tn(left, right):
    return lax.dot_general(left, right, TN, preferred_element_type=F32)


def params(megabytes=16):
    return pltpu.CompilerParams(
        dimension_semantics=("arbitrary",), vmem_limit_bytes=megabytes * 1024 * 1024
    )


def shaped(rows, cols, dtype):
    return jax.ShapeDtypeStruct((rows, cols), dtype)


def in_hbm(array):
    return pltpu.with_memory_space_constraint(array, pltpu.HBM)


def whole(rows, cols):
    return pl.BlockSpec((rows, cols), lambda i: (0, 0))


SCALAR = pl.BlockSpec(memory_space=pltpu.SMEM)


def cost(flops, moved, transcendentals=0):
    return pl.CostEstimate(
        flops=int(flops), bytes_accessed=int(moved), transcendentals=int(transcendentals)
    )


def gain_of(table_ref, layer):
    return table_ref[layer : layer + 1, :D]


def shift_of(table_ref, layer):
    return table_ref[layer : layer + 1, D : 2 * D]


def norm_parts(summed):
    average = jnp.mean(summed, axis=-1, keepdims=True)
    centered = summed - average
    spread = jnp.mean(centered * centered, axis=-1, keepdims=True)
    inverse = lax.rsqrt(spread + 1e-05)
    return centered * inverse, inverse


def norm_forward(summed, table_ref, layer):
    normal, _ = norm_parts(summed)
    return normal * gain_of(table_ref, layer) + shift_of(table_ref, layer)


def norm_back(summed, gain, upstream):
    normal, inverse = norm_parts(summed)
    scaled = upstream * gain
    mean_one = jnp.mean(scaled, axis=-1, keepdims=True)
    mean_two = jnp.mean(scaled * normal, axis=-1, keepdims=True)
    grad = (scaled - mean_one - normal * mean_two) * inverse
    gain_grad = jnp.sum(upstream * normal, axis=0, keepdims=True)
    shift_grad = jnp.sum(upstream, axis=0, keepdims=True)
    return grad, gain_grad, shift_grad


def head_mask(which):
    lane = lax.broadcasted_iota(jnp.int32, (1, LANES), 1)
    return (lane // HEAD) == which


def three_way(column):
    high = column.astype(BF)
    rest = column - high.astype(F32)
    middle = rest.astype(BF)
    low = (rest - middle.astype(F32)).astype(BF)
    return high, middle, low


GROUP = 6


def fetch(where_ref, layer, own_ref, piece_refs, own_first, first, width, target, sem):
    section, core, turned = where_ref[0], where_ref[1], where_ref[3]
    half = D // 2
    step = section ^ layer
    mine_rows = pl.ds(pl.multiple_of(core * half, half), half)
    far_rows = pl.ds(pl.multiple_of((1 - core) * half, half), half)

    @pl.when(step == 0)
    def _():
        pltpu.make_async_copy(own_ref.at[:, pl.ds(own_first, width)], target, sem).start()

    for number, (partner, far_number) in enumerate(((1 + turned, 1), (2 - turned, 0), (3, 2))):

        @pl.when(step == partner)
        def _():
            part = (pl.ds(0, half), pl.ds(first, width))
            mine, far = piece_refs[number].at[part], piece_refs[3 + far_number].at[part]
            pltpu.make_async_copy(mine, target.at[mine_rows], sem).start()
            pltpu.make_async_copy(far, target.at[far_rows], sem).start()


def arrived(own_ref, width, target, sem):
    pltpu.make_async_copy(own_ref.at[:, pl.ds(0, width)], target, sem).wait()


def weight_specs(groups):
    return [pl.BlockSpec(memory_space=pl.ANY)] * (1 + GROUP * groups)


def column_of(pair):
    return pl.ds(pl.multiple_of(pair * LANES, LANES), LANES)


def fetch_projection(layer, where_ref, own_ref, near, weight_ref, sems):
    for part in range(3):
        fetch(
            where_ref, layer, own_ref, near, part * D, part * D, D, weight_ref.at[part],
            sems.at[part],
        )


def fetch_outward(layer, where_ref, own_ref, near, weight_ref, sem):
    fetch(where_ref, layer, own_ref, near, 3 * D, 3 * D, D, weight_ref, sem)


def fetch_feed(layer, where_ref, own_ref, near, late, weight_ref, sems):
    for chunk in range(4):
        turn = chunk % 2
        if chunk < 2:
            inner = (layer - 1, late, (4 + turn) * D, turn * D)
            outer = (layer, near, (2 + turn) * D, (2 + turn) * D)
        else:
            inner = (layer, near, turn * D, turn * D)
            outer = (layer, late, (4 + turn) * D, turn * D)
        for number, (whose, pieces, own_first, first) in enumerate((inner, outer)):
            fetch(
                where_ref, whose, own_ref, pieces, own_first, first, D,
                weight_ref.at[chunk, number], sems.at[chunk, number],
            )


PROJECTION = [pltpu.VMEM((3, D, D), BF), pltpu.SemaphoreType.DMA((3,))]
OUTWARD = [pltpu.VMEM((D, D), BF), pltpu.SemaphoreType.DMA]
FEED = [pltpu.VMEM((4, 2, D, D), BF), pltpu.SemaphoreType.DMA((4, 2))]


def put_projection(own_ref, x, q_ref, kv_ref, weight_ref, sems):
    def times(part):
        arrived(own_ref, D, weight_ref.at[part], sems.at[part])
        return mm(x, weight_ref[part]).astype(BF)

    q_ref[...] = times(0)
    keys, values = times(1), times(2)
    for pair in range(PAIRS):
        lanes = slice(pair * LANES, (pair + 1) * LANES)
        kv_ref[pair, :, :LANES] = keys[:, lanes]
        kv_ref[pair, :, LANES:] = values[:, lanes]


def put_attention(q_ref, own_ref, far_ref, qs_ref, kso_ref, ksx_ref, ctx_ref, lse_ref):
    none = jnp.zeros((), BF)
    lane = lax.broadcasted_iota(jnp.int32, (1, LANES), 1)
    ones = jnp.ones((HALF, LANES), BF)
    lse_ref[...] = jnp.zeros((HALF, LANES), F32)

    @pl.loop(0, PAIRS)
    def _(pair):
        q = q_ref[:, column_of(pair)] * jnp.asarray(SCALE, BF)
        keys_own = jnp.concatenate([own_ref[pair, :, :LANES], kso_ref[...]], axis=1)
        keys_other = jnp.concatenate([far_ref[pair, :, :LANES], ksx_ref[...]], axis=1)
        values_own, values_other = own_ref[pair, :, LANES:], far_ref[pair, :, LANES:]
        context = jnp.zeros((HALF, LANES), F32)
        logs = lse_ref[...]
        for which in range(2):
            mask = head_mask(which)
            query = jnp.concatenate([jnp.where(mask, q, none), qs_ref[...]], axis=1)
            score_own = mm_nt(query, keys_own)
            score_other = mm_nt(query, keys_other)
            peak = jnp.maximum(
                jnp.max(score_own, axis=1, keepdims=True),
                jnp.max(score_other, axis=1, keepdims=True),
            )
            own = jnp.exp(score_own - peak).astype(BF)
            other = jnp.exp(score_other - peak).astype(BF)
            total = mm(
                own, jnp.concatenate([jnp.where(mask, values_own, none), ones], axis=1)
            ) + mm(other, jnp.concatenate([jnp.where(mask, values_other, none), ones], axis=1))
            row_total = total[:, LANES:]
            context = context + total[:, :LANES] / row_total
            logs = jnp.where(lane == 2 * pair + which, peak + jnp.log(row_total), logs)
        lse_ref[...] = logs
        ctx_ref[:, column_of(pair)] = context.astype(BF)


def gelu_parts(v):
    root = 0.7978845608028654
    squared = v * v
    inner = root * (v + 0.044715 * v * squared)
    t = jnp.tanh(inner)
    hidden = 0.5 * v * (1.0 + t)
    slope = 0.5 * (1.0 + t) + 0.5 * v * (1.0 - t * t) * (root * (1.0 + 3 * 0.044715 * squared))
    return hidden, slope


def feed_weight(own_ref, weight_ref, sems, chunk, number):
    arrived(own_ref, D, weight_ref.at[chunk, number], sems.at[chunk, number])
    return weight_ref[chunk, number]


def split_rows(core, blk, row, value, keep_ref, give_ref):
    step = math.gcd(D, blk)
    for k in range(value.shape[0] // step):
        part = value[k * step : (k + 1) * step]
        first = row + k * step
        block, offset = first // blk, first % blk

        @pl.when(block % 2 == core)
        def _():
            keep_ref[block // 2, offset : offset + step, :] = part

        @pl.when(block % 2 != core)
        def _():
            give_ref[block // 2, offset : offset + step, :] = part


def side_rows(grads, final_grads, keep_ref, give_ref):
    extra = jnp.concatenate([grads, final_grads, jnp.zeros((12, D), F32)], axis=0).astype(BF)
    blk = keep_ref.shape[1] - 16
    for block in range(keep_ref.shape[0]):
        keep_ref[block, blk:, :] = extra
        give_ref[block, blk:, :] = extra


def split_shapes(count, blk):
    return [full(count, blk + 16, D)] * 2, [pltpu.HBM((count, blk + 16, D), BF)] * 2


def put_outward_back(
    summed, upstream, dy, context, gain, weight_of, dctx_ref, delta_ref, grad_ref, rest_ref
):
    grad, gain_grad, shift_grad = norm_back(summed, gain, upstream)
    grad_ref[...] = jnp.concatenate([gain_grad, shift_grad], axis=0)
    df = (grad + dy).astype(BF)
    rest_ref[:D] = mm_tn(df, context).astype(BF)
    context_grad = mm_nt(df, weight_of()).astype(BF)
    dctx_ref[...] = context_grad
    product = context.astype(F32) * context_grad.astype(F32)
    lane = lax.broadcasted_iota(jnp.int32, (1, LANES), 1)
    delta = jnp.zeros((HALF, LANES), F32)
    for head in range(HEADS):
        part = product[:, (head // 2) * LANES : (head // 2 + 1) * LANES]
        inner = jnp.sum(jnp.where(head_mask(head % 2), part, 0.0), axis=1, keepdims=True)
        delta = jnp.where(lane == head, inner, delta)
    delta_ref[...] = delta
    return grad


def put_feed_back(
    core, x, hidden_of, df, grad, weight_of, rest_ref, keep_ref, give_ref
):
    blk = keep_ref.shape[1] - 16
    total = grad
    for chunk in range(4):
        inner, outer = weight_of(chunk, 0), weight_of(chunk, 1)
        hidden, slope = hidden_of(chunk, inner)
        split_rows(core, blk, (2 + chunk) * D, mm_tn(hidden, df).astype(BF), keep_ref, give_ref)
        preact_grad = (mm(df, outer) * slope).astype(BF)
        inner_grad = mm_tn(preact_grad, x).astype(BF)
        if chunk < 2:
            rest_ref[(1 + chunk) * D : (2 + chunk) * D] = inner_grad
        else:
            split_rows(core, blk, (chunk - 2) * D, inner_grad, keep_ref, give_ref)
        total = total + mm_nt(preact_grad, inner)
    return total


def put_project_back(
    core, x, dq_ref, dkv_ref, far_ref, dz, grads, final_grads, rest_ref, weight_of, keep_ref,
    give_ref,
):
    blk = keep_ref.shape[1] - 16
    side_rows(grads, final_grads, keep_ref, give_ref)
    split_rows(core, blk, 3 * D, rest_ref[...], keep_ref, give_ref)
    parts = [(dkv_ref[k].astype(F32) + far_ref[k].astype(F32)).astype(BF) for k in range(PAIRS)]
    dk = jnp.concatenate([part[:, :LANES] for part in parts], axis=1)
    dv = jnp.concatenate([part[:, LANES:] for part in parts], axis=1)
    total = dz
    for place, grad in enumerate((dq_ref[...].astype(BF), dk, dv)):
        split_rows(core, blk, place * D, mm_tn(grad, x).astype(BF), keep_ref, give_ref)
        total = total + mm_nt(grad, weight_of(place))
    return total


def full(*shape):
    return pl.BlockSpec(shape, lambda i: (0,) * len(shape), pipeline_mode=pl.Buffered(1))


KV = (PAIRS, HALF, 2 * LANES)
TABLE = (SECTIONS, 4 * D)


def project_kernel(layer, where_ref, x_ref, own_ref, *refs):
    near, (q_ref, kv_ref, weight_ref, sems) = refs[:GROUP], refs[GROUP:]
    fetch_projection(layer, where_ref, own_ref, near, weight_ref, sems)
    put_projection(own_ref, x_ref[...], q_ref, kv_ref, weight_ref, sems)


def project(places, stream, own, near, layer):
    return pl.pallas_call(
        functools.partial(project_kernel, layer),
        grid=(1,),
        in_specs=[SCALAR, full(HALF, D), *weight_specs(1)],
        out_specs=[full(HALF, D), full(*KV)],
        out_shape=[shaped(HALF, D, BF), jax.ShapeDtypeStruct(KV, BF)],
        scratch_shapes=PROJECTION,
        compiler_params=params(),
        cost_estimate=cost(2 * HALF * D * 3 * D, 4e6),
        name="project",
    )(places.where, stream, *map(in_hbm, (own, *near)))


def layer_kernel(
    layer, where_ref, q_ref, own_kv_ref, far_kv_ref, qs_ref, kso_ref, ksx_ref, x_ref, norm_ref,
    own_ref, *refs,
):
    near, late, refs = refs[:GROUP], refs[GROUP : 2 * GROUP], refs[2 * GROUP :]
    (
        ctx_ref, lse_ref, middle_ref, sum_a_ref, sum_f_ref, branch_ref, next_ref, q_next_ref,
        kv_next_ref, outward_ref, outward_sem, feed_ref, feed_sems, project_ref, project_sems,
    ) = refs
    fetch_outward(layer, where_ref, own_ref, near, outward_ref, outward_sem)
    fetch_feed(layer + 1, where_ref, own_ref, near, late, feed_ref, feed_sems)
    fetch_projection(layer + 2, where_ref, own_ref, near, project_ref, project_sems)
    put_attention(
        q_ref, own_kv_ref, far_kv_ref, qs_ref, kso_ref, ksx_ref, ctx_ref, lse_ref
    )
    arrived(own_ref, D, outward_ref, outward_sem)
    branch = mm(ctx_ref[...], outward_ref[...])
    summed = x_ref[...].astype(F32) + branch
    sum_a_ref[...] = summed
    middle = norm_forward(summed, norm_ref, layer).astype(BF)
    middle_ref[...] = middle
    total = jnp.zeros((HALF, D), F32)
    for chunk in range(4):
        inner = feed_weight(own_ref, feed_ref, feed_sems, chunk, 0)
        hidden = gelu_parts(mm(middle, inner))[0].astype(BF)
        total = total + mm_nt(hidden, feed_weight(own_ref, feed_ref, feed_sems, chunk, 1))
    summed = middle.astype(F32) + total
    sum_f_ref[...] = summed
    branch_ref[...] = branch + total
    following = norm_forward(summed, norm_ref, layer + 1).astype(BF)
    next_ref[...] = following
    put_projection(own_ref, following, q_next_ref, kv_next_ref, project_ref, project_sems)


def first_layer(places, stream, queries, own_kv, far_kv, segs, own, near, late, norms):
    return pl.pallas_call(
        functools.partial(layer_kernel, 0),
        grid=(1,),
        in_specs=[
            SCALAR, full(HALF, D), full(*KV), full(*KV), *[full(HALF, LANES)] * 3, full(HALF, D),
            full(*TABLE), *weight_specs(2),
        ],
        out_specs=[
            full(HALF, D), full(HALF, LANES), *[full(HALF, D)] * 6, full(*KV),
        ],
        out_shape=[
            shaped(HALF, D, BF), shaped(HALF, LANES, F32), shaped(HALF, D, BF),
            shaped(HALF, D, F32), shaped(HALF, D, F32), shaped(HALF, D, F32), shaped(HALF, D, BF),
            shaped(HALF, D, BF), jax.ShapeDtypeStruct(KV, BF),
        ],
        scratch_shapes=[*OUTWARD, *FEED, *PROJECTION],
        compiler_params=params(30),
        cost_estimate=cost(14e9, 20e6, 4e6),
        name="first_layer",
    )(
        places.where, queries, own_kv, far_kv, *segs, stream, norms, *map(in_hbm, (own, *near, *late))
    )


def attend_kernel(
    layer, where_ref, q_ref, own_kv_ref, far_kv_ref, qs_ref, kso_ref, ksx_ref, x_ref, norm_ref,
    own_ref, *refs,
):
    near, refs = refs[:GROUP], refs[GROUP:]
    ctx_ref, lse_ref, middle_ref, sum_ref, outward_ref, outward_sem = refs
    fetch_outward(layer, where_ref, own_ref, near, outward_ref, outward_sem)
    put_attention(
        q_ref, own_kv_ref, far_kv_ref, qs_ref, kso_ref, ksx_ref, ctx_ref, lse_ref
    )
    arrived(own_ref, D, outward_ref, outward_sem)
    summed = x_ref[...].astype(F32) + mm(ctx_ref[...], outward_ref[...])
    sum_ref[...] = summed
    middle_ref[...] = norm_forward(summed, norm_ref, layer).astype(BF)


def second_attention(places, stream, queries, own_kv, far_kv, segs, own, near, norms):
    return pl.pallas_call(
        functools.partial(attend_kernel, 2),
        grid=(1,),
        in_specs=[
            SCALAR, full(HALF, D), full(*KV), full(*KV), *[full(HALF, LANES)] * 3, full(HALF, D),
            full(*TABLE), *weight_specs(1),
        ],
        out_specs=[full(HALF, D), full(HALF, LANES), full(HALF, D), full(HALF, D)],
        out_shape=[
            shaped(HALF, D, BF), shaped(HALF, LANES, F32), shaped(HALF, D, BF),
            shaped(HALF, D, F32),
        ],
        scratch_shapes=OUTWARD,
        compiler_params=params(),
        cost_estimate=cost(9e9, 10e6, 4e6),
        name="second_attention",
    )(places.where, queries, own_kv, far_kv, *segs, stream, norms, *map(in_hbm, (own, *near)))


def turn_kernel(
    layer, where_ref, middle_ref, x_ref, sum_ref, ctx_ref, norm_ref, branch_ref,
    a_ref, b_ref, c_ref, d_ref, live_ref, own_ref, *refs,
):
    near, late, refs = refs[:GROUP], refs[GROUP : 2 * GROUP], refs[2 * GROUP :]
    (
        result_ref, low_ref, dy_ref, final_ref, dz_ref, dctx_ref, delta_ref, grad_ref,
        feed_keep, feed_give, rest_ref,
        hidden_ref, slope_ref, outward_ref, outward_sem, feed_ref, feed_sems,
    ) = refs
    core, mine = where_ref[1], where_ref[2]
    fetch_feed(layer + 1, where_ref, own_ref, near, late, feed_ref, feed_sems)
    fetch_outward(layer, where_ref, own_ref, near, outward_ref, outward_sem)
    middle, sum_a = middle_ref[...], sum_ref[...]
    branch = sum_a - x_ref[...].astype(F32)
    total = jnp.zeros((HALF, D), F32)
    for chunk in range(4):
        inner = feed_weight(own_ref, feed_ref, feed_sems, chunk, 0)
        hidden, slope = gelu_parts(mm(middle, inner))
        hidden = hidden.astype(BF)
        hidden_ref[chunk] = hidden
        slope_ref[chunk] = slope
        total = total + mm_nt(hidden, feed_weight(own_ref, feed_ref, feed_sems, chunk, 1))
    sum_f = middle.astype(F32) + total
    last = norm_forward(sum_f, norm_ref, layer + 1)

    pieces = in_order([ref[...] for ref in (a_ref, b_ref, c_ref, d_ref)], mine)
    accum, cot = (jnp.concatenate([piece[k] for piece in pieces], axis=1) for k in range(2))
    summed = accum.astype(F32) + (branch_ref[...] + (branch + total))
    normal, _ = norm_parts(summed)
    width = D // SECTIONS
    gain, shift = (
        jnp.concatenate(
            [
                norm_ref[k : k + 1, 2 * D + part * width : 2 * D + (part + 1) * width]
                for k in range(SECTIONS)
            ],
            axis=1,
        )
        for part in range(2)
    )
    result_ref[...] = (last + normal * gain + shift).astype(BF)
    cot = cot.astype(F32) * live_ref[:, 0:1]
    dy, gain_grad, shift_grad = norm_back(summed, gain, cot)
    dy_ref[...] = dy
    low_ref[...] = dy.astype(BF)
    final_grads = jnp.concatenate([gain_grad, shift_grad], axis=0)
    final_ref[...] = final_grads

    grad, gain_grad, shift_grad = norm_back(sum_f, gain_of(norm_ref, layer + 1), cot)
    side_rows(
        jnp.concatenate([gain_grad, shift_grad], axis=0), final_grads, feed_keep, feed_give
    )
    upstream = put_feed_back(
        core, middle, lambda chunk, inner: (hidden_ref[chunk], slope_ref[chunk]),
        (grad + dy).astype(BF), grad, lambda chunk, number: feed_ref[chunk, number],
        rest_ref, feed_keep, feed_give,
    )
    arrived(own_ref, D, outward_ref, outward_sem)
    dz_ref[...] = put_outward_back(
        sum_a, upstream.astype(BF).astype(F32), dy, ctx_ref[...], gain_of(norm_ref, layer),
        lambda: outward_ref[...], dctx_ref, delta_ref, grad_ref, rest_ref,
    )


def turn(places, middle, stream, sum_a, context, own, near, late, norms, branch_sum, pieces, live):
    specs, shapes = split_shapes(places.ndp // 2, places.blk)
    return pl.pallas_call(
        functools.partial(turn_kernel, 2),
        grid=(1,),
        in_specs=[
            SCALAR, *[full(HALF, D)] * 4, full(*TABLE), full(HALF, D),
            *[full(2, HALF, D // SECTIONS)] * 4, full(HALF, LANES), *weight_specs(2),
        ],
        out_specs=[
            *[full(HALF, D)] * 3, full(2, D), full(HALF, D), full(HALF, D),
            full(HALF, LANES), full(2, D), *specs, full(3 * D, D),
        ],
        out_shape=[
            shaped(HALF, D, BF), shaped(HALF, D, BF),
            shaped(HALF, D, F32), shaped(2, D, F32), shaped(HALF, D, F32), shaped(HALF, D, BF),
            shaped(HALF, LANES, F32), shaped(2, D, F32), *shapes, shaped(3 * D, D, BF),
        ],
        scratch_shapes=[
            pltpu.VMEM((4, HALF, D), BF), pltpu.VMEM((4, HALF, D), F32), *OUTWARD, *FEED,
        ],
        compiler_params=params(40),
        cost_estimate=cost(16e9, 30e6, 2e6),
        name="turn",
    )(
        places.where, middle, stream, sum_a, context, norms, branch_sum, *pieces, live, *map(in_hbm, (own, *near, *late)),
    )


def column():
    return pl.BlockSpec((HALF, LANES), lambda i: (0, i))


def pair_block():
    return pl.BlockSpec((1, HALF, 2 * LANES), lambda i: (i, 0, 0))


def scores_back_kernel(
    q_ref, kv_ref, dctx_ref, qs_ref, ks_ref, lse_ref, delta_ref, before_ref, dq_ref, dkv_ref
):
    pair = pl.program_id(0)
    none = jnp.zeros((), BF)
    lane = lax.broadcasted_iota(jnp.int32, (1, LANES), 1)
    q = q_ref[...] * jnp.asarray(SCALE, BF)
    k = kv_ref[0, :, :LANES]
    k_scaled = k * jnp.asarray(SCALE, BF)
    dctx = dctx_ref[...]
    extra = jnp.where((lane >= LANES - 3), jnp.ones((), BF), none)
    keys = jnp.concatenate([k, ks_ref[...] + extra], axis=1)
    values = jnp.concatenate(
        [kv_ref[0, :, LANES:], jnp.broadcast_to(extra, (HALF, LANES))], axis=1
    )
    dq = before_ref[...]
    dk = jnp.zeros((HALF, LANES), F32)
    dv = jnp.zeros((HALF, LANES), F32)
    for which in range(2):
        mask = head_mask(which)
        here = lane == 2 * pair + which

        def lanes_of(table, base):
            column = -jnp.sum(jnp.where(here, table, 0.0), axis=1, keepdims=True)
            high, middle, low = three_way(column)
            base = jnp.where(lane == LANES - 3, high, base)
            base = jnp.where(lane == LANES - 2, middle, base)
            return jnp.where(lane == LANES - 1, low, base)

        query_part = jnp.where(mask, q, none)
        dctx_part = jnp.where(mask, dctx, none)
        query = jnp.concatenate([query_part, lanes_of(lse_ref[...], qs_ref[...])], axis=1)
        dcontext = jnp.concatenate(
            [dctx_part, lanes_of(delta_ref[...], jnp.zeros((HALF, LANES), BF))], axis=1
        )
        probability = jnp.exp(mm_nt(keys, query))
        score_grad = (probability * mm_nt(values, dcontext)).astype(BF)
        dv = dv + mm(probability.astype(BF), dctx_part)
        dk = dk + mm(score_grad, query_part)
        dq = dq + mm_tn(score_grad, jnp.where(mask, k_scaled, none))
    dq_ref[...] = dq
    dkv_ref[0, :, :LANES] = dk.astype(dkv_ref.dtype)
    dkv_ref[0, :, LANES:] = dv.astype(dkv_ref.dtype)


def scores_back(queries, kv, dctx, qseg, kseg, lse, delta, before, out_type):
    return pl.pallas_call(
        scores_back_kernel,
        grid=(PAIRS,),
        in_specs=[
            column(), pair_block(), column(),
            whole(HALF, LANES), whole(HALF, LANES), whole(HALF, LANES), whole(HALF, LANES),
            column(),
        ],
        out_specs=[column(), pair_block()],
        out_shape=[
            shaped(HALF, D, F32), jax.ShapeDtypeStruct((PAIRS, HALF, 2 * LANES), out_type),
        ],
        compiler_params=params(),
        cost_estimate=cost(8e9, 8e6, 2e6),
        name="scores_back",
    )(queries, kv, dctx, qseg, kseg, lse, delta, before)


def middle_kernel(
    layer, where_ref, x_ref, dq_ref, dkv_ref, far_ref, dz_ref, dy_ref, grad_ref, final_ref,
    before_ref, middle_ref, sum_f_ref, sum_a_ref, ctx_ref, norm_ref, own_ref, *refs,
):
    near, late, refs = refs[:GROUP], refs[GROUP : 2 * GROUP], refs[2 * GROUP :]
    (
        dz_out, dctx_ref, delta_ref, grad_out, project_keep, project_give, feed_keep, feed_give,
        rest_ref,
        project_ref, project_sems, feed_ref, feed_sems, outward_ref, outward_sem,
    ) = refs
    core = where_ref[1]
    fetch_projection(layer, where_ref, own_ref, near, project_ref, project_sems)
    fetch_feed(layer - 1, where_ref, own_ref, near, late, feed_ref, feed_sems)
    fetch_outward(layer - 2, where_ref, own_ref, near, outward_ref, outward_sem)
    final_grads = final_ref[...]

    def project_weight(place):
        arrived(own_ref, D, project_ref.at[place], project_sems.at[place])
        return project_ref[place]

    def outward_weight():
        arrived(own_ref, D, outward_ref, outward_sem)
        return outward_ref[...]

    upstream = put_project_back(
        core, x_ref[...], dq_ref, dkv_ref, far_ref, dz_ref[...], grad_ref[...], final_grads,
        before_ref, project_weight, project_keep, project_give,
    ).astype(BF).astype(F32)
    dy = dy_ref[...]
    grad, gain_grad, shift_grad = norm_back(
        sum_f_ref[...], gain_of(norm_ref, layer - 1), upstream
    )
    side_rows(
        jnp.concatenate([gain_grad, shift_grad], axis=0), final_grads, feed_keep, feed_give
    )
    middle = middle_ref[...]

    def hidden_of(chunk, inner):
        hidden, slope = gelu_parts(mm(middle, inner))
        return hidden.astype(BF), slope

    upstream = put_feed_back(
        core, middle, hidden_of, (grad + dy).astype(BF), grad,
        functools.partial(feed_weight, own_ref, feed_ref, feed_sems), rest_ref, feed_keep, feed_give,
    ).astype(BF).astype(F32)
    dz_out[...] = put_outward_back(
        sum_a_ref[...], upstream, dy, ctx_ref[...], gain_of(norm_ref, layer - 2),
        outward_weight, dctx_ref, delta_ref, grad_out, rest_ref,
    )


def between(
    places, stream, dq, dkv, far, dz, dy, grads, final_grads, rest, kept, own, near, late, norms
):
    context, _, middle, sum_a, sum_f = kept
    specs, shapes = split_shapes(places.ndp // 2, places.blk)
    return pl.pallas_call(
        functools.partial(middle_kernel, 2),
        grid=(1,),
        in_specs=[
            SCALAR, full(HALF, D), full(HALF, D), full(*KV), full(*KV), full(HALF, D),
            full(HALF, D), full(2, D), full(2, D), full(3 * D, D), *[full(HALF, D)] * 4,
            full(*TABLE), *weight_specs(2),
        ],
        out_specs=[
            full(HALF, D), full(HALF, D), full(HALF, LANES), full(2, D), *specs, *specs,
            full(3 * D, D),
        ],
        out_shape=[
            shaped(HALF, D, F32), shaped(HALF, D, BF), shaped(HALF, LANES, F32),
            shaped(2, D, F32), *shapes, *shapes, shaped(3 * D, D, BF),
        ],
        scratch_shapes=[*PROJECTION, *FEED, *OUTWARD],
        compiler_params=params(44),
        cost_estimate=cost(20e9, 30e6, 2e6),
        name="between",
    )(
        places.where, stream, dq, dkv, far, dz, dy, grads, final_grads, rest, middle, sum_f,
        sum_a, context, norms, *map(in_hbm, (own, *near, *late)),
    )


def project_back_kernel(
    layer, where_ref, x_ref, dq_ref, dkv_ref, far_ref, dz_ref, grad_ref, final_ref, rest_ref,
    own_ref, *refs,
):
    near, (dx_ref, keep_ref, give_ref, weight_ref, sems) = refs[:GROUP], refs[GROUP:]
    fetch_projection(layer, where_ref, own_ref, near, weight_ref, sems)

    def weight_of(place):
        arrived(own_ref, D, weight_ref.at[place], sems.at[place])
        return weight_ref[place]

    dx_ref[...] = put_project_back(
        where_ref[1], x_ref[...], dq_ref, dkv_ref, far_ref, dz_ref[...], grad_ref[...],
        final_ref[...], rest_ref, weight_of, keep_ref, give_ref,
    ).astype(BF)


def project_back(places, stream, dq, dkv, far, dz, own, near, layer, grads, final_grads, rest):
    specs, shapes = split_shapes(places.ndp // 2, places.blk)
    return pl.pallas_call(
        functools.partial(project_back_kernel, layer),
        grid=(1,),
        in_specs=[
            SCALAR, full(HALF, D), full(HALF, D), full(*KV), full(*KV), full(HALF, D),
            full(2, D), full(2, D), full(3 * D, D), *weight_specs(1),
        ],
        out_specs=[full(HALF, D), *specs],
        out_shape=[shaped(HALF, D, BF), *shapes],
        scratch_shapes=PROJECTION,
        compiler_params=params(20),
        cost_estimate=cost(4 * HALF * D * 3 * D, 10e6),
        name="project_back",
    )(places.where, stream, dq, dkv, far, dz, grads, final_grads, rest, *map(in_hbm, (own, *near)))


class Places:
    def __init__(self):
        self.ndp = lax.axis_size("dp")
        self.section = lax.axis_index("section")
        self.dp = lax.axis_index("dp")
        self.core = self.dp % 2
        self.blk = 6 * D // self.ndp
        self.mine = 2 * (self.section % 2) + self.core
        self.turned = (self.dp + self.dp // 2) % 2
        self.where = jnp.stack([self.section, self.core, self.mine, self.turned]).astype(jnp.int32)
        bits = (self.section % 2 == 1, self.section // 2 == 1)
        self.is_first = self.core == 0
        self.first_bit = jnp.where(self.is_first, bits[0], bits[1])
        self.second_bit = jnp.where(self.is_first, bits[1], bits[0])

    def swap_dp(self, block, step):
        return lax.ppermute(block, "dp", [(i, i ^ step) for i in range(self.ndp)])

    def swap_core(self, block):
        return self.swap_dp(block, 1)

    def swap_plane(self, block, turn):
        return self.send(block, lambda s, d: (s ^ (1 + (d + turn) % 2), d))

    def swap_turned(self, block, turn):
        return self.send(block, lambda s, d: (s ^ (1 + (d + d // 2 + turn) % 2), d))

    def send(self, block, route):
        pairs = []
        for s in range(SECTIONS):
            for d in range(self.ndp):
                to = route(s, d)
                pairs.append((s * self.ndp + d, to[0] * self.ndp + to[1]))
        return lax.ppermute(block, ("section", "dp"), pairs)


def pick(stack, index):
    return lax.dynamic_index_in_dim(stack, index, 0, keepdims=False)


ANYWHERE = pl.BlockSpec(memory_space=pl.ANY)


def sequence_kernel(where_ref, own_ref, far_ref, qseg_ref, own_seg_ref, far_seg_ref, live_ref):
    section, core = where_ref[0], where_ref[1]
    here = core == section // 2
    row = section % 2
    lane = lax.broadcasted_iota(jnp.int32, (HALF, LANES), 1)
    spot = lax.broadcasted_iota(jnp.int32, (HALF, LANES), 0)
    own = jnp.zeros((HALF, LANES), jnp.int32)
    far = jnp.zeros((HALF, LANES), jnp.int32)
    ending = jnp.int32(0)
    for k in range(own_ref.shape[1]):
        ending = ending + jnp.where(here, own_ref[row, k], far_ref[row, k])
        own = own + (spot + core * HALF >= ending).astype(jnp.int32)
        far = far + (spot + (1 - core) * HALF >= ending).astype(jnp.int32)
    own_seg_ref[...] = jnp.where(own == lane, 1.0, 0.0).astype(BF)
    far_seg_ref[...] = jnp.where(far == lane, 1.0, 0.0).astype(BF)
    qseg_ref[...] = jnp.where((own != lane) & (lane < 32), -FAR, 0.0).astype(BF)
    live_ref[...] = jnp.where(spot + core * HALF < ending, 1.0, 0.0)


def sequences(places, lengths):
    return pl.pallas_call(
        sequence_kernel,
        grid=(1,),
        in_specs=[SCALAR] * 3,
        out_specs=[whole(HALF, LANES)] * 4,
        out_shape=[shaped(HALF, LANES, BF)] * 3 + [shaped(HALF, LANES, F32)],
        compiler_params=params(),
        cost_estimate=cost(1e6, 1e6),
        name="sequences",
    )(places.where, lengths, places.swap_core(lengths))


def gate_kernel(*refs):
    del refs


def gate(value, *earlier):
    return pl.pallas_call(
        gate_kernel,
        in_specs=[ANYWHERE] * (1 + len(earlier)),
        out_specs=ANYWHERE,
        out_shape=jax.ShapeDtypeStruct(value.shape, value.dtype),
        input_output_aliases={0: 0},
        cost_estimate=cost(0, 0),
        name="gate",
    )(value, *earlier)


def token_pieces(places, block):
    several = block.shape[0]
    pieces = jnp.swapaxes(block.reshape(several, 4, HALF, D // SECTIONS), 0, 1)
    got = []
    for turn in range(4):

        def route(s, d, turn=turn):
            piece = s ^ turn
            return 2 * (d % 2) + piece // 2, d - d % 2 + piece % 2

        got.append(places.send(pick(pieces, places.section ^ turn), route))
    return got


def in_order(pieces, mine):
    one, two = mine % 2 == 1, mine // 2 == 1
    a, b, c, d = pieces
    a, b, c, d = (
        jnp.where(one, b, a), jnp.where(one, a, b), jnp.where(one, d, c), jnp.where(one, c, d)
    )
    return (
        jnp.where(two, c, a), jnp.where(two, d, b), jnp.where(two, a, c), jnp.where(two, b, d)
    )


def deal_kernel(mine_ref, a_ref, b_ref, c_ref, later_ref, *out_refs):
    width = D // SECTIONS
    for k, ref in enumerate((a_ref, b_ref, c_ref)):
        rows = ref[...]
        features = [rows[:, f * width : (f + 1) * width] for f in range(SECTIONS)]
        for out_ref, piece in zip(out_refs, in_order(features, mine_ref[0]), strict=True):
            out_ref[k] = piece


def tokens_out(places, rows, later):
    width = D // SECTIONS
    features = pl.pallas_call(
        deal_kernel,
        grid=(1,),
        in_specs=[SCALAR, *[whole(HALF, D)] * 3, pl.BlockSpec(memory_space=pl.ANY)],
        out_specs=[pl.BlockSpec((3, HALF, width), lambda i: (0, 0, 0))] * SECTIONS,
        out_shape=[jax.ShapeDtypeStruct((3, HALF, width), BF)] * SECTIONS,
        compiler_params=params(),
        cost_estimate=cost(0, 4e6),
        name="deal",
    )(places.mine.reshape(1).astype(jnp.int32), *rows, later)
    got = []
    for turn in range(4):

        def route(s, d, turn=turn):
            return (2 * (s % 2) + d % 2) ^ turn, d - d % 2 + s // 2

        got.append(places.send(features[turn], route))
    return got


def undeal_kernel(section_ref, a_ref, b_ref, c_ref, d_ref, later_ref, x_ref, y_ref, z_ref):
    refs = (a_ref, b_ref, c_ref, d_ref)
    for k, out_ref in enumerate((x_ref, y_ref, z_ref)):
        pieces = in_order([ref[k] for ref in refs], section_ref[0])
        for number, piece in enumerate(pieces):
            out_ref[number * HALF : (number + 1) * HALF] = piece.astype(out_ref.dtype)


def tokens_placed(places, pieces, types, later):
    width = D // SECTIONS
    return pl.pallas_call(
        undeal_kernel,
        grid=(1,),
        in_specs=[SCALAR, *[pl.BlockSpec((3, HALF, width), lambda i: (0, 0, 0))] * 4, ANYWHERE],
        out_specs=[whole(4 * HALF, width)] * 3,
        out_shape=[shaped(4 * HALF, width, kind) for kind in types],
        compiler_params=params(),
        cost_estimate=cost(0, 4e6),
        name="undeal",
    )(places.section.reshape(1).astype(jnp.int32), *pieces, later)


def gather_start(places, mine, *earlier):
    one = places.swap_turned(mine, 0)
    if earlier:
        one = gate(one, *earlier)
    return one, places.swap_dp(one, 2), places.swap_turned(one, 1)


def gather_finish(places, pieces):
    return (*pieces, *(places.swap_core(piece) for piece in pieces))


def chosen_kernel(counts, starts, which_ref, *refs):
    total = sum(counts)
    arrays, (out_ref, held_ref, sems) = refs[:total], refs[total:]

    def rows_of(number):
        return arrays[number].at[:, pl.ds(starts[number], out_ref.shape[1])]

    first = 0
    for place, count in enumerate(counts):
        for number in range(count):

            @pl.when(which_ref[place] == number)
            def _():
                pltpu.make_async_copy(
                    rows_of(first + number), held_ref.at[place], sems.at[place]
                ).start()

        first += count
    for place in range(len(counts)):
        pltpu.make_async_copy(rows_of(0), held_ref.at[place], sems.at[place]).wait()
    for block in range(out_ref.shape[0]):
        value = held_ref[0, block].astype(F32)
        for place in range(1, len(counts)):
            value = value + held_ref[place, block].astype(F32)
        out_ref[block] = value.astype(BF)


def chosen_sum(which, groups, first, rows):
    arrays = [array for group in groups for array in group]
    shape = (arrays[0].shape[0], rows, D)
    counts = tuple(len(group) for group in groups)
    starts = tuple(0 if array.shape[1] == rows else first for array in arrays)
    return pl.pallas_call(
        functools.partial(chosen_kernel, counts, starts),
        grid=(1,),
        in_specs=[SCALAR, *[ANYWHERE] * sum(counts)],
        out_specs=full(*shape),
        out_shape=jax.ShapeDtypeStruct(shape, BF),
        scratch_shapes=[
            pltpu.VMEM((len(counts), *shape), BF), pltpu.SemaphoreType.DMA((len(counts),)),
        ],
        compiler_params=params(),
        cost_estimate=cost(1e6, 5e6),
        name="chosen_sum",
    )(
        jnp.stack([w.astype(jnp.int32) for w in which]), *[in_hbm(array) for array in arrays],
    )


class Reduction:
    def __init__(self, places):
        self.places = places
        rows = places.blk + 16
        cut = rows // 32 * 16
        self.ranges = ((0, cut), (cut, rows - cut))

    def cores(self, keep, give):
        return keep, self.places.swap_core(give)

    def total(self, which, *sections):
        groups = tuple(zip(*sections, strict=True))
        return [
            self.places.swap_plane(chosen_sum((which, which), groups, *rows), 0)
            for rows in self.ranges
        ]

    def send_early(self, one, two, three):
        places = self.places
        self.sections = (one, two, three)
        low, first = jnp.logical_not(places.first_bit), places.is_first
        which = jnp.where(low, 2, jnp.where(first, 1, 0))
        self.early = self.total(which, one, two, three)

    def plane(self, zero):
        places = self.places
        one, two, three = self.sections
        low, first = jnp.logical_not(places.first_bit), places.is_first
        which = jnp.where(low, jnp.where(first, 1, 2), 0)
        late = self.total(which, zero, one, two)
        keeps, gots = zip(zero, one, two, three, strict=True)
        other = places.section ^ jnp.where(first, 2, 1)
        sums = []
        for early_part, late_part, rows in zip(self.early, late, self.ranges, strict=True):

            def held(section, arrived=(early_part, late_part), rows=rows):
                is_late = (section == 0) | ((section == 1) & first) | ((section == 2) & (~first))
                return chosen_sum((section, section, is_late), (keeps, gots, arrived), *rows)

            got = places.swap_plane(held(other), 1)
            sums.append(held(places.section) + got)
        return sums

    def shared(self, rows):
        return jnp.where(self.places.is_first, rows, self.places.swap_core(rows))

    def depth(self, blocks, beside):
        places = self.places
        place = places.dp // 2
        if blocks.shape[0] == 4:
            near, far = place % 2, place // 2
            mine = jnp.where(places.is_first, near, 2 * far)
            theirs = jnp.where(places.is_first, 1 - near, 2 - 2 * far)
            step = 2 - places.core

            def two(first):
                return jnp.stack([pick(blocks, first), pick(blocks, first + step)])

            blocks = two(mine) + places.send(two(theirs), lambda s, d: (s, d ^ (2 + 2 * (d % 2))))
            mine = jnp.where(places.is_first, far, near)
            got = places.send(
                gate(pick(blocks, 1 - mine), beside), lambda s, d: (s, d ^ (4 - 2 * (d % 2)))
            )
            return pick(blocks, mine).astype(F32) + got.astype(F32), blocks
        bit = 1
        while blocks.shape[0] > 1:
            pairs = blocks.reshape(-1, 2, *blocks.shape[1:])
            mine = (place // bit) % 2
            keep = lax.dynamic_index_in_dim(pairs, mine, 1, keepdims=False)
            give = lax.dynamic_index_in_dim(pairs, 1 - mine, 1, keepdims=False)
            blocks = keep + places.swap_dp(give, 2 * bit)
            bit *= 2
        return blocks[0].astype(F32), blocks


def on_device(
    stream_input,
    accum_input,
    section_weights,
    section_norms,
    final_norm,
    seq_lengths,
    out_cotangent,
):
    places = Places()
    section, core = places.section, places.core
    width = D // SECTIONS
    rows = D // 2

    own = section_weights[0]
    pieces = token_pieces(places, stream_input[None])
    near_pieces = gather_start(
        places, lax.dynamic_slice(own, (core * rows, 0), (rows, 4 * D)), *pieces
    )
    small = jnp.stack(
        [section_norms.reshape(2 * D), jnp.pad(final_norm.reshape(2 * width), (0, 2 * D - 2 * width))]
    )
    late_mine = jnp.concatenate(
        [
            lax.dynamic_slice(own, (core * rows, 4 * D), (rows, 2 * D)),
            jnp.pad(small, ((0, 14), (0, 0))),
        ],
        axis=0,
    )
    late_pieces = gather_start(places, late_mine)
    near = gather_finish(places, near_pieces)
    late = gather_finish(places, late_pieces)
    stream = jnp.concatenate(in_order([piece[0] for piece in pieces], places.mine), axis=1)
    one, two, three = (piece[rows : rows + 2] for piece in late_pieces)
    table = in_order(
        (
            small, jnp.where(places.turned == 0, one, two), jnp.where(places.turned == 0, two, one),
            three,
        ),
        section,
    )
    norms = jnp.stack(table).reshape(SECTIONS, 4 * D).astype(F32)

    *segs, live = sequences(places, seq_lengths)
    qseg = segs[0]
    both = token_pieces(places, jnp.stack([accum_input, out_cotangent]))

    queries, own_kv = project(places, stream, own, near, 0)
    far_kv = places.swap_core(own_kv)
    *kept, branch_sum, turning, queries_two, own_kv_two = first_layer(
        places, stream, queries, own_kv, far_kv, segs, own, near, late, norms
    )
    far_kv_two = places.swap_core(own_kv_two)
    context, lse, middle, sum_a = second_attention(
        places, turning, queries_two, own_kv_two, far_kv_two, segs, own, near, norms
    )
    (
        result, dy_low, dy, final_grad, dz, dctx, delta, grads, keep_f, give_f, rest,
    ) = turn(
        places, middle, turning, sum_a, context, own, near, late, norms, branch_sum, both, live
    )

    reduction = Reduction(places)
    zero = jnp.zeros((HALF, D), F32)

    def scores(queries, own_kv, far_kv, dctx, lse, delta):
        dq, dkv_far = scores_back(queries, far_kv, dctx, qseg, segs[2], lse, delta, zero, BF)
        from_far = places.swap_core(dkv_far)
        dq, dkv = scores_back(queries, own_kv, dctx, qseg, segs[1], lse, delta, dq, BF)
        return dq, dkv, from_far

    third = reduction.cores(keep_f, give_f)
    dq, dkv, from_far = scores(queries_two, own_kv_two, far_kv_two, dctx, lse, delta)
    dz, dctx, delta, grads_first, keep_p, give_p, keep_f, give_f, rest = between(
        places, turning, dq, dkv, from_far, dz, dy, grads, final_grad, rest, kept, own, near,
        late, norms,
    )
    reduction.send_early(reduction.cores(keep_f, give_f), reduction.cores(keep_p, give_p), third)
    dq, dkv, from_far = scores(queries, own_kv, far_kv, dctx, kept[1], delta)
    upstream, keep, give = project_back(
        places, stream, dq, dkv, from_far, dz, own, near, 0, grads_first, final_grad, rest
    )
    blocks = reduction.plane(reduction.cores(keep, give))
    leaving = tokens_out(places, (upstream, result, dy_low), blocks[0])
    reduced, early = zip(*(reduction.depth(part, leaving[0]) for part in blocks), strict=True)
    reduced = jnp.concatenate(reduced, axis=0)
    shared = reduction.shared(reduced[places.blk :])
    stream_out, result_out, accum_out = tokens_placed(places, leaving, (F32, BF, F32), early[1])
    slab = reduced[: places.blk].T
    cut = D // places.ndp
    norm_out = lax.dynamic_slice(reduced, (places.blk, places.dp * cut), (2, cut))
    final_out = lax.dynamic_slice(shared, (2, section * width), (2, width))

    return (
        result_out,
        stream_out,
        accum_out,
        slab[None],
        norm_out[None],
        final_out,
    )


def solution(mesh):
    placed = (
        P("dp", "section"),
        P("dp", "section"),
        P("section", None, None),
        P("section", None, None),
        P(None, "section"),
        P("dp", None),
        P("dp", "section"),
    )
    return jax.shard_map(
        on_device,
        mesh=mesh,
        in_specs=placed,
        out_specs=(
            P("dp", "section"),
            P("dp", "section"),
            P("dp", "section"),
            P("section", None, "dp"),
            P("section", None, "dp"),
            P(None, "section"),
        ),
        check_vma=False,
    )
```

```python
import functools
import math

import jax
import jax.numpy as jnp
from jax import lax
from jax.experimental import pallas as pl
from jax.experimental.pallas import tpu as pltpu
from jax.sharding import PartitionSpec as P

D = 512
HEADS = 8
HEAD = 64
PACK = 1024
HALF = PACK // 2
PAIRS = HEADS // 2
LANES = 2 * HEAD
SECTIONS = 4
FAR = 1e30
SCALE = HEAD ** (-0.5)
BF = jnp.bfloat16
F32 = jnp.float32
NT = (((1,), (1,)), ((), ()))
TN = (((0,), (0,)), ((), ()))


def mm(left, right):
    return jnp.dot(left, right, preferred_element_type=F32)


def mm_nt(left, right):
    return lax.dot_general(left, right, NT, preferred_element_type=F32)


def mm_tn(left, right):
    return lax.dot_general(left, right, TN, preferred_element_type=F32)


def params(megabytes=16):
    return pltpu.CompilerParams(
        dimension_semantics=("arbitrary",), vmem_limit_bytes=megabytes * 1024 * 1024
    )


def shaped(rows, cols, dtype):
    return jax.ShapeDtypeStruct((rows, cols), dtype)


def in_hbm(array):
    return pltpu.with_memory_space_constraint(array, pltpu.HBM)


def whole(rows, cols):
    return pl.BlockSpec((rows, cols), lambda i: (0, 0))


SCALAR = pl.BlockSpec(memory_space=pltpu.SMEM)


def cost(flops, moved, transcendentals=0):
    return pl.CostEstimate(
        flops=int(flops), bytes_accessed=int(moved), transcendentals=int(transcendentals)
    )


def gain_of(table_ref, layer):
    return table_ref[layer : layer + 1, :D]


def shift_of(table_ref, layer):
    return table_ref[layer : layer + 1, D : 2 * D]


def norm_parts(summed):
    average = jnp.mean(summed, axis=-1, keepdims=True)
    centered = summed - average
    spread = jnp.mean(centered * centered, axis=-1, keepdims=True)
    inverse = lax.rsqrt(spread + 1e-05)
    return centered * inverse, inverse


def norm_forward(summed, table_ref, layer):
    normal, _ = norm_parts(summed)
    return normal * gain_of(table_ref, layer) + shift_of(table_ref, layer)


def norm_back(summed, gain, upstream):
    normal, inverse = norm_parts(summed)
    scaled = upstream * gain
    mean_one = jnp.mean(scaled, axis=-1, keepdims=True)
    mean_two = jnp.mean(scaled * normal, axis=-1, keepdims=True)
    grad = (scaled - mean_one - normal * mean_two) * inverse
    gain_grad = jnp.sum(upstream * normal, axis=0, keepdims=True)
    shift_grad = jnp.sum(upstream, axis=0, keepdims=True)
    return grad, gain_grad, shift_grad


def head_mask(which):
    lane = lax.broadcasted_iota(jnp.int32, (1, LANES), 1)
    return (lane // HEAD) == which


def three_way(column):
    high = column.astype(BF)
    rest = column - high.astype(F32)
    middle = rest.astype(BF)
    low = (rest - middle.astype(F32)).astype(BF)
    return high, middle, low


GROUP = 6


def fetch(where_ref, layer, own_ref, piece_refs, own_first, first, width, target, sem):
    section, core, turned = where_ref[0], where_ref[1], where_ref[3]
    half = D // 2
    step = section ^ layer
    mine_rows = pl.ds(pl.multiple_of(core * half, half), half)
    far_rows = pl.ds(pl.multiple_of((1 - core) * half, half), half)

    @pl.when(step == 0)
    def _():
        pltpu.make_async_copy(own_ref.at[:, pl.ds(own_first, width)], target, sem).start()

    for number, (partner, far_number) in enumerate(((1 + turned, 1), (2 - turned, 0), (3, 2))):

        @pl.when(step == partner)
        def _():
            part = (pl.ds(0, half), pl.ds(first, width))
            mine, far = piece_refs[number].at[part], piece_refs[3 + far_number].at[part]
            pltpu.make_async_copy(mine, target.at[mine_rows], sem).start()
            pltpu.make_async_copy(far, target.at[far_rows], sem).start()


def arrived(own_ref, width, target, sem):
    pltpu.make_async_copy(own_ref.at[:, pl.ds(0, width)], target, sem).wait()


def weight_specs(groups):
    return [pl.BlockSpec(memory_space=pl.ANY)] * (1 + GROUP * groups)


def column_of(pair):
    return pl.ds(pl.multiple_of(pair * LANES, LANES), LANES)


def fetch_projection(layer, where_ref, own_ref, near, weight_ref, sems):
    for part in range(3):
        fetch(
            where_ref, layer, own_ref, near, part * D, part * D, D, weight_ref.at[part],
            sems.at[part],
        )


def fetch_outward(layer, where_ref, own_ref, near, weight_ref, sem):
    fetch(where_ref, layer, own_ref, near, 3 * D, 3 * D, D, weight_ref, sem)


def fetch_feed(layer, where_ref, own_ref, near, late, weight_ref, sems):
    for chunk in range(4):
        turn = chunk % 2
        if chunk < 2:
            inner = (layer - 1, late, (4 + turn) * D, turn * D)
            outer = (layer, near, (2 + turn) * D, (2 + turn) * D)
        else:
            inner = (layer, near, turn * D, turn * D)
            outer = (layer, late, (4 + turn) * D, turn * D)
        for number, (whose, pieces, own_first, first) in enumerate((inner, outer)):
            fetch(
                where_ref, whose, own_ref, pieces, own_first, first, D,
                weight_ref.at[chunk, number], sems.at[chunk, number],
            )


PROJECTION = [pltpu.VMEM((3, D, D), BF), pltpu.SemaphoreType.DMA((3,))]
OUTWARD = [pltpu.VMEM((D, D), BF), pltpu.SemaphoreType.DMA]
FEED = [pltpu.VMEM((4, 2, D, D), BF), pltpu.SemaphoreType.DMA((4, 2))]


def put_projection(own_ref, x, q_ref, kv_ref, weight_ref, sems):
    def times(part):
        arrived(own_ref, D, weight_ref.at[part], sems.at[part])
        return mm(x, weight_ref[part]).astype(BF)

    q_ref[...] = times(0)
    keys, values = times(1), times(2)
    for pair in range(PAIRS):
        lanes = slice(pair * LANES, (pair + 1) * LANES)
        kv_ref[pair, :, :LANES] = keys[:, lanes]
        kv_ref[pair, :, LANES:] = values[:, lanes]


def put_attention(q_ref, own_ref, far_ref, qs_ref, kso_ref, ksx_ref, ctx_ref, lse_ref):
    none = jnp.zeros((), BF)
    lane = lax.broadcasted_iota(jnp.int32, (1, LANES), 1)
    ones = jnp.ones((HALF, LANES), BF)
    lse_ref[...] = jnp.zeros((HALF, LANES), F32)

    @pl.loop(0, PAIRS)
    def _(pair):
        q = q_ref[:, column_of(pair)] * jnp.asarray(SCALE, BF)
        keys_own = jnp.concatenate([own_ref[pair, :, :LANES], kso_ref[...]], axis=1)
        keys_other = jnp.concatenate([far_ref[pair, :, :LANES], ksx_ref[...]], axis=1)
        values_own, values_other = own_ref[pair, :, LANES:], far_ref[pair, :, LANES:]
        context = jnp.zeros((HALF, LANES), F32)
        logs = lse_ref[...]
        for which in range(2):
            mask = head_mask(which)
            query = jnp.concatenate([jnp.where(mask, q, none), qs_ref[...]], axis=1)
            score_own = mm_nt(query, keys_own)
            score_other = mm_nt(query, keys_other)
            peak = jnp.maximum(
                jnp.max(score_own, axis=1, keepdims=True),
                jnp.max(score_other, axis=1, keepdims=True),
            )
            own = jnp.exp(score_own - peak).astype(BF)
            other = jnp.exp(score_other - peak).astype(BF)
            total = mm(
                own, jnp.concatenate([jnp.where(mask, values_own, none), ones], axis=1)
            ) + mm(other, jnp.concatenate([jnp.where(mask, values_other, none), ones], axis=1))
            row_total = total[:, LANES:]
            context = context + total[:, :LANES] / row_total
            logs = jnp.where(lane == 2 * pair + which, peak + jnp.log(row_total), logs)
        lse_ref[...] = logs
        ctx_ref[:, column_of(pair)] = context.astype(BF)


def gelu_parts(v):
    root = 0.7978845608028654
    squared = v * v
    inner = root * (v + 0.044715 * v * squared)
    t = jnp.tanh(inner)
    hidden = 0.5 * v * (1.0 + t)
    slope = 0.5 * (1.0 + t) + 0.5 * v * (1.0 - t * t) * (root * (1.0 + 3 * 0.044715 * squared))
    return hidden, slope


def feed_weight(own_ref, weight_ref, sems, chunk, number):
    arrived(own_ref, D, weight_ref.at[chunk, number], sems.at[chunk, number])
    return weight_ref[chunk, number]


def half_of(refs, place):
    if not isinstance(refs, tuple):
        return refs, place
    half = refs[0].shape[0]
    return refs[place // half], place % half


def split_rows(core, blk, row, value, keep_ref, give_ref):
    step = math.gcd(D, blk)
    for k in range(value.shape[0] // step):
        part = value[k * step : (k + 1) * step]
        first = row + k * step
        block, offset = first // blk, first % blk

        @pl.when(block % 2 == core)
        def _():
            keep_ref[block // 2, offset : offset + step, :] = part

        @pl.when(block % 2 != core)
        def _():
            ref, place = half_of(give_ref, block // 2)
            ref[place, offset : offset + step, :] = part


def side_rows(grads, final_grads, keep_ref, give_ref):
    extra = jnp.concatenate([grads, final_grads, jnp.zeros((12, D), F32)], axis=0).astype(BF)
    blk = keep_ref.shape[1] - 16
    for block in range(keep_ref.shape[0]):
        keep_ref[block, blk:, :] = extra
        ref, place = half_of(give_ref, block)
        ref[place, blk:, :] = extra


def split_shapes(count, blk):
    return [full(count, blk + 16, D)] * 2, [pltpu.HBM((count, blk + 16, D), BF)] * 2


def put_outward_back(
    summed, upstream, dy, context, gain, weight_of, dctx_ref, delta_ref, grad_ref, rest_ref
):
    grad, gain_grad, shift_grad = norm_back(summed, gain, upstream)
    grad_ref[...] = jnp.concatenate([gain_grad, shift_grad], axis=0)
    df = (grad + dy).astype(BF)
    rest_ref[:D] = mm_tn(df, context).astype(BF)
    context_grad = mm_nt(df, weight_of()).astype(BF)
    dctx_ref[...] = context_grad
    product = context.astype(F32) * context_grad.astype(F32)
    lane = lax.broadcasted_iota(jnp.int32, (1, LANES), 1)
    delta = jnp.zeros((HALF, LANES), F32)
    for head in range(HEADS):
        part = product[:, (head // 2) * LANES : (head // 2 + 1) * LANES]
        inner = jnp.sum(jnp.where(head_mask(head % 2), part, 0.0), axis=1, keepdims=True)
        delta = jnp.where(lane == head, inner, delta)
    delta_ref[...] = delta
    return grad


def put_feed_back(
    core, x, hidden_of, df, grad, weight_of, rest_ref, keep_ref, give_ref
):
    blk = keep_ref.shape[1] - 16
    total = grad
    for chunk in range(4):
        inner, outer = weight_of(chunk, 0), weight_of(chunk, 1)
        hidden, slope = hidden_of(chunk, inner)
        split_rows(core, blk, (2 + chunk) * D, mm_tn(hidden, df).astype(BF), keep_ref, give_ref)
        preact_grad = (mm(df, outer) * slope).astype(BF)
        inner_grad = mm_tn(preact_grad, x).astype(BF)
        if chunk < 2:
            rest_ref[(1 + chunk) * D : (2 + chunk) * D] = inner_grad
        else:
            split_rows(core, blk, (chunk - 2) * D, inner_grad, keep_ref, give_ref)
        total = total + mm_nt(preact_grad, inner)
    return total


def put_project_back(
    core, x, dq_ref, dkv_ref, far_ref, dz, grads, final_grads, rest_ref, weight_of, keep_ref,
    give_ref,
):
    blk = keep_ref.shape[1] - 16
    side_rows(grads, final_grads, keep_ref, give_ref)
    split_rows(core, blk, 3 * D, rest_ref[...], keep_ref, give_ref)
    parts = [(dkv_ref[k].astype(F32) + far_ref[k].astype(F32)).astype(BF) for k in range(PAIRS)]
    dk = jnp.concatenate([part[:, :LANES] for part in parts], axis=1)
    dv = jnp.concatenate([part[:, LANES:] for part in parts], axis=1)
    total = dz
    for place, grad in enumerate((dq_ref[...].astype(BF), dk, dv)):
        split_rows(core, blk, place * D, mm_tn(grad, x).astype(BF), keep_ref, give_ref)
        total = total + mm_nt(grad, weight_of(place))
    return total


def full(*shape):
    return pl.BlockSpec(shape, lambda i: (0,) * len(shape), pipeline_mode=pl.Buffered(1))


KV = (PAIRS, HALF, 2 * LANES)
TABLE = (SECTIONS, 4 * D)


def project_kernel(layer, where_ref, x_ref, own_ref, *refs):
    near, (q_ref, kv_ref, weight_ref, sems) = refs[:GROUP], refs[GROUP:]
    fetch_projection(layer, where_ref, own_ref, near, weight_ref, sems)
    put_projection(own_ref, x_ref[...], q_ref, kv_ref, weight_ref, sems)


def project(places, stream, own, near, layer):
    return pl.pallas_call(
        functools.partial(project_kernel, layer),
        grid=(1,),
        in_specs=[SCALAR, full(HALF, D), *weight_specs(1)],
        out_specs=[full(HALF, D), full(*KV)],
        out_shape=[shaped(HALF, D, BF), jax.ShapeDtypeStruct(KV, BF)],
        scratch_shapes=PROJECTION,
        compiler_params=params(),
        cost_estimate=cost(2 * HALF * D * 3 * D, 4e6),
        name="project",
    )(places.where, stream, *map(in_hbm, (own, *near)))


def feed_kernel(layer, where_ref, x_ref, sum_ref, middle_ref, norm_ref, own_ref, *refs):
    near, late, refs = refs[:GROUP], refs[GROUP : 2 * GROUP], refs[2 * GROUP :]
    (
        sum_f_ref, branch_ref, next_ref, q_next_ref, kv_next_ref, feed_ref, feed_sems,
        project_ref, project_sems,
    ) = refs
    fetch_feed(layer, where_ref, own_ref, near, late, feed_ref, feed_sems)
    fetch_projection(layer + 1, where_ref, own_ref, near, project_ref, project_sems)
    middle = middle_ref[...]
    total = jnp.zeros((HALF, D), F32)
    for chunk in range(4):
        inner = feed_weight(own_ref, feed_ref, feed_sems, chunk, 0)
        hidden = gelu_parts(mm(middle, inner))[0].astype(BF)
        total = total + mm_nt(hidden, feed_weight(own_ref, feed_ref, feed_sems, chunk, 1))
    summed = middle.astype(F32) + total
    sum_f_ref[...] = summed
    branch_ref[...] = sum_ref[...] - x_ref[...].astype(F32) + total
    following = norm_forward(summed, norm_ref, layer).astype(BF)
    next_ref[...] = following
    put_projection(own_ref, following, q_next_ref, kv_next_ref, project_ref, project_sems)


def feed(places, stream, sum_a, middle, own, near, late, norms, layer):
    return pl.pallas_call(
        functools.partial(feed_kernel, layer),
        grid=(1,),
        in_specs=[SCALAR, *[full(HALF, D)] * 3, full(*TABLE), *weight_specs(2)],
        out_specs=[*[full(HALF, D)] * 4, full(*KV)],
        out_shape=[
            shaped(HALF, D, F32), shaped(HALF, D, F32), shaped(HALF, D, BF), shaped(HALF, D, BF),
            jax.ShapeDtypeStruct(KV, BF),
        ],
        scratch_shapes=[*FEED, *PROJECTION],
        compiler_params=params(24),
        cost_estimate=cost(6e9, 14e6, 1e6),
        name="feed",
    )(places.where, *map(in_hbm, (stream, sum_a, middle)), norms, *map(in_hbm, (own, *near, *late)))


def attend_kernel(
    layer, where_ref, q_ref, own_kv_ref, far_kv_ref, qs_ref, kso_ref, ksx_ref, x_ref, norm_ref,
    own_ref, *refs,
):
    near, refs = refs[:GROUP], refs[GROUP:]
    ctx_ref, lse_ref, middle_ref, sum_ref, outward_ref, outward_sem = refs
    fetch_outward(layer, where_ref, own_ref, near, outward_ref, outward_sem)
    put_attention(
        q_ref, own_kv_ref, far_kv_ref, qs_ref, kso_ref, ksx_ref, ctx_ref, lse_ref
    )
    arrived(own_ref, D, outward_ref, outward_sem)
    summed = x_ref[...].astype(F32) + mm(ctx_ref[...], outward_ref[...])
    sum_ref[...] = summed
    middle_ref[...] = norm_forward(summed, norm_ref, layer).astype(BF)


def attend(places, stream, queries, own_kv, far_kv, segs, own, near, norms, layer):
    kind = jax.ShapeDtypeStruct if layer else pltpu.HBM
    return pl.pallas_call(
        functools.partial(attend_kernel, layer),
        grid=(1,),
        in_specs=[
            SCALAR, full(HALF, D), full(*KV), full(*KV), *[full(HALF, LANES)] * 3, full(HALF, D),
            full(*TABLE), *weight_specs(1),
        ],
        out_specs=[full(HALF, D), full(HALF, LANES), full(HALF, D), full(HALF, D)],
        out_shape=[
            kind((HALF, D), BF), kind((HALF, LANES), F32), kind((HALF, D), BF),
            kind((HALF, D), F32),
        ],
        scratch_shapes=OUTWARD,
        compiler_params=params(),
        cost_estimate=cost(9e9, 10e6, 4e6),
        name="attend",
    )(places.where, queries, own_kv, far_kv, *segs, stream, norms, *map(in_hbm, (own, *near)))


def turn_kernel(
    layer, where_ref, middle_ref, x_ref, sum_ref, ctx_ref, norm_ref, branch_ref,
    a_ref, b_ref, c_ref, d_ref, live_ref, own_ref, *refs,
):
    near, late, refs = refs[:GROUP], refs[GROUP : 2 * GROUP], refs[2 * GROUP :]
    (
        result_ref, low_ref, dy_ref, final_ref, dz_ref, dctx_ref, delta_ref, grad_ref,
        feed_keep, feed_give, rest_ref,
        hidden_ref, slope_ref, outward_ref, outward_sem, feed_ref, feed_sems,
    ) = refs
    core, mine = where_ref[1], where_ref[2]
    fetch_feed(layer + 1, where_ref, own_ref, near, late, feed_ref, feed_sems)
    fetch_outward(layer, where_ref, own_ref, near, outward_ref, outward_sem)
    middle, sum_a = middle_ref[...], sum_ref[...]
    branch = sum_a - x_ref[...].astype(F32)
    total = jnp.zeros((HALF, D), F32)
    for chunk in range(4):
        inner = feed_weight(own_ref, feed_ref, feed_sems, chunk, 0)
        hidden, slope = gelu_parts(mm(middle, inner))
        hidden = hidden.astype(BF)
        hidden_ref[chunk] = hidden
        slope_ref[chunk] = slope
        total = total + mm_nt(hidden, feed_weight(own_ref, feed_ref, feed_sems, chunk, 1))
    sum_f = middle.astype(F32) + total
    last = norm_forward(sum_f, norm_ref, layer + 1)

    pieces = in_order([ref[...] for ref in (a_ref, b_ref, c_ref, d_ref)], mine)
    accum, cot = (jnp.concatenate([piece[k] for piece in pieces], axis=1) for k in range(2))
    summed = accum.astype(F32) + (branch_ref[...] + (branch + total))
    normal, _ = norm_parts(summed)
    width = D // SECTIONS
    gain, shift = (
        jnp.concatenate(
            [
                norm_ref[k : k + 1, 2 * D + part * width : 2 * D + (part + 1) * width]
                for k in range(SECTIONS)
            ],
            axis=1,
        )
        for part in range(2)
    )
    result_ref[...] = (last + normal * gain + shift).astype(BF)
    cot = cot.astype(F32) * live_ref[:, 0:1]
    dy, gain_grad, shift_grad = norm_back(summed, gain, cot)
    dy_ref[...] = dy
    low_ref[...] = dy.astype(BF)
    final_grads = jnp.concatenate([gain_grad, shift_grad], axis=0)
    final_ref[...] = final_grads

    grad, gain_grad, shift_grad = norm_back(sum_f, gain_of(norm_ref, layer + 1), cot)
    side_rows(
        jnp.concatenate([gain_grad, shift_grad], axis=0), final_grads, feed_keep, feed_give
    )
    upstream = put_feed_back(
        core, middle, lambda chunk, inner: (hidden_ref[chunk], slope_ref[chunk]),
        (grad + dy).astype(BF), grad, lambda chunk, number: feed_ref[chunk, number],
        rest_ref, feed_keep, feed_give,
    )
    arrived(own_ref, D, outward_ref, outward_sem)
    dz_ref[...] = put_outward_back(
        sum_a, upstream.astype(BF).astype(F32), dy, ctx_ref[...], gain_of(norm_ref, layer),
        lambda: outward_ref[...], dctx_ref, delta_ref, grad_ref, rest_ref,
    )


def turn(places, middle, stream, sum_a, context, own, near, late, norms, branch_sum, pieces, live):
    specs, shapes = split_shapes(places.ndp // 2, places.blk)
    return pl.pallas_call(
        functools.partial(turn_kernel, 2),
        grid=(1,),
        in_specs=[
            SCALAR, *[full(HALF, D)] * 4, full(*TABLE), full(HALF, D),
            *[full(2, HALF, D // SECTIONS)] * 4, full(HALF, LANES), *weight_specs(2),
        ],
        out_specs=[
            *[full(HALF, D)] * 3, full(2, D), full(HALF, D), full(HALF, D),
            full(HALF, LANES), full(2, D), *specs, full(3 * D, D),
        ],
        out_shape=[
            shaped(HALF, D, BF), shaped(HALF, D, BF),
            shaped(HALF, D, F32), shaped(2, D, F32), shaped(HALF, D, F32), shaped(HALF, D, BF),
            shaped(HALF, LANES, F32), shaped(2, D, F32), *shapes, shaped(3 * D, D, BF),
        ],
        scratch_shapes=[
            pltpu.VMEM((4, HALF, D), BF), pltpu.VMEM((4, HALF, D), F32), *OUTWARD, *FEED,
        ],
        compiler_params=params(40),
        cost_estimate=cost(16e9, 30e6, 2e6),
        name="turn",
    )(
        places.where, middle, stream, sum_a, context, norms, branch_sum, *pieces, live, *map(in_hbm, (own, *near, *late)),
    )


def column():
    return pl.BlockSpec((HALF, LANES), lambda i: (0, i))


def pair_block():
    return pl.BlockSpec((1, HALF, 2 * LANES), lambda i: (i, 0, 0))


def scores_back_kernel(
    q_ref, kv_ref, dctx_ref, qs_ref, ks_ref, lse_ref, delta_ref, before_ref, dq_ref, dkv_ref
):
    pair = pl.program_id(0)
    none = jnp.zeros((), BF)
    lane = lax.broadcasted_iota(jnp.int32, (1, LANES), 1)
    q = q_ref[...] * jnp.asarray(SCALE, BF)
    k = kv_ref[0, :, :LANES]
    k_scaled = k * jnp.asarray(SCALE, BF)
    dctx = dctx_ref[...]
    extra = jnp.where((lane >= LANES - 3), jnp.ones((), BF), none)
    keys = jnp.concatenate([k, ks_ref[...] + extra], axis=1)
    values = jnp.concatenate(
        [kv_ref[0, :, LANES:], jnp.broadcast_to(extra, (HALF, LANES))], axis=1
    )
    dq = before_ref[...]
    dk = jnp.zeros((HALF, LANES), F32)
    dv = jnp.zeros((HALF, LANES), F32)
    for which in range(2):
        mask = head_mask(which)
        here = lane == 2 * pair + which

        def lanes_of(table, base):
            column = -jnp.sum(jnp.where(here, table, 0.0), axis=1, keepdims=True)
            high, middle, low = three_way(column)
            base = jnp.where(lane == LANES - 3, high, base)
            base = jnp.where(lane == LANES - 2, middle, base)
            return jnp.where(lane == LANES - 1, low, base)

        query_part = jnp.where(mask, q, none)
        dctx_part = jnp.where(mask, dctx, none)
        query = jnp.concatenate([query_part, lanes_of(lse_ref[...], qs_ref[...])], axis=1)
        dcontext = jnp.concatenate(
            [dctx_part, lanes_of(delta_ref[...], jnp.zeros((HALF, LANES), BF))], axis=1
        )
        probability = jnp.exp(mm_nt(keys, query))
        score_grad = (probability * mm_nt(values, dcontext)).astype(BF)
        dv = dv + mm(probability.astype(BF), dctx_part)
        dk = dk + mm(score_grad, query_part)
        dq = dq + mm_tn(score_grad, jnp.where(mask, k_scaled, none))
    dq_ref[...] = dq
    dkv_ref[0, :, :LANES] = dk.astype(dkv_ref.dtype)
    dkv_ref[0, :, LANES:] = dv.astype(dkv_ref.dtype)


def scores_back(queries, kv, dctx, qseg, kseg, lse, delta, before, out_type):
    return pl.pallas_call(
        scores_back_kernel,
        grid=(PAIRS,),
        in_specs=[
            column(), pair_block(), column(),
            whole(HALF, LANES), whole(HALF, LANES), whole(HALF, LANES), whole(HALF, LANES),
            column(),
        ],
        out_specs=[column(), pair_block()],
        out_shape=[
            shaped(HALF, D, F32), jax.ShapeDtypeStruct((PAIRS, HALF, 2 * LANES), out_type),
        ],
        compiler_params=params(),
        cost_estimate=cost(8e9, 8e6, 2e6),
        name="scores_back",
    )(queries, kv, dctx, qseg, kseg, lse, delta, before)


def middle_kernel(
    layer, where_ref, x_ref, dq_ref, dkv_ref, far_ref, dz_ref, dy_ref, grad_ref, final_ref,
    before_ref, middle_ref, sum_f_ref, sum_a_ref, ctx_ref, norm_ref, own_ref, *refs,
):
    near, late, refs = refs[:GROUP], refs[GROUP : 2 * GROUP], refs[2 * GROUP :]
    (
        dz_out, dctx_ref, delta_ref, grad_out, project_keep, project_give, feed_keep, feed_give,
        rest_ref,
        project_ref, project_sems, feed_ref, feed_sems, outward_ref, outward_sem,
    ) = refs
    core = where_ref[1]
    fetch_projection(layer, where_ref, own_ref, near, project_ref, project_sems)
    fetch_feed(layer - 1, where_ref, own_ref, near, late, feed_ref, feed_sems)
    fetch_outward(layer - 2, where_ref, own_ref, near, outward_ref, outward_sem)
    final_grads = final_ref[...]

    def project_weight(place):
        arrived(own_ref, D, project_ref.at[place], project_sems.at[place])
        return project_ref[place]

    def outward_weight():
        arrived(own_ref, D, outward_ref, outward_sem)
        return outward_ref[...]

    upstream = put_project_back(
        core, x_ref[...], dq_ref, dkv_ref, far_ref, dz_ref[...], grad_ref[...], final_grads,
        before_ref, project_weight, project_keep, project_give,
    ).astype(BF).astype(F32)
    dy = dy_ref[...]
    grad, gain_grad, shift_grad = norm_back(
        sum_f_ref[...], gain_of(norm_ref, layer - 1), upstream
    )
    side_rows(
        jnp.concatenate([gain_grad, shift_grad], axis=0), final_grads, feed_keep, feed_give
    )
    middle = middle_ref[...]

    def hidden_of(chunk, inner):
        hidden, slope = gelu_parts(mm(middle, inner))
        return hidden.astype(BF), slope

    upstream = put_feed_back(
        core, middle, hidden_of, (grad + dy).astype(BF), grad,
        functools.partial(feed_weight, own_ref, feed_ref, feed_sems), rest_ref, feed_keep, feed_give,
    ).astype(BF).astype(F32)
    dz_out[...] = put_outward_back(
        sum_a_ref[...], upstream, dy, ctx_ref[...], gain_of(norm_ref, layer - 2),
        outward_weight, dctx_ref, delta_ref, grad_out, rest_ref,
    )


def between(
    places, stream, dq, dkv, far, dz, dy, grads, final_grads, rest, kept, own, near, late, norms
):
    context, _, middle, sum_a, sum_f = kept
    specs, shapes = split_shapes(places.ndp // 2, places.blk)
    return pl.pallas_call(
        functools.partial(middle_kernel, 2),
        grid=(1,),
        in_specs=[
            SCALAR, full(HALF, D), full(HALF, D), full(*KV), full(*KV), full(HALF, D),
            full(HALF, D), full(2, D), full(2, D), full(3 * D, D), *[full(HALF, D)] * 4,
            full(*TABLE), *weight_specs(2),
        ],
        out_specs=[
            full(HALF, D), full(HALF, D), full(HALF, LANES), full(2, D), *specs, *specs,
            full(3 * D, D),
        ],
        out_shape=[
            shaped(HALF, D, F32), shaped(HALF, D, BF), shaped(HALF, LANES, F32),
            shaped(2, D, F32), *shapes, *shapes, shaped(3 * D, D, BF),
        ],
        scratch_shapes=[*PROJECTION, *FEED, *OUTWARD],
        compiler_params=params(44),
        cost_estimate=cost(20e9, 30e6, 2e6),
        name="between",
    )(
        places.where, stream, dq, dkv, far, dz, dy, grads, final_grads, rest, middle, sum_f,
        sum_a, context, norms, *map(in_hbm, (own, *near, *late)),
    )


def project_back_kernel(
    layer, where_ref, x_ref, dq_ref, dkv_ref, far_ref, dz_ref, grad_ref, final_ref, rest_ref,
    own_ref, *refs,
):
    near, (dx_ref, keep_ref, *give, weight_ref, sems) = refs[:GROUP], refs[GROUP:]
    fetch_projection(layer, where_ref, own_ref, near, weight_ref, sems)

    def weight_of(place):
        arrived(own_ref, D, weight_ref.at[place], sems.at[place])
        return weight_ref[place]

    dx_ref[...] = put_project_back(
        where_ref[1], x_ref[...], dq_ref, dkv_ref, far_ref, dz_ref[...], grad_ref[...],
        final_ref[...], rest_ref, weight_of, keep_ref, tuple(give),
    ).astype(BF)


def project_back(places, stream, dq, dkv, far, dz, own, near, layer, grads, final_grads, rest):
    specs, shapes = split_shapes(places.ndp // 2, places.blk)
    half_specs, half_shapes = split_shapes(places.ndp // 4, places.blk)
    return pl.pallas_call(
        functools.partial(project_back_kernel, layer),
        grid=(1,),
        in_specs=[
            SCALAR, full(HALF, D), full(HALF, D), full(*KV), full(*KV), full(HALF, D),
            full(2, D), full(2, D), full(3 * D, D), *weight_specs(1),
        ],
        out_specs=[full(HALF, D), specs[0], *half_specs],
        out_shape=[shaped(HALF, D, BF), shapes[0], *half_shapes],
        scratch_shapes=PROJECTION,
        compiler_params=params(20),
        cost_estimate=cost(4 * HALF * D * 3 * D, 10e6),
        name="project_back",
    )(places.where, stream, dq, dkv, far, dz, grads, final_grads, rest, *map(in_hbm, (own, *near)))


class Places:
    def __init__(self):
        self.ndp = lax.axis_size("dp")
        self.section = lax.axis_index("section")
        self.dp = lax.axis_index("dp")
        self.core = self.dp % 2
        self.blk = 6 * D // self.ndp
        self.mine = 2 * (self.section % 2) + self.core
        self.turned = (self.dp + self.dp // 2) % 2
        self.where = jnp.stack([self.section, self.core, self.mine, self.turned]).astype(jnp.int32)
        bits = (self.section % 2 == 1, self.section // 2 == 1)
        self.is_first = self.core == 0
        self.first_bit = jnp.where(self.is_first, bits[0], bits[1])
        self.second_bit = jnp.where(self.is_first, bits[1], bits[0])

    def swap_dp(self, block, step):
        return lax.ppermute(block, "dp", [(i, i ^ step) for i in range(self.ndp)])

    def swap_core(self, block):
        return self.swap_dp(block, 1)

    def swap_plane(self, block, turn):
        return self.send(block, lambda s, d: (s ^ (1 + (d + turn) % 2), d))

    def swap_turned(self, block, turn):
        return self.send(block, lambda s, d: (s ^ (1 + (d + d // 2 + turn) % 2), d))

    def send(self, block, route):
        pairs = []
        for s in range(SECTIONS):
            for d in range(self.ndp):
                to = route(s, d)
                pairs.append((s * self.ndp + d, to[0] * self.ndp + to[1]))
        return lax.ppermute(block, ("section", "dp"), pairs)


def pick(stack, index):
    return lax.dynamic_index_in_dim(stack, index, 0, keepdims=False)


ANYWHERE = pl.BlockSpec(memory_space=pl.ANY)


def sequence_kernel(where_ref, own_ref, far_ref, qseg_ref, own_seg_ref, far_seg_ref, live_ref):
    section, core = where_ref[0], where_ref[1]
    here = core == section // 2
    row = section % 2
    lane = lax.broadcasted_iota(jnp.int32, (HALF, LANES), 1)
    spot = lax.broadcasted_iota(jnp.int32, (HALF, LANES), 0)
    own = jnp.zeros((HALF, LANES), jnp.int32)
    far = jnp.zeros((HALF, LANES), jnp.int32)
    ending = jnp.int32(0)
    for k in range(own_ref.shape[1]):
        ending = ending + jnp.where(here, own_ref[row, k], far_ref[row, k])
        own = own + (spot + core * HALF >= ending).astype(jnp.int32)
        far = far + (spot + (1 - core) * HALF >= ending).astype(jnp.int32)
    own_seg_ref[...] = jnp.where(own == lane, 1.0, 0.0).astype(BF)
    far_seg_ref[...] = jnp.where(far == lane, 1.0, 0.0).astype(BF)
    qseg_ref[...] = jnp.where((own != lane) & (lane < 32), -FAR, 0.0).astype(BF)
    live_ref[...] = jnp.where(spot + core * HALF < ending, 1.0, 0.0)


def sequences(places, lengths):
    return pl.pallas_call(
        sequence_kernel,
        grid=(1,),
        in_specs=[SCALAR] * 3,
        out_specs=[whole(HALF, LANES)] * 4,
        out_shape=[shaped(HALF, LANES, BF)] * 3 + [shaped(HALF, LANES, F32)],
        compiler_params=params(),
        cost_estimate=cost(1e6, 1e6),
        name="sequences",
    )(places.where, lengths, places.swap_core(lengths))


def gate_kernel(*refs):
    del refs


def gate(value, *earlier):
    return pl.pallas_call(
        gate_kernel,
        in_specs=[ANYWHERE] * (1 + len(earlier)),
        out_specs=ANYWHERE,
        out_shape=jax.ShapeDtypeStruct(value.shape, value.dtype),
        input_output_aliases={0: 0},
        cost_estimate=cost(0, 0),
        name="gate",
    )(value, *earlier)


def token_pieces(places, block):
    several = block.shape[0]
    pieces = jnp.swapaxes(block.reshape(several, 4, HALF, D // SECTIONS), 0, 1)
    got = []
    for turn in range(4):

        def route(s, d, turn=turn):
            piece = s ^ turn
            return 2 * (d % 2) + piece // 2, d - d % 2 + piece % 2

        got.append(places.send(pick(pieces, places.section ^ turn), route))
    return got


def in_order(pieces, mine):
    one, two = mine % 2 == 1, mine // 2 == 1
    a, b, c, d = pieces
    a, b, c, d = (
        jnp.where(one, b, a), jnp.where(one, a, b), jnp.where(one, d, c), jnp.where(one, c, d)
    )
    return (
        jnp.where(two, c, a), jnp.where(two, d, b), jnp.where(two, a, c), jnp.where(two, b, d)
    )


def deal_kernel(mine_ref, a_ref, b_ref, c_ref, later_ref, *out_refs):
    width = D // SECTIONS
    for k, ref in enumerate((a_ref, b_ref, c_ref)):
        rows = ref[...]
        features = [rows[:, f * width : (f + 1) * width] for f in range(SECTIONS)]
        for out_ref, piece in zip(out_refs, in_order(features, mine_ref[0]), strict=True):
            out_ref[k] = piece


def tokens_out(places, rows, later):
    width = D // SECTIONS
    features = pl.pallas_call(
        deal_kernel,
        grid=(1,),
        in_specs=[SCALAR, *[whole(HALF, D)] * 3, pl.BlockSpec(memory_space=pl.ANY)],
        out_specs=[pl.BlockSpec((3, HALF, width), lambda i: (0, 0, 0))] * SECTIONS,
        out_shape=[jax.ShapeDtypeStruct((3, HALF, width), BF)] * SECTIONS,
        compiler_params=params(),
        cost_estimate=cost(0, 4e6),
        name="deal",
    )(places.mine.reshape(1).astype(jnp.int32), *rows, later)
    got = []
    for turn in range(4):

        def route(s, d, turn=turn):
            return (2 * (s % 2) + d % 2) ^ turn, d - d % 2 + s // 2

        got.append(places.send(features[turn], route))
    return got


def undeal_kernel(section_ref, a_ref, b_ref, c_ref, d_ref, later_ref, x_ref, y_ref, z_ref):
    refs = (a_ref, b_ref, c_ref, d_ref)
    for k, out_ref in enumerate((x_ref, y_ref, z_ref)):
        pieces = in_order([ref[k] for ref in refs], section_ref[0])
        for number, piece in enumerate(pieces):
            out_ref[number * HALF : (number + 1) * HALF] = piece.astype(out_ref.dtype)


def tokens_placed(places, pieces, types, later):
    width = D // SECTIONS
    return pl.pallas_call(
        undeal_kernel,
        grid=(1,),
        in_specs=[SCALAR, *[pl.BlockSpec((3, HALF, width), lambda i: (0, 0, 0))] * 4, ANYWHERE],
        out_specs=[whole(4 * HALF, width)] * 3,
        out_shape=[shaped(4 * HALF, width, kind) for kind in types],
        compiler_params=params(),
        cost_estimate=cost(0, 4e6),
        name="undeal",
    )(places.section.reshape(1).astype(jnp.int32), *pieces, later)


def gather_start(places, mine, *earlier):
    one = places.swap_turned(mine, 0)
    if earlier:
        one = gate(one, *earlier)
    return one, places.swap_dp(one, 2), places.swap_turned(one, 1)


def gather_finish(places, pieces):
    return (*pieces, *(places.swap_core(piece) for piece in pieces))


def chosen_kernel(counts, parts, starts, which_ref, *refs):
    total = sum(parts)
    arrays, (out_ref, held_ref, sems) = refs[:total], refs[total:]
    blocks, rows, _ = out_ref.shape

    def copies(number, place):
        first = sum(parts[:number])
        count = blocks // parts[number]
        for k in range(parts[number]):
            source = arrays[first + k].at[:, pl.ds(starts[number], rows)]
            target = held_ref.at[place, pl.ds(k * count, count)]
            yield pltpu.make_async_copy(source, target, sems.at[place])

    first = 0
    for place, count in enumerate(counts):
        for number in range(count):

            @pl.when(which_ref[place] == number)
            def _():
                for copy in copies(first + number, place):
                    copy.start()

        first += count
    for place in range(len(counts)):
        held = held_ref.at[place]
        pltpu.make_async_copy(held, held, sems.at[place]).wait()
    for block in range(out_ref.shape[0]):
        value = held_ref[0, block].astype(F32)
        for place in range(1, len(counts)):
            value = value + held_ref[place, block].astype(F32)
        out_ref[block] = value.astype(BF)


def chosen_sum(which, groups, first, rows):
    entries = [
        array if isinstance(array, tuple) else (array,) for group in groups for array in group
    ]
    arrays = [array for entry in entries for array in entry]
    shape = (sum(array.shape[0] for array in entries[0]), rows, D)
    counts = tuple(len(group) for group in groups)
    parts = tuple(len(entry) for entry in entries)
    starts = tuple(0 if entry[0].shape[1] == rows else first for entry in entries)
    return pl.pallas_call(
        functools.partial(chosen_kernel, counts, parts, starts),
        grid=(1,),
        in_specs=[SCALAR, *[ANYWHERE] * len(arrays)],
        out_specs=full(*shape),
        out_shape=jax.ShapeDtypeStruct(shape, BF),
        scratch_shapes=[
            pltpu.VMEM((len(counts), *shape), BF), pltpu.SemaphoreType.DMA((len(counts),)),
        ],
        compiler_params=params(),
        cost_estimate=cost(1e6, 5e6),
        name="chosen_sum",
    )(
        jnp.stack([w.astype(jnp.int32) for w in which]), *[in_hbm(array) for array in arrays],
    )


class Reduction:
    def __init__(self, places):
        self.places = places
        rows = places.blk + 16
        cut = rows // 32 * 16
        self.ranges = ((0, cut), (cut, rows - cut))

    def cores(self, keep, give):
        return keep, self.places.swap_core(give)

    def total(self, which, *sections):
        groups = tuple(zip(*sections, strict=True))
        return [
            self.places.swap_plane(chosen_sum((which, which), groups, *rows), 0)
            for rows in self.ranges
        ]

    def send_early(self, one, two, three):
        places = self.places
        self.sections = (one, two, three)
        low, first = jnp.logical_not(places.first_bit), places.is_first
        which = jnp.where(low, 2, jnp.where(first, 1, 0))
        self.early = self.total(which, one, two, three)

    def plane(self, zero):
        places = self.places
        one, two, three = self.sections
        low, first = jnp.logical_not(places.first_bit), places.is_first
        which = jnp.where(low, jnp.where(first, 1, 2), 0)
        late = self.total(which, zero, one, two)
        keeps, gots = zip(zero, one, two, three, strict=True)
        other = places.section ^ jnp.where(first, 2, 1)
        sums = []
        for early_part, late_part, rows in zip(self.early, late, self.ranges, strict=True):

            def held(section, arrived=(early_part, late_part), rows=rows):
                is_late = (section == 0) | ((section == 1) & first) | ((section == 2) & (~first))
                return chosen_sum((section, section, is_late), (keeps, gots, arrived), *rows)

            got = places.swap_plane(held(other), 1)
            sums.append(held(places.section) + got)
        return sums

    def shared(self, rows):
        return jnp.where(self.places.is_first, rows, self.places.swap_core(rows))

    def depth(self, blocks, beside):
        places = self.places
        place = places.dp // 2
        if blocks.shape[0] == 4:
            near, far = place % 2, place // 2
            mine = jnp.where(places.is_first, near, 2 * far)
            theirs = jnp.where(places.is_first, 1 - near, 2 - 2 * far)
            step = 2 - places.core

            def two(first):
                return jnp.stack([pick(blocks, first), pick(blocks, first + step)])

            blocks = two(mine) + places.send(two(theirs), lambda s, d: (s, d ^ (2 + 2 * (d % 2))))
            mine = jnp.where(places.is_first, far, near)
            got = places.send(
                gate(pick(blocks, 1 - mine), beside), lambda s, d: (s, d ^ (4 - 2 * (d % 2)))
            )
            return pick(blocks, mine).astype(F32) + got.astype(F32), blocks
        bit = 1
        while blocks.shape[0] > 1:
            pairs = blocks.reshape(-1, 2, *blocks.shape[1:])
            mine = (place // bit) % 2
            keep = lax.dynamic_index_in_dim(pairs, mine, 1, keepdims=False)
            give = lax.dynamic_index_in_dim(pairs, 1 - mine, 1, keepdims=False)
            blocks = keep + places.swap_dp(give, 2 * bit)
            bit *= 2
        return blocks[0].astype(F32), blocks


def on_device(
    stream_input,
    accum_input,
    section_weights,
    section_norms,
    final_norm,
    seq_lengths,
    out_cotangent,
):
    places = Places()
    section, core = places.section, places.core
    width = D // SECTIONS
    rows = D // 2

    own = section_weights[0]
    pieces = token_pieces(places, stream_input[None])
    small = jnp.concatenate([section_norms.reshape(2 * D), final_norm.reshape(2 * width)])
    small = jnp.pad(small[None], ((0, 15), (0, 4 * D - small.shape[0])))
    near_pieces = gather_start(
        places,
        jnp.concatenate([lax.dynamic_slice(own, (core * rows, 0), (rows, 4 * D)), small], axis=0),
        *pieces,
    )
    near = gather_finish(places, near_pieces)
    stream = jnp.concatenate(in_order([piece[0] for piece in pieces], places.mine), axis=1)
    one, two, three = (piece[rows] for piece in near_pieces)
    table = in_order(
        (
            small[0], jnp.where(places.turned == 0, one, two), jnp.where(places.turned == 0, two, one),
            three,
        ),
        section,
    )
    norms = jnp.stack(table).astype(F32)
    queries, own_kv = project(places, stream, own, near, 0)
    far_kv = places.swap_core(own_kv)
    late_pieces = gather_start(
        places, lax.dynamic_slice(own, (core * rows, 4 * D), (rows, 2 * D)), queries
    )

    *segs, live = sequences(places, seq_lengths)
    qseg = segs[0]
    both = token_pieces(places, jnp.stack([accum_input, out_cotangent]))

    kept = attend(places, stream, queries, own_kv, far_kv, segs, own, near, norms, 0)
    late = gather_finish(places, [late_pieces[0], gate(late_pieces[1], kept[0]), gate(late_pieces[2], kept[0])])
    sum_f, branch_sum, turning, queries_two, own_kv_two = feed(
        places, stream, kept[3], kept[2], own, near, late, norms, 1
    )
    far_kv_two = places.swap_core(own_kv_two)
    context, lse, middle, sum_a = attend(
        places, turning, queries_two, own_kv_two, far_kv_two, segs, own, near, norms, 2
    )
    (
        result, dy_low, dy, final_grad, dz, dctx, delta, grads, keep_f, give_f, rest,
    ) = turn(
        places, middle, turning, sum_a, context, own, near, late, norms, branch_sum, both, live
    )

    reduction = Reduction(places)
    zero = jnp.zeros((HALF, D), F32)

    def scores(queries, own_kv, far_kv, dctx, lse, delta):
        dq, dkv_far = scores_back(queries, far_kv, dctx, qseg, segs[2], lse, delta, zero, BF)
        from_far = places.swap_core(dkv_far)
        dq, dkv = scores_back(queries, own_kv, dctx, qseg, segs[1], lse, delta, dq, BF)
        return dq, dkv, from_far

    third = reduction.cores(keep_f, give_f)
    dq, dkv, from_far = scores(queries_two, own_kv_two, far_kv_two, dctx, lse, delta)
    dz, dctx, delta, grads_first, keep_p, give_p, keep_f, give_f, rest = between(
        places, turning, dq, dkv, from_far, dz, dy, grads, final_grad, rest, (*kept, sum_f), own,
        near, late, norms,
    )
    reduction.send_early(reduction.cores(keep_f, give_f), reduction.cores(keep_p, give_p), third)
    dq, dkv, from_far = scores(queries, own_kv, far_kv, dctx, kept[1], delta)
    upstream, keep, *give = project_back(
        places, stream, dq, dkv, from_far, dz, own, near, 0, grads_first, final_grad, rest
    )
    swapped = places.swap_core(give[0]), places.swap_core(gate(give[1], *reduction.early))
    blocks = reduction.plane((keep, swapped))
    leaving = tokens_out(places, (upstream, result, dy_low), blocks[0])
    reduced, early = zip(*(reduction.depth(part, leaving[0]) for part in blocks), strict=True)
    reduced = jnp.concatenate(reduced, axis=0)
    shared = reduction.shared(reduced[places.blk :])
    stream_out, result_out, accum_out = tokens_placed(places, leaving, (F32, BF, F32), early[1])
    slab = reduced[: places.blk].T
    cut = D // places.ndp
    norm_out = lax.dynamic_slice(reduced, (places.blk, places.dp * cut), (2, cut))
    final_out = lax.dynamic_slice(shared, (2, section * width), (2, width))

    return (
        result_out,
        stream_out,
        accum_out,
        slab[None],
        norm_out[None],
        final_out,
    )


def solution(mesh):
    placed = (
        P("dp", "section"),
        P("dp", "section"),
        P("section", None, None),
        P("section", None, None),
        P(None, "section"),
        P("dp", None),
        P("dp", "section"),
    )
    return jax.shard_map(
        on_device,
        mesh=mesh,
        in_specs=placed,
        out_specs=(
            P("dp", "section"),
            P("dp", "section"),
            P("dp", "section"),
            P("section", None, "dp"),
            P("section", None, "dp"),
            P(None, "section"),
        ),
        check_vma=False,
    )
```

```python
import functools
import math

import jax
import jax.numpy as jnp
from jax import lax
from jax.experimental import pallas as pl
from jax.experimental.pallas import tpu as pltpu
from jax.sharding import PartitionSpec as P

D = 512
HEADS = 8
HEAD = 64
PACK = 1024
HALF = PACK // 2
PAIRS = HEADS // 2
LANES = 2 * HEAD
SECTIONS = 4
FAR = 1e30
SCALE = HEAD ** (-0.5)
BF = jnp.bfloat16
F32 = jnp.float32
NT = (((1,), (1,)), ((), ()))
TN = (((0,), (0,)), ((), ()))


def mm(left, right):
    return jnp.dot(left, right, preferred_element_type=F32)


def mm_nt(left, right):
    return lax.dot_general(left, right, NT, preferred_element_type=F32)


def mm_tn(left, right):
    return lax.dot_general(left, right, TN, preferred_element_type=F32)


def params(megabytes=16):
    return pltpu.CompilerParams(
        dimension_semantics=("arbitrary",), vmem_limit_bytes=megabytes * 1024 * 1024
    )


def shaped(rows, cols, dtype):
    return jax.ShapeDtypeStruct((rows, cols), dtype)


def in_hbm(array):
    return pltpu.with_memory_space_constraint(array, pltpu.HBM)


def whole(rows, cols):
    return pl.BlockSpec((rows, cols), lambda i: (0, 0))


SCALAR = pl.BlockSpec(memory_space=pltpu.SMEM)


def cost(flops, moved, transcendentals=0):
    return pl.CostEstimate(
        flops=int(flops), bytes_accessed=int(moved), transcendentals=int(transcendentals)
    )


def gain_of(table_ref, layer):
    return table_ref[layer : layer + 1, :D]


def shift_of(table_ref, layer):
    return table_ref[layer : layer + 1, D : 2 * D]


def norm_parts(summed):
    average = jnp.mean(summed, axis=-1, keepdims=True)
    centered = summed - average
    spread = jnp.mean(centered * centered, axis=-1, keepdims=True)
    inverse = lax.rsqrt(spread + 1e-05)
    return centered * inverse, inverse


def norm_forward(summed, table_ref, layer):
    normal, _ = norm_parts(summed)
    return normal * gain_of(table_ref, layer) + shift_of(table_ref, layer)


def norm_back(summed, gain, upstream):
    normal, inverse = norm_parts(summed)
    scaled = upstream * gain
    mean_one = jnp.mean(scaled, axis=-1, keepdims=True)
    mean_two = jnp.mean(scaled * normal, axis=-1, keepdims=True)
    grad = (scaled - mean_one - normal * mean_two) * inverse
    gain_grad = jnp.sum(upstream * normal, axis=0, keepdims=True)
    shift_grad = jnp.sum(upstream, axis=0, keepdims=True)
    return grad, gain_grad, shift_grad


def head_mask(which):
    lane = lax.broadcasted_iota(jnp.int32, (1, LANES), 1)
    return (lane // HEAD) == which


def three_way(column):
    high = column.astype(BF)
    rest = column - high.astype(F32)
    middle = rest.astype(BF)
    low = (rest - middle.astype(F32)).astype(BF)
    return high, middle, low


GROUP = 6


def fetch(where_ref, layer, own_ref, piece_refs, own_first, first, width, target, sem):
    section, core, turned = where_ref[0], where_ref[1], where_ref[3]
    half = D // 2
    step = section ^ layer
    mine_rows = pl.ds(pl.multiple_of(core * half, half), half)
    far_rows = pl.ds(pl.multiple_of((1 - core) * half, half), half)

    @pl.when(step == 0)
    def _():
        pltpu.make_async_copy(own_ref.at[:, pl.ds(own_first, width)], target, sem).start()

    for number, (partner, far_number) in enumerate(((1 + turned, 1), (2 - turned, 0), (3, 2))):

        @pl.when(step == partner)
        def _():
            part = (pl.ds(0, half), pl.ds(first, width))
            mine, far = piece_refs[number].at[part], piece_refs[3 + far_number].at[part]
            pltpu.make_async_copy(mine, target.at[mine_rows], sem).start()
            pltpu.make_async_copy(far, target.at[far_rows], sem).start()


def arrived(own_ref, width, target, sem):
    pltpu.make_async_copy(own_ref.at[:, pl.ds(0, width)], target, sem).wait()


def weight_specs(groups):
    return [pl.BlockSpec(memory_space=pl.ANY)] * (1 + GROUP * groups)


def column_of(pair):
    return pl.ds(pl.multiple_of(pair * LANES, LANES), LANES)


def fetch_projection(layer, where_ref, own_ref, near, weight_ref, sems):
    for part in range(3):
        fetch(
            where_ref, layer, own_ref, near, part * D, part * D, D, weight_ref.at[part],
            sems.at[part],
        )


def fetch_outward(layer, where_ref, own_ref, near, weight_ref, sem):
    fetch(where_ref, layer, own_ref, near, 3 * D, 3 * D, D, weight_ref, sem)


def fetch_feed(layer, where_ref, own_ref, near, late, weight_ref, sems):
    for chunk in range(4):
        turn = chunk % 2
        if chunk < 2:
            inner = (layer - 1, late, (4 + turn) * D, turn * D)
            outer = (layer, near, (2 + turn) * D, (2 + turn) * D)
        else:
            inner = (layer, near, turn * D, turn * D)
            outer = (layer, late, (4 + turn) * D, turn * D)
        for number, (whose, pieces, own_first, first) in enumerate((inner, outer)):
            fetch(
                where_ref, whose, own_ref, pieces, own_first, first, D,
                weight_ref.at[chunk, number], sems.at[chunk, number],
            )


PROJECTION = [pltpu.VMEM((3, D, D), BF), pltpu.SemaphoreType.DMA((3,))]
OUTWARD = [pltpu.VMEM((D, D), BF), pltpu.SemaphoreType.DMA]
FEED = [pltpu.VMEM((4, 2, D, D), BF), pltpu.SemaphoreType.DMA((4, 2))]


def put_projection(own_ref, x, q_ref, kv_ref, weight_ref, sems):
    def times(part):
        arrived(own_ref, D, weight_ref.at[part], sems.at[part])
        return mm(x, weight_ref[part]).astype(BF)

    q_ref[...] = times(0)
    keys, values = times(1), times(2)
    for pair in range(PAIRS):
        lanes = slice(pair * LANES, (pair + 1) * LANES)
        kv_ref[pair, :, :LANES] = keys[:, lanes]
        kv_ref[pair, :, LANES:] = values[:, lanes]


def put_attention(q_ref, own_ref, far_ref, qs_ref, kso_ref, ksx_ref, ctx_ref, lse_ref):
    none = jnp.zeros((), BF)
    lane = lax.broadcasted_iota(jnp.int32, (1, LANES), 1)
    ones = jnp.ones((HALF, LANES), BF)
    lse_ref[...] = jnp.zeros((HALF, LANES), F32)

    @pl.loop(0, PAIRS)
    def _(pair):
        q = q_ref[:, column_of(pair)] * jnp.asarray(SCALE, BF)
        keys_own = jnp.concatenate([own_ref[pair, :, :LANES], kso_ref[...]], axis=1)
        keys_other = jnp.concatenate([far_ref[pair, :, :LANES], ksx_ref[...]], axis=1)
        values_own, values_other = own_ref[pair, :, LANES:], far_ref[pair, :, LANES:]
        context = jnp.zeros((HALF, LANES), F32)
        logs = lse_ref[...]
        for which in range(2):
            mask = head_mask(which)
            query = jnp.concatenate([jnp.where(mask, q, none), qs_ref[...]], axis=1)
            score_own = mm_nt(query, keys_own)
            score_other = mm_nt(query, keys_other)
            peak = jnp.maximum(
                jnp.max(score_own, axis=1, keepdims=True),
                jnp.max(score_other, axis=1, keepdims=True),
            )
            own = jnp.exp(score_own - peak).astype(BF)
            other = jnp.exp(score_other - peak).astype(BF)
            total = mm(
                own, jnp.concatenate([jnp.where(mask, values_own, none), ones], axis=1)
            ) + mm(other, jnp.concatenate([jnp.where(mask, values_other, none), ones], axis=1))
            row_total = total[:, LANES:]
            context = context + total[:, :LANES] / row_total
            logs = jnp.where(lane == 2 * pair + which, peak + jnp.log(row_total), logs)
        lse_ref[...] = logs
        ctx_ref[:, column_of(pair)] = context.astype(BF)


def gelu_parts(v):
    root = 0.7978845608028654
    squared = v * v
    inner = root * (v + 0.044715 * v * squared)
    t = jnp.tanh(inner)
    hidden = 0.5 * v * (1.0 + t)
    slope = 0.5 * (1.0 + t) + 0.5 * v * (1.0 - t * t) * (root * (1.0 + 3 * 0.044715 * squared))
    return hidden, slope


def feed_weight(own_ref, weight_ref, sems, chunk, number):
    arrived(own_ref, D, weight_ref.at[chunk, number], sems.at[chunk, number])
    return weight_ref[chunk, number]


def half_of(refs, place):
    if not isinstance(refs, tuple):
        return refs, place
    half = refs[0].shape[0]
    return refs[place // half], place % half


def split_rows(core, blk, row, value, keep_ref, give_ref):
    step = math.gcd(D, blk)
    for k in range(value.shape[0] // step):
        part = value[k * step : (k + 1) * step]
        first = row + k * step
        block, offset = first // blk, first % blk

        @pl.when(block % 2 == core)
        def _():
            keep_ref[block // 2, offset : offset + step, :] = part

        @pl.when(block % 2 != core)
        def _():
            ref, place = half_of(give_ref, block // 2)
            ref[place, offset : offset + step, :] = part


def side_rows(grads, final_grads, keep_ref, give_ref):
    extra = jnp.concatenate([grads, final_grads, jnp.zeros((12, D), F32)], axis=0).astype(BF)
    blk = keep_ref.shape[1] - 16
    for block in range(keep_ref.shape[0]):
        keep_ref[block, blk:, :] = extra
        ref, place = half_of(give_ref, block)
        ref[place, blk:, :] = extra


def split_shapes(count, blk):
    return [full(count, blk + 16, D)] * 2, [pltpu.HBM((count, blk + 16, D), BF)] * 2


def put_outward_back(
    summed, upstream, dy, context, gain, weight_of, dctx_ref, delta_ref, grad_ref, rest_ref
):
    grad, gain_grad, shift_grad = norm_back(summed, gain, upstream)
    grad_ref[...] = jnp.concatenate([gain_grad, shift_grad], axis=0)
    df = (grad + dy).astype(BF)
    rest_ref[:D] = mm_tn(df, context).astype(BF)
    context_grad = mm_nt(df, weight_of()).astype(BF)
    dctx_ref[...] = context_grad
    product = context.astype(F32) * context_grad.astype(F32)
    lane = lax.broadcasted_iota(jnp.int32, (1, LANES), 1)
    delta = jnp.zeros((HALF, LANES), F32)
    for head in range(HEADS):
        part = product[:, (head // 2) * LANES : (head // 2 + 1) * LANES]
        inner = jnp.sum(jnp.where(head_mask(head % 2), part, 0.0), axis=1, keepdims=True)
        delta = jnp.where(lane == head, inner, delta)
    delta_ref[...] = delta
    return grad


def put_feed_back(
    core, x, hidden_of, df, grad, weight_of, rest_ref, keep_ref, give_ref
):
    blk = keep_ref.shape[1] - 16
    total = grad
    for chunk in range(4):
        inner, outer = weight_of(chunk, 0), weight_of(chunk, 1)
        hidden, slope = hidden_of(chunk, inner)
        split_rows(core, blk, (2 + chunk) * D, mm_tn(hidden, df).astype(BF), keep_ref, give_ref)
        preact_grad = (mm(df, outer) * slope).astype(BF)
        inner_grad = mm_tn(preact_grad, x).astype(BF)
        if chunk < 2:
            rest_ref[(1 + chunk) * D : (2 + chunk) * D] = inner_grad
        else:
            split_rows(core, blk, (chunk - 2) * D, inner_grad, keep_ref, give_ref)
        total = total + mm_nt(preact_grad, inner)
    return total


def put_project_back(
    core, x, dq_ref, dkv_ref, far_ref, dz, grads, final_grads, rest_ref, weight_of, keep_ref,
    give_ref,
):
    blk = keep_ref.shape[1] - 16
    side_rows(grads, final_grads, keep_ref, give_ref)
    split_rows(core, blk, 3 * D, rest_ref[...], keep_ref, give_ref)
    parts = [(dkv_ref[k].astype(F32) + far_ref[k].astype(F32)).astype(BF) for k in range(PAIRS)]
    dk = jnp.concatenate([part[:, :LANES] for part in parts], axis=1)
    dv = jnp.concatenate([part[:, LANES:] for part in parts], axis=1)
    total = dz
    for place, grad in enumerate((dq_ref[...].astype(BF), dk, dv)):
        split_rows(core, blk, place * D, mm_tn(grad, x).astype(BF), keep_ref, give_ref)
        total = total + mm_nt(grad, weight_of(place))
    return total


def full(*shape):
    return pl.BlockSpec(shape, lambda i: (0,) * len(shape), pipeline_mode=pl.Buffered(1))


KV = (PAIRS, HALF, 2 * LANES)
TABLE = (SECTIONS, 4 * D)


def project_kernel(layer, where_ref, x_ref, own_ref, *refs):
    near, (q_ref, kv_ref, weight_ref, sems) = refs[:GROUP], refs[GROUP:]
    fetch_projection(layer, where_ref, own_ref, near, weight_ref, sems)
    put_projection(own_ref, x_ref[...], q_ref, kv_ref, weight_ref, sems)


def project(places, stream, own, near, layer):
    return pl.pallas_call(
        functools.partial(project_kernel, layer),
        grid=(1,),
        in_specs=[SCALAR, full(HALF, D), *weight_specs(1)],
        out_specs=[full(HALF, D), full(*KV)],
        out_shape=[shaped(HALF, D, BF), jax.ShapeDtypeStruct(KV, BF)],
        scratch_shapes=PROJECTION,
        compiler_params=params(),
        cost_estimate=cost(2 * HALF * D * 3 * D, 4e6),
        name="project",
    )(places.where, stream, *map(in_hbm, (own, *near)))


def feed_kernel(layer, where_ref, x_ref, sum_ref, middle_ref, norm_ref, own_ref, *refs):
    near, late, refs = refs[:GROUP], refs[GROUP : 2 * GROUP], refs[2 * GROUP :]
    (
        sum_f_ref, branch_ref, next_ref, q_next_ref, kv_next_ref, feed_ref, feed_sems,
        project_ref, project_sems,
    ) = refs
    fetch_feed(layer, where_ref, own_ref, near, late, feed_ref, feed_sems)
    fetch_projection(layer + 1, where_ref, own_ref, near, project_ref, project_sems)
    middle = middle_ref[...]
    total = jnp.zeros((HALF, D), F32)
    for chunk in range(4):
        inner = feed_weight(own_ref, feed_ref, feed_sems, chunk, 0)
        hidden = gelu_parts(mm(middle, inner))[0].astype(BF)
        total = total + mm_nt(hidden, feed_weight(own_ref, feed_ref, feed_sems, chunk, 1))
    summed = middle.astype(F32) + total
    sum_f_ref[...] = summed
    branch_ref[...] = sum_ref[...] - x_ref[...].astype(F32) + total
    following = norm_forward(summed, norm_ref, layer).astype(BF)
    next_ref[...] = following
    put_projection(own_ref, following, q_next_ref, kv_next_ref, project_ref, project_sems)


def feed(places, stream, sum_a, middle, own, near, late, norms, layer):
    return pl.pallas_call(
        functools.partial(feed_kernel, layer),
        grid=(1,),
        in_specs=[SCALAR, *[full(HALF, D)] * 3, full(*TABLE), *weight_specs(2)],
        out_specs=[*[full(HALF, D)] * 4, full(*KV)],
        out_shape=[
            shaped(HALF, D, F32), shaped(HALF, D, F32), shaped(HALF, D, BF), shaped(HALF, D, BF),
            jax.ShapeDtypeStruct(KV, BF),
        ],
        scratch_shapes=[*FEED, *PROJECTION],
        compiler_params=params(18),
        cost_estimate=cost(6e9, 14e6, 1e6),
        name="feed",
    )(places.where, *map(in_hbm, (stream, sum_a, middle)), norms, *map(in_hbm, (own, *near, *late)))


def attend_kernel(
    layer, where_ref, q_ref, own_kv_ref, far_kv_ref, qs_ref, kso_ref, ksx_ref, x_ref, norm_ref,
    own_ref, *refs,
):
    near, refs = refs[:GROUP], refs[GROUP:]
    ctx_ref, lse_ref, middle_ref, sum_ref, outward_ref, outward_sem = refs
    fetch_outward(layer, where_ref, own_ref, near, outward_ref, outward_sem)
    put_attention(
        q_ref, own_kv_ref, far_kv_ref, qs_ref, kso_ref, ksx_ref, ctx_ref, lse_ref
    )
    arrived(own_ref, D, outward_ref, outward_sem)
    summed = x_ref[...].astype(F32) + mm(ctx_ref[...], outward_ref[...])
    sum_ref[...] = summed
    middle_ref[...] = norm_forward(summed, norm_ref, layer).astype(BF)


def attend(places, stream, queries, own_kv, far_kv, segs, own, near, norms, layer):
    kind = jax.ShapeDtypeStruct if layer else pltpu.HBM
    return pl.pallas_call(
        functools.partial(attend_kernel, layer),
        grid=(1,),
        in_specs=[
            SCALAR, full(HALF, D), full(*KV), full(*KV), *[full(HALF, LANES)] * 3, full(HALF, D),
            full(*TABLE), *weight_specs(1),
        ],
        out_specs=[full(HALF, D), full(HALF, LANES), full(HALF, D), full(HALF, D)],
        out_shape=[
            kind((HALF, D), BF), kind((HALF, LANES), F32), kind((HALF, D), BF),
            kind((HALF, D), F32),
        ],
        scratch_shapes=OUTWARD,
        compiler_params=params(),
        cost_estimate=cost(9e9, 10e6, 4e6),
        name="attend",
    )(places.where, queries, own_kv, far_kv, *segs, stream, norms, *map(in_hbm, (own, *near)))


def turn_kernel(
    layer, where_ref, middle_ref, x_ref, sum_ref, ctx_ref, norm_ref, branch_ref,
    a_ref, b_ref, c_ref, d_ref, live_ref, own_ref, *refs,
):
    near, late, refs = refs[:GROUP], refs[GROUP : 2 * GROUP], refs[2 * GROUP :]
    (
        result_ref, low_ref, dy_ref, final_ref, dz_ref, dctx_ref, delta_ref, grad_ref,
        feed_keep, feed_give, rest_ref,
        hidden_ref, slope_ref, outward_ref, outward_sem, feed_ref, feed_sems,
    ) = refs
    core, mine = where_ref[1], where_ref[2]
    fetch_feed(layer + 1, where_ref, own_ref, near, late, feed_ref, feed_sems)
    fetch_outward(layer, where_ref, own_ref, near, outward_ref, outward_sem)
    middle, sum_a = middle_ref[...], sum_ref[...]
    branch = sum_a - x_ref[...].astype(F32)
    total = jnp.zeros((HALF, D), F32)
    for chunk in range(4):
        inner = feed_weight(own_ref, feed_ref, feed_sems, chunk, 0)
        hidden, slope = gelu_parts(mm(middle, inner))
        hidden = hidden.astype(BF)
        hidden_ref[chunk] = hidden
        slope_ref[chunk] = slope
        total = total + mm_nt(hidden, feed_weight(own_ref, feed_ref, feed_sems, chunk, 1))
    sum_f = middle.astype(F32) + total
    last = norm_forward(sum_f, norm_ref, layer + 1)

    pieces = in_order([ref[...] for ref in (a_ref, b_ref, c_ref, d_ref)], mine)
    accum, cot = (jnp.concatenate([piece[k] for piece in pieces], axis=1) for k in range(2))
    summed = accum.astype(F32) + (branch_ref[...] + (branch + total))
    normal, _ = norm_parts(summed)
    width = D // SECTIONS
    gain, shift = (
        jnp.concatenate(
            [
                norm_ref[k : k + 1, 2 * D + part * width : 2 * D + (part + 1) * width]
                for k in range(SECTIONS)
            ],
            axis=1,
        )
        for part in range(2)
    )
    result_ref[...] = (last + normal * gain + shift).astype(BF)
    cot = cot.astype(F32) * live_ref[:, 0:1]
    dy, gain_grad, shift_grad = norm_back(summed, gain, cot)
    dy_ref[...] = dy
    low_ref[...] = dy.astype(BF)
    final_grads = jnp.concatenate([gain_grad, shift_grad], axis=0)
    final_ref[...] = final_grads

    grad, gain_grad, shift_grad = norm_back(sum_f, gain_of(norm_ref, layer + 1), cot)
    side_rows(
        jnp.concatenate([gain_grad, shift_grad], axis=0), final_grads, feed_keep, feed_give
    )
    upstream = put_feed_back(
        core, middle, lambda chunk, inner: (hidden_ref[chunk], slope_ref[chunk]),
        (grad + dy).astype(BF), grad, lambda chunk, number: feed_ref[chunk, number],
        rest_ref, feed_keep, feed_give,
    )
    arrived(own_ref, D, outward_ref, outward_sem)
    dz_ref[...] = put_outward_back(
        sum_a, upstream.astype(BF).astype(F32), dy, ctx_ref[...], gain_of(norm_ref, layer),
        lambda: outward_ref[...], dctx_ref, delta_ref, grad_ref, rest_ref,
    )


def turn(places, middle, stream, sum_a, context, own, near, late, norms, branch_sum, pieces, live):
    specs, shapes = split_shapes(places.ndp // 2, places.blk)
    return pl.pallas_call(
        functools.partial(turn_kernel, 2),
        grid=(1,),
        in_specs=[
            SCALAR, *[full(HALF, D)] * 4, full(*TABLE), full(HALF, D),
            *[full(2, HALF, D // SECTIONS)] * 4, full(HALF, LANES), *weight_specs(2),
        ],
        out_specs=[
            *[full(HALF, D)] * 3, full(2, D), full(HALF, D), full(HALF, D),
            full(HALF, LANES), full(2, D), *specs, full(3 * D, D),
        ],
        out_shape=[
            shaped(HALF, D, BF), shaped(HALF, D, BF),
            shaped(HALF, D, F32), shaped(2, D, F32), shaped(HALF, D, F32), shaped(HALF, D, BF),
            shaped(HALF, LANES, F32), shaped(2, D, F32), *shapes, shaped(3 * D, D, BF),
        ],
        scratch_shapes=[
            pltpu.VMEM((4, HALF, D), BF), pltpu.VMEM((4, HALF, D), F32), *OUTWARD, *FEED,
        ],
        compiler_params=params(28),
        cost_estimate=cost(16e9, 30e6, 2e6),
        name="turn",
    )(
        places.where, middle, stream, sum_a, context, norms, branch_sum, *pieces, live, *map(in_hbm, (own, *near, *late)),
    )


def column():
    return pl.BlockSpec((HALF, LANES), lambda i: (0, i))


def pair_block():
    return pl.BlockSpec((1, HALF, 2 * LANES), lambda i: (i, 0, 0))


def scores_back_kernel(
    q_ref, kv_ref, dctx_ref, qs_ref, ks_ref, lse_ref, delta_ref, before_ref, dq_ref, dkv_ref
):
    pair = pl.program_id(0)
    none = jnp.zeros((), BF)
    lane = lax.broadcasted_iota(jnp.int32, (1, LANES), 1)
    q = q_ref[...] * jnp.asarray(SCALE, BF)
    k = kv_ref[0, :, :LANES]
    k_scaled = k * jnp.asarray(SCALE, BF)
    dctx = dctx_ref[...]
    extra = jnp.where((lane >= LANES - 3), jnp.ones((), BF), none)
    keys = jnp.concatenate([k, ks_ref[...] + extra], axis=1)
    values = jnp.concatenate(
        [kv_ref[0, :, LANES:], jnp.broadcast_to(extra, (HALF, LANES))], axis=1
    )
    dq = before_ref[...]
    dk = jnp.zeros((HALF, LANES), F32)
    dv = jnp.zeros((HALF, LANES), F32)
    for which in range(2):
        mask = head_mask(which)
        here = lane == 2 * pair + which

        def lanes_of(table, base):
            column = -jnp.sum(jnp.where(here, table, 0.0), axis=1, keepdims=True)
            high, middle, low = three_way(column)
            base = jnp.where(lane == LANES - 3, high, base)
            base = jnp.where(lane == LANES - 2, middle, base)
            return jnp.where(lane == LANES - 1, low, base)

        query_part = jnp.where(mask, q, none)
        dctx_part = jnp.where(mask, dctx, none)
        query = jnp.concatenate([query_part, lanes_of(lse_ref[...], qs_ref[...])], axis=1)
        dcontext = jnp.concatenate(
            [dctx_part, lanes_of(delta_ref[...], jnp.zeros((HALF, LANES), BF))], axis=1
        )
        probability = jnp.exp(mm_nt(keys, query))
        score_grad = (probability * mm_nt(values, dcontext)).astype(BF)
        dv = dv + mm(probability.astype(BF), dctx_part)
        dk = dk + mm(score_grad, query_part)
        dq = dq + mm_tn(score_grad, jnp.where(mask, k_scaled, none))
    dq_ref[...] = dq
    dkv_ref[0, :, :LANES] = dk.astype(dkv_ref.dtype)
    dkv_ref[0, :, LANES:] = dv.astype(dkv_ref.dtype)


def scores_back(queries, kv, dctx, qseg, kseg, lse, delta, before, out_type):
    return pl.pallas_call(
        scores_back_kernel,
        grid=(PAIRS,),
        in_specs=[
            column(), pair_block(), column(),
            whole(HALF, LANES), whole(HALF, LANES), whole(HALF, LANES), whole(HALF, LANES),
            column(),
        ],
        out_specs=[column(), pair_block()],
        out_shape=[
            shaped(HALF, D, F32), jax.ShapeDtypeStruct((PAIRS, HALF, 2 * LANES), out_type),
        ],
        compiler_params=params(),
        cost_estimate=cost(8e9, 8e6, 2e6),
        name="scores_back",
    )(queries, kv, dctx, qseg, kseg, lse, delta, before)


def middle_kernel(
    layer, where_ref, x_ref, dq_ref, dkv_ref, far_ref, dz_ref, dy_ref, grad_ref, final_ref,
    before_ref, middle_ref, sum_f_ref, sum_a_ref, ctx_ref, norm_ref, own_ref, *refs,
):
    near, late, refs = refs[:GROUP], refs[GROUP : 2 * GROUP], refs[2 * GROUP :]
    (
        dz_out, dctx_ref, delta_ref, grad_out, project_keep, project_give, feed_keep, feed_give,
        rest_ref,
        project_ref, project_sems, feed_ref, feed_sems, outward_ref, outward_sem,
    ) = refs
    core = where_ref[1]
    fetch_projection(layer, where_ref, own_ref, near, project_ref, project_sems)
    fetch_feed(layer - 1, where_ref, own_ref, near, late, feed_ref, feed_sems)
    fetch_outward(layer - 2, where_ref, own_ref, near, outward_ref, outward_sem)
    final_grads = final_ref[...]

    def project_weight(place):
        arrived(own_ref, D, project_ref.at[place], project_sems.at[place])
        return project_ref[place]

    def outward_weight():
        arrived(own_ref, D, outward_ref, outward_sem)
        return outward_ref[...]

    upstream = put_project_back(
        core, x_ref[...], dq_ref, dkv_ref, far_ref, dz_ref[...], grad_ref[...], final_grads,
        before_ref, project_weight, project_keep, project_give,
    ).astype(BF).astype(F32)
    dy = dy_ref[...]
    grad, gain_grad, shift_grad = norm_back(
        sum_f_ref[...], gain_of(norm_ref, layer - 1), upstream
    )
    side_rows(
        jnp.concatenate([gain_grad, shift_grad], axis=0), final_grads, feed_keep, feed_give
    )
    middle = middle_ref[...]

    def hidden_of(chunk, inner):
        hidden, slope = gelu_parts(mm(middle, inner))
        return hidden.astype(BF), slope

    upstream = put_feed_back(
        core, middle, hidden_of, (grad + dy).astype(BF), grad,
        functools.partial(feed_weight, own_ref, feed_ref, feed_sems), rest_ref, feed_keep, feed_give,
    ).astype(BF).astype(F32)
    dz_out[...] = put_outward_back(
        sum_a_ref[...], upstream, dy, ctx_ref[...], gain_of(norm_ref, layer - 2),
        outward_weight, dctx_ref, delta_ref, grad_out, rest_ref,
    )


def between(
    places, stream, dq, dkv, far, dz, dy, grads, final_grads, rest, kept, own, near, late, norms
):
    context, _, middle, sum_a, sum_f = kept
    specs, shapes = split_shapes(places.ndp // 2, places.blk)
    return pl.pallas_call(
        functools.partial(middle_kernel, 2),
        grid=(1,),
        in_specs=[
            SCALAR, full(HALF, D), full(HALF, D), full(*KV), full(*KV), full(HALF, D),
            full(HALF, D), full(2, D), full(2, D), full(3 * D, D), *[full(HALF, D)] * 4,
            full(*TABLE), *weight_specs(2),
        ],
        out_specs=[
            full(HALF, D), full(HALF, D), full(HALF, LANES), full(2, D), *specs, *specs,
            full(3 * D, D),
        ],
        out_shape=[
            shaped(HALF, D, F32), shaped(HALF, D, BF), shaped(HALF, LANES, F32),
            shaped(2, D, F32), *shapes, *shapes, shaped(3 * D, D, BF),
        ],
        scratch_shapes=[*PROJECTION, *FEED, *OUTWARD],
        compiler_params=params(28),
        cost_estimate=cost(20e9, 30e6, 2e6),
        name="between",
    )(
        places.where, stream, dq, dkv, far, dz, dy, grads, final_grads, rest, middle, sum_f,
        sum_a, context, norms, *map(in_hbm, (own, *near, *late)),
    )


def project_back_kernel(
    layer, where_ref, x_ref, dq_ref, dkv_ref, far_ref, dz_ref, grad_ref, final_ref, rest_ref,
    own_ref, *refs,
):
    near, (dx_ref, keep_ref, *give, weight_ref, sems) = refs[:GROUP], refs[GROUP:]
    fetch_projection(layer, where_ref, own_ref, near, weight_ref, sems)

    def weight_of(place):
        arrived(own_ref, D, weight_ref.at[place], sems.at[place])
        return weight_ref[place]

    dx_ref[...] = put_project_back(
        where_ref[1], x_ref[...], dq_ref, dkv_ref, far_ref, dz_ref[...], grad_ref[...],
        final_ref[...], rest_ref, weight_of, keep_ref, tuple(give),
    ).astype(BF)


def project_back(places, stream, dq, dkv, far, dz, own, near, layer, grads, final_grads, rest):
    specs, shapes = split_shapes(places.ndp // 2, places.blk)
    half_specs, half_shapes = split_shapes(places.ndp // 4, places.blk)
    return pl.pallas_call(
        functools.partial(project_back_kernel, layer),
        grid=(1,),
        in_specs=[
            SCALAR, full(HALF, D), full(HALF, D), full(*KV), full(*KV), full(HALF, D),
            full(2, D), full(2, D), full(3 * D, D), *weight_specs(1),
        ],
        out_specs=[full(HALF, D), specs[0], *half_specs],
        out_shape=[shaped(HALF, D, BF), shapes[0], *half_shapes],
        scratch_shapes=PROJECTION,
        compiler_params=params(20),
        cost_estimate=cost(4 * HALF * D * 3 * D, 10e6),
        name="project_back",
    )(places.where, stream, dq, dkv, far, dz, grads, final_grads, rest, *map(in_hbm, (own, *near)))


class Places:
    def __init__(self):
        self.ndp = lax.axis_size("dp")
        self.section = lax.axis_index("section")
        self.dp = lax.axis_index("dp")
        self.core = self.dp % 2
        self.blk = 6 * D // self.ndp
        self.mine = 2 * (self.section % 2) + self.core
        self.turned = (self.dp + self.dp // 2) % 2
        self.where = jnp.stack([self.section, self.core, self.mine, self.turned]).astype(jnp.int32)
        bits = (self.section % 2 == 1, self.section // 2 == 1)
        self.is_first = self.core == 0
        self.first_bit = jnp.where(self.is_first, bits[0], bits[1])
        self.second_bit = jnp.where(self.is_first, bits[1], bits[0])

    def swap_dp(self, block, step):
        return lax.ppermute(block, "dp", [(i, i ^ step) for i in range(self.ndp)])

    def swap_core(self, block):
        return self.swap_dp(block, 1)

    def swap_plane(self, block, turn):
        return self.send(block, lambda s, d: (s ^ (1 + (d + turn) % 2), d))

    def swap_turned(self, block, turn):
        return self.send(block, lambda s, d: (s ^ (1 + (d + d // 2 + turn) % 2), d))

    def send(self, block, route):
        pairs = []
        for s in range(SECTIONS):
            for d in range(self.ndp):
                to = route(s, d)
                pairs.append((s * self.ndp + d, to[0] * self.ndp + to[1]))
        return lax.ppermute(block, ("section", "dp"), pairs)


def pick(stack, index):
    return lax.dynamic_index_in_dim(stack, index, 0, keepdims=False)


ANYWHERE = pl.BlockSpec(memory_space=pl.ANY)


def sequence_kernel(where_ref, own_ref, far_ref, qseg_ref, own_seg_ref, far_seg_ref, live_ref):
    section, core = where_ref[0], where_ref[1]
    here = core == section // 2
    row = section % 2
    lane = lax.broadcasted_iota(jnp.int32, (HALF, LANES), 1)
    spot = lax.broadcasted_iota(jnp.int32, (HALF, LANES), 0)
    own = jnp.zeros((HALF, LANES), jnp.int32)
    far = jnp.zeros((HALF, LANES), jnp.int32)
    ending = jnp.int32(0)
    for k in range(own_ref.shape[1]):
        ending = ending + jnp.where(here, own_ref[row, k], far_ref[row, k])
        own = own + (spot + core * HALF >= ending).astype(jnp.int32)
        far = far + (spot + (1 - core) * HALF >= ending).astype(jnp.int32)
    own_seg_ref[...] = jnp.where(own == lane, 1.0, 0.0).astype(BF)
    far_seg_ref[...] = jnp.where(far == lane, 1.0, 0.0).astype(BF)
    qseg_ref[...] = jnp.where((own != lane) & (lane < 32), -FAR, 0.0).astype(BF)
    live_ref[...] = jnp.where(spot + core * HALF < ending, 1.0, 0.0)


def sequences(places, lengths):
    return pl.pallas_call(
        sequence_kernel,
        grid=(1,),
        in_specs=[SCALAR] * 3,
        out_specs=[whole(HALF, LANES)] * 4,
        out_shape=[shaped(HALF, LANES, BF)] * 3 + [shaped(HALF, LANES, F32)],
        compiler_params=params(),
        cost_estimate=cost(1e6, 1e6),
        name="sequences",
    )(places.where, lengths, places.swap_core(lengths))


def gate_kernel(*refs):
    del refs


def gate(value, *earlier):
    return pl.pallas_call(
        gate_kernel,
        in_specs=[ANYWHERE] * (1 + len(earlier)),
        out_specs=ANYWHERE,
        out_shape=jax.ShapeDtypeStruct(value.shape, value.dtype),
        input_output_aliases={0: 0},
        cost_estimate=cost(0, 0),
        name="gate",
    )(value, *earlier)


def token_pieces(places, block):
    several = block.shape[0]
    pieces = jnp.swapaxes(block.reshape(several, 4, HALF, D // SECTIONS), 0, 1)
    got = []
    for turn in range(4):

        def route(s, d, turn=turn):
            piece = s ^ turn
            return 2 * (d % 2) + piece // 2, d - d % 2 + piece % 2

        got.append(places.send(pick(pieces, places.section ^ turn), route))
    return got


def in_order(pieces, mine):
    one, two = mine % 2 == 1, mine // 2 == 1
    a, b, c, d = pieces
    a, b, c, d = (
        jnp.where(one, b, a), jnp.where(one, a, b), jnp.where(one, d, c), jnp.where(one, c, d)
    )
    return (
        jnp.where(two, c, a), jnp.where(two, d, b), jnp.where(two, a, c), jnp.where(two, b, d)
    )


def deal_kernel(mine_ref, a_ref, b_ref, c_ref, later_ref, *out_refs):
    width = D // SECTIONS
    for k, ref in enumerate((a_ref, b_ref, c_ref)):
        rows = ref[...]
        features = [rows[:, f * width : (f + 1) * width] for f in range(SECTIONS)]
        for out_ref, piece in zip(out_refs, in_order(features, mine_ref[0]), strict=True):
            out_ref[k] = piece


def tokens_out(places, rows, later):
    width = D // SECTIONS
    features = pl.pallas_call(
        deal_kernel,
        grid=(1,),
        in_specs=[SCALAR, *[whole(HALF, D)] * 3, pl.BlockSpec(memory_space=pl.ANY)],
        out_specs=[pl.BlockSpec((3, HALF, width), lambda i: (0, 0, 0))] * SECTIONS,
        out_shape=[jax.ShapeDtypeStruct((3, HALF, width), BF)] * SECTIONS,
        compiler_params=params(),
        cost_estimate=cost(0, 4e6),
        name="deal",
    )(places.mine.reshape(1).astype(jnp.int32), *rows, later)
    got = []
    for turn in range(4):

        def route(s, d, turn=turn):
            return (2 * (s % 2) + d % 2) ^ turn, d - d % 2 + s // 2

        got.append(places.send(features[turn], route))
    return got


def undeal_kernel(section_ref, a_ref, b_ref, c_ref, d_ref, later_ref, x_ref, y_ref, z_ref):
    refs = (a_ref, b_ref, c_ref, d_ref)
    for k, out_ref in enumerate((x_ref, y_ref, z_ref)):
        pieces = in_order([ref[k] for ref in refs], section_ref[0])
        for number, piece in enumerate(pieces):
            out_ref[number * HALF : (number + 1) * HALF] = piece.astype(out_ref.dtype)


def tokens_placed(places, pieces, types, later):
    width = D // SECTIONS
    return pl.pallas_call(
        undeal_kernel,
        grid=(1,),
        in_specs=[SCALAR, *[pl.BlockSpec((3, HALF, width), lambda i: (0, 0, 0))] * 4, ANYWHERE],
        out_specs=[whole(4 * HALF, width)] * 3,
        out_shape=[shaped(4 * HALF, width, kind) for kind in types],
        compiler_params=params(),
        cost_estimate=cost(0, 4e6),
        name="undeal",
    )(places.section.reshape(1).astype(jnp.int32), *pieces, later)


def gather_start(places, mine, *earlier):
    one = places.swap_turned(mine, 0)
    if earlier:
        one = gate(one, *earlier)
    return one, places.swap_dp(one, 2), places.swap_turned(one, 1)


def gather_finish(places, pieces):
    return (*pieces, *(places.swap_core(piece) for piece in pieces))


def chosen_kernel(counts, parts, starts, which_ref, *refs):
    total = sum(parts)
    arrays, (out_ref, held_ref, sems) = refs[:total], refs[total:]
    blocks, rows, _ = out_ref.shape

    def copies(number, place):
        first = sum(parts[:number])
        count = blocks // parts[number]
        for k in range(parts[number]):
            source = arrays[first + k].at[:, pl.ds(starts[number], rows)]
            target = held_ref.at[place, pl.ds(k * count, count)]
            yield pltpu.make_async_copy(source, target, sems.at[place])

    first = 0
    for place, count in enumerate(counts):
        for number in range(count):

            @pl.when(which_ref[place] == number)
            def _():
                for copy in copies(first + number, place):
                    copy.start()

        first += count
    for place in range(len(counts)):
        held = held_ref.at[place]
        pltpu.make_async_copy(held, held, sems.at[place]).wait()
    for block in range(out_ref.shape[0]):
        value = held_ref[0, block].astype(F32)
        for place in range(1, len(counts)):
            value = value + held_ref[place, block].astype(F32)
        out_ref[block] = value.astype(BF)


def chosen_sum(which, groups, first, rows):
    entries = [
        array if isinstance(array, tuple) else (array,) for group in groups for array in group
    ]
    arrays = [array for entry in entries for array in entry]
    shape = (sum(array.shape[0] for array in entries[0]), rows, D)
    counts = tuple(len(group) for group in groups)
    parts = tuple(len(entry) for entry in entries)
    starts = tuple(0 if entry[0].shape[1] == rows else first for entry in entries)
    return pl.pallas_call(
        functools.partial(chosen_kernel, counts, parts, starts),
        grid=(1,),
        in_specs=[SCALAR, *[ANYWHERE] * len(arrays)],
        out_specs=full(*shape),
        out_shape=jax.ShapeDtypeStruct(shape, BF),
        scratch_shapes=[
            pltpu.VMEM((len(counts), *shape), BF), pltpu.SemaphoreType.DMA((len(counts),)),
        ],
        compiler_params=params(),
        cost_estimate=cost(1e6, 5e6),
        name="chosen_sum",
    )(
        jnp.stack([w.astype(jnp.int32) for w in which]), *[in_hbm(array) for array in arrays],
    )


class Reduction:
    def __init__(self, places):
        self.places = places
        rows = places.blk + 16
        cut = rows // 32 * 16
        self.ranges = ((0, cut), (cut, rows - cut))

    def cores(self, keep, give):
        return keep, self.places.swap_core(give)

    def total(self, which, *sections):
        groups = tuple(zip(*sections, strict=True))
        return [
            self.places.swap_plane(chosen_sum((which, which), groups, *rows), 0)
            for rows in self.ranges
        ]

    def send_early(self, one, two, three):
        places = self.places
        self.sections = (one, two, three)
        low, first = jnp.logical_not(places.first_bit), places.is_first
        which = jnp.where(low, 2, jnp.where(first, 1, 0))
        self.early = self.total(which, one, two, three)

    def plane(self, zero):
        places = self.places
        one, two, three = self.sections
        low, first = jnp.logical_not(places.first_bit), places.is_first
        which = jnp.where(low, jnp.where(first, 1, 2), 0)
        late = self.total(which, zero, one, two)
        keeps, gots = zip(zero, one, two, three, strict=True)
        other = places.section ^ jnp.where(first, 2, 1)
        sums = []
        for early_part, late_part, rows in zip(self.early, late, self.ranges, strict=True):

            def held(section, arrived=(early_part, late_part), rows=rows):
                is_late = (section == 0) | ((section == 1) & first) | ((section == 2) & (~first))
                return chosen_sum((section, section, is_late), (keeps, gots, arrived), *rows)

            got = places.swap_plane(held(other), 1)
            sums.append(held(places.section) + got)
        return sums

    def shared(self, rows):
        return jnp.where(self.places.is_first, rows, self.places.swap_core(rows))

    def depth(self, blocks, beside):
        places = self.places
        place = places.dp // 2
        if blocks.shape[0] == 4:
            near, far = place % 2, place // 2
            mine = jnp.where(places.is_first, near, 2 * far)
            theirs = jnp.where(places.is_first, 1 - near, 2 - 2 * far)
            step = 2 - places.core

            def two(first):
                return jnp.stack([pick(blocks, first), pick(blocks, first + step)])

            blocks = two(mine) + places.send(two(theirs), lambda s, d: (s, d ^ (2 + 2 * (d % 2))))
            mine = jnp.where(places.is_first, far, near)
            got = places.send(
                gate(pick(blocks, 1 - mine), beside), lambda s, d: (s, d ^ (4 - 2 * (d % 2)))
            )
            return pick(blocks, mine).astype(F32) + got.astype(F32), blocks
        bit = 1
        while blocks.shape[0] > 1:
            pairs = blocks.reshape(-1, 2, *blocks.shape[1:])
            mine = (place // bit) % 2
            keep = lax.dynamic_index_in_dim(pairs, mine, 1, keepdims=False)
            give = lax.dynamic_index_in_dim(pairs, 1 - mine, 1, keepdims=False)
            blocks = keep + places.swap_dp(give, 2 * bit)
            bit *= 2
        return blocks[0].astype(F32), blocks


def on_device(
    stream_input,
    accum_input,
    section_weights,
    section_norms,
    final_norm,
    seq_lengths,
    out_cotangent,
):
    places = Places()
    section, core = places.section, places.core
    width = D // SECTIONS
    rows = D // 2

    own = section_weights[0]
    pieces = token_pieces(places, stream_input[None])
    small = jnp.concatenate([section_norms.reshape(2 * D), final_norm.reshape(2 * width)])
    small = jnp.pad(small[None], ((0, 15), (0, 4 * D - small.shape[0])))
    near_pieces = gather_start(
        places,
        jnp.concatenate([lax.dynamic_slice(own, (core * rows, 0), (rows, 4 * D)), small], axis=0),
        *pieces,
    )
    near = gather_finish(places, near_pieces)
    stream = jnp.concatenate(in_order([piece[0] for piece in pieces], places.mine), axis=1)
    one, two, three = (piece[rows] for piece in near_pieces)
    table = in_order(
        (
            small[0], jnp.where(places.turned == 0, one, two), jnp.where(places.turned == 0, two, one),
            three,
        ),
        section,
    )
    norms = jnp.stack(table).astype(F32)
    queries, own_kv = project(places, stream, own, near, 0)
    far_kv = places.swap_core(own_kv)
    late_pieces = gather_start(
        places, lax.dynamic_slice(own, (core * rows, 4 * D), (rows, 2 * D)), queries
    )

    *segs, live = sequences(places, seq_lengths)
    qseg = segs[0]
    both = token_pieces(places, jnp.stack([accum_input, out_cotangent]))

    kept = attend(places, stream, queries, own_kv, far_kv, segs, own, near, norms, 0)
    late = gather_finish(places, [late_pieces[0], gate(late_pieces[1], kept[0]), gate(late_pieces[2], kept[0])])
    sum_f, branch_sum, turning, queries_two, own_kv_two = feed(
        places, stream, kept[3], kept[2], own, near, late, norms, 1
    )
    far_kv_two = places.swap_core(own_kv_two)
    context, lse, middle, sum_a = attend(
        places, turning, queries_two, own_kv_two, far_kv_two, segs, own, near, norms, 2
    )
    (
        result, dy_low, dy, final_grad, dz, dctx, delta, grads, keep_f, give_f, rest,
    ) = turn(
        places, middle, turning, sum_a, context, own, near, late, norms, branch_sum, both, live
    )

    reduction = Reduction(places)
    zero = jnp.zeros((HALF, D), F32)

    def scores(queries, own_kv, far_kv, dctx, lse, delta):
        dq, dkv_far = scores_back(queries, far_kv, dctx, qseg, segs[2], lse, delta, zero, BF)
        from_far = places.swap_core(dkv_far)
        dq, dkv = scores_back(queries, own_kv, dctx, qseg, segs[1], lse, delta, dq, BF)
        return dq, dkv, from_far

    third = reduction.cores(keep_f, give_f)
    dq, dkv, from_far = scores(queries_two, own_kv_two, far_kv_two, dctx, lse, delta)
    dz, dctx, delta, grads_first, keep_p, give_p, keep_f, give_f, rest = between(
        places, turning, dq, dkv, from_far, dz, dy, grads, final_grad, rest, (*kept, sum_f), own,
        near, late, norms,
    )
    reduction.send_early(reduction.cores(keep_f, give_f), reduction.cores(keep_p, give_p), third)
    dq, dkv, from_far = scores(queries, own_kv, far_kv, dctx, kept[1], delta)
    upstream, keep, *give = project_back(
        places, stream, dq, dkv, from_far, dz, own, near, 0, grads_first, final_grad, rest
    )
    swapped = places.swap_core(give[0]), places.swap_core(gate(give[1], *reduction.early))
    blocks = reduction.plane((keep, swapped))
    leaving = tokens_out(places, (upstream, result, dy_low), blocks[0])
    reduced, early = zip(*(reduction.depth(part, leaving[2]) for part in blocks), strict=True)
    reduced = jnp.concatenate(reduced, axis=0)
    shared = reduction.shared(reduced[places.blk :])
    stream_out, result_out, accum_out = tokens_placed(places, leaving, (F32, BF, F32), early[1])
    slab = reduced[: places.blk].T
    cut = D // places.ndp
    norm_out = lax.dynamic_slice(reduced, (places.blk, places.dp * cut), (2, cut))
    final_out = lax.dynamic_slice(shared, (2, section * width), (2, width))

    return (
        result_out,
        stream_out,
        accum_out,
        slab[None],
        norm_out[None],
        final_out,
    )


def solution(mesh):
    placed = (
        P("dp", "section"),
        P("dp", "section"),
        P("section", None, None),
        P("section", None, None),
        P(None, "section"),
        P("dp", None),
        P("dp", "section"),
    )
    return jax.shard_map(
        on_device,
        mesh=mesh,
        in_specs=placed,
        out_specs=(
            P("dp", "section"),
            P("dp", "section"),
            P("dp", "section"),
            P("section", None, "dp"),
            P("section", None, "dp"),
            P(None, "section"),
        ),
        check_vma=False,
    )
```

```python
import functools
import math

import jax
import jax.numpy as jnp
from jax import lax
from jax.experimental import pallas as pl
from jax.experimental.pallas import tpu as pltpu
from jax.sharding import PartitionSpec as P

D = 512
HEADS = 8
HEAD = 64
PACK = 1024
HALF = PACK // 2
PAIRS = HEADS // 2
LANES = 2 * HEAD
SECTIONS = 4
FAR = 1e30
SCALE = HEAD ** (-0.5)
BF = jnp.bfloat16
F32 = jnp.float32
NT = (((1,), (1,)), ((), ()))
TN = (((0,), (0,)), ((), ()))


def mm(left, right):
    return jnp.dot(left, right, preferred_element_type=F32)


def mm_nt(left, right):
    return lax.dot_general(left, right, NT, preferred_element_type=F32)


def mm_tn(left, right):
    return lax.dot_general(left, right, TN, preferred_element_type=F32)


def params(megabytes=16):
    return pltpu.CompilerParams(
        dimension_semantics=("arbitrary",), vmem_limit_bytes=megabytes * 1024 * 1024
    )


def shaped(rows, cols, dtype):
    return jax.ShapeDtypeStruct((rows, cols), dtype)


def in_hbm(array):
    return pltpu.with_memory_space_constraint(array, pltpu.HBM)


def whole(rows, cols):
    return pl.BlockSpec((rows, cols), lambda i: (0, 0))


SCALAR = pl.BlockSpec(memory_space=pltpu.SMEM)


def cost(flops, moved, transcendentals=0):
    return pl.CostEstimate(
        flops=int(flops), bytes_accessed=int(moved), transcendentals=int(transcendentals)
    )


def gain_of(table_ref, layer):
    return table_ref[layer : layer + 1, :D]


def shift_of(table_ref, layer):
    return table_ref[layer : layer + 1, D : 2 * D]


def norm_parts(summed):
    average = jnp.mean(summed, axis=-1, keepdims=True)
    centered = summed - average
    spread = jnp.mean(centered * centered, axis=-1, keepdims=True)
    inverse = lax.rsqrt(spread + 1e-05)
    return centered * inverse, inverse


def norm_forward(summed, table_ref, layer):
    normal, _ = norm_parts(summed)
    return normal * gain_of(table_ref, layer) + shift_of(table_ref, layer)


def norm_back(summed, gain, upstream):
    normal, inverse = norm_parts(summed)
    scaled = upstream * gain
    mean_one = jnp.mean(scaled, axis=-1, keepdims=True)
    mean_two = jnp.mean(scaled * normal, axis=-1, keepdims=True)
    grad = (scaled - mean_one - normal * mean_two) * inverse
    gain_grad = jnp.sum(upstream * normal, axis=0, keepdims=True)
    shift_grad = jnp.sum(upstream, axis=0, keepdims=True)
    return grad, gain_grad, shift_grad


def head_mask(which):
    lane = lax.broadcasted_iota(jnp.int32, (1, LANES), 1)
    return (lane // HEAD) == which


def three_way(column):
    high = column.astype(BF)
    rest = column - high.astype(F32)
    middle = rest.astype(BF)
    low = (rest - middle.astype(F32)).astype(BF)
    return high, middle, low


GROUP = 6


def fetch(where_ref, layer, own_ref, piece_refs, own_first, first, width, target, sem):
    section, core, turned = where_ref[0], where_ref[1], where_ref[3]
    half = D // 2
    step = section ^ layer
    mine_rows = pl.ds(pl.multiple_of(core * half, half), half)
    far_rows = pl.ds(pl.multiple_of((1 - core) * half, half), half)

    @pl.when(step == 0)
    def _():
        pltpu.make_async_copy(own_ref.at[:, pl.ds(own_first, width)], target, sem).start()

    for number, (partner, far_number) in enumerate(((1 + turned, 1), (2 - turned, 0), (3, 2))):

        @pl.when(step == partner)
        def _():
            part = (pl.ds(0, half), pl.ds(first, width))
            mine, far = piece_refs[number].at[part], piece_refs[3 + far_number].at[part]
            pltpu.make_async_copy(mine, target.at[mine_rows], sem).start()
            pltpu.make_async_copy(far, target.at[far_rows], sem).start()


def arrived(own_ref, width, target, sem):
    pltpu.make_async_copy(own_ref.at[:, pl.ds(0, width)], target, sem).wait()


def weight_specs(groups):
    return [pl.BlockSpec(memory_space=pl.ANY)] * (1 + GROUP * groups)


def column_of(pair):
    return pl.ds(pl.multiple_of(pair * LANES, LANES), LANES)


def fetch_projection(layer, where_ref, own_ref, near, weight_ref, sems):
    for part in range(3):
        fetch(
            where_ref, layer, own_ref, near, part * D, part * D, D, weight_ref.at[part],
            sems.at[part],
        )


def fetch_outward(layer, where_ref, own_ref, near, weight_ref, sem):
    fetch(where_ref, layer, own_ref, near, 3 * D, 3 * D, D, weight_ref, sem)


def fetch_feed(layer, where_ref, own_ref, near, late, weight_ref, sems):
    for chunk in range(4):
        turn = chunk % 2
        if chunk < 2:
            inner = (layer - 1, late, (4 + turn) * D, turn * D)
            outer = (layer, near, (2 + turn) * D, (2 + turn) * D)
        else:
            inner = (layer, near, turn * D, turn * D)
            outer = (layer, late, (4 + turn) * D, turn * D)
        for number, (whose, pieces, own_first, first) in enumerate((inner, outer)):
            fetch(
                where_ref, whose, own_ref, pieces, own_first, first, D,
                weight_ref.at[chunk, number], sems.at[chunk, number],
            )


PROJECTION = [pltpu.VMEM((3, D, D), BF), pltpu.SemaphoreType.DMA((3,))]
OUTWARD = [pltpu.VMEM((D, D), BF), pltpu.SemaphoreType.DMA]
FEED = [pltpu.VMEM((4, 2, D, D), BF), pltpu.SemaphoreType.DMA((4, 2))]


def put_projection(own_ref, x, q_ref, kv_ref, weight_ref, sems):
    def times(part):
        arrived(own_ref, D, weight_ref.at[part], sems.at[part])
        return mm(x, weight_ref[part]).astype(BF)

    q_ref[...] = times(0)
    keys, values = times(1), times(2)
    for pair in range(PAIRS):
        lanes = slice(pair * LANES, (pair + 1) * LANES)
        kv_ref[pair, :, :LANES] = keys[:, lanes]
        kv_ref[pair, :, LANES:] = values[:, lanes]


def put_attention(q_ref, own_ref, far_ref, qs_ref, kso_ref, ksx_ref, ctx_ref, lse_ref):
    none = jnp.zeros((), BF)
    lane = lax.broadcasted_iota(jnp.int32, (1, LANES), 1)
    ones = jnp.ones((HALF, LANES), BF)
    lse_ref[...] = jnp.zeros((HALF, LANES), F32)

    @pl.loop(0, PAIRS)
    def _(pair):
        q = q_ref[:, column_of(pair)] * jnp.asarray(SCALE, BF)
        keys_own = jnp.concatenate([own_ref[pair, :, :LANES], kso_ref[...]], axis=1)
        keys_other = jnp.concatenate([far_ref[pair, :, :LANES], ksx_ref[...]], axis=1)
        values_own, values_other = own_ref[pair, :, LANES:], far_ref[pair, :, LANES:]
        context = jnp.zeros((HALF, LANES), F32)
        logs = lse_ref[...]
        for which in range(2):
            mask = head_mask(which)
            query = jnp.concatenate([jnp.where(mask, q, none), qs_ref[...]], axis=1)
            score_own = mm_nt(query, keys_own)
            score_other = mm_nt(query, keys_other)
            peak = jnp.maximum(
                jnp.max(score_own, axis=1, keepdims=True),
                jnp.max(score_other, axis=1, keepdims=True),
            )
            own = jnp.exp(score_own - peak).astype(BF)
            other = jnp.exp(score_other - peak).astype(BF)
            total = mm(
                own, jnp.concatenate([jnp.where(mask, values_own, none), ones], axis=1)
            ) + mm(other, jnp.concatenate([jnp.where(mask, values_other, none), ones], axis=1))
            row_total = total[:, LANES:]
            context = context + total[:, :LANES] / row_total
            logs = jnp.where(lane == 2 * pair + which, peak + jnp.log(row_total), logs)
        lse_ref[...] = logs
        ctx_ref[:, column_of(pair)] = context.astype(BF)


def gelu_parts(v):
    root = 0.7978845608028654
    squared = v * v
    inner = root * (v + 0.044715 * v * squared)
    t = jnp.tanh(inner)
    hidden = 0.5 * v * (1.0 + t)
    slope = 0.5 * (1.0 + t) + 0.5 * v * (1.0 - t * t) * (root * (1.0 + 3 * 0.044715 * squared))
    return hidden, slope


def feed_weight(own_ref, weight_ref, sems, chunk, number):
    arrived(own_ref, D, weight_ref.at[chunk, number], sems.at[chunk, number])
    return weight_ref[chunk, number]


def half_of(refs, place):
    if not isinstance(refs, tuple):
        return refs, place
    half = refs[0].shape[0]
    return refs[place // half], place % half


def split_rows(core, blk, row, value, keep_ref, give_ref):
    step = math.gcd(D, blk)
    for k in range(value.shape[0] // step):
        part = value[k * step : (k + 1) * step]
        first = row + k * step
        block, offset = first // blk, first % blk

        @pl.when(block % 2 == core)
        def _():
            keep_ref[block // 2, offset : offset + step, :] = part

        @pl.when(block % 2 != core)
        def _():
            ref, place = half_of(give_ref, block // 2)
            ref[place, offset : offset + step, :] = part


def side_rows(grads, final_grads, keep_ref, give_ref):
    extra = jnp.concatenate([grads, final_grads, jnp.zeros((12, D), F32)], axis=0).astype(BF)
    blk = keep_ref.shape[1] - 16
    for block in range(keep_ref.shape[0]):
        keep_ref[block, blk:, :] = extra
        ref, place = half_of(give_ref, block)
        ref[place, blk:, :] = extra


def split_shapes(count, blk):
    return [full(count, blk + 16, D)] * 2, [pltpu.HBM((count, blk + 16, D), BF)] * 2


def put_outward_back(
    summed, upstream, dy, context, gain, weight_of, dctx_ref, delta_ref, grad_ref, rest_ref
):
    grad, gain_grad, shift_grad = norm_back(summed, gain, upstream)
    grad_ref[...] = jnp.concatenate([gain_grad, shift_grad], axis=0)
    df = (grad + dy).astype(BF)
    rest_ref[:D] = mm_tn(df, context).astype(BF)
    context_grad = mm_nt(df, weight_of()).astype(BF)
    dctx_ref[...] = context_grad
    product = context.astype(F32) * context_grad.astype(F32)
    lane = lax.broadcasted_iota(jnp.int32, (1, LANES), 1)
    delta = jnp.zeros((HALF, LANES), F32)
    for head in range(HEADS):
        part = product[:, (head // 2) * LANES : (head // 2 + 1) * LANES]
        inner = jnp.sum(jnp.where(head_mask(head % 2), part, 0.0), axis=1, keepdims=True)
        delta = jnp.where(lane == head, inner, delta)
    delta_ref[...] = delta
    return grad


def put_feed_back(
    core, x, hidden_of, df, grad, weight_of, rest_ref, keep_ref, give_ref
):
    blk = keep_ref.shape[1] - 16
    total = grad
    for chunk in range(4):
        inner, outer = weight_of(chunk, 0), weight_of(chunk, 1)
        hidden, slope = hidden_of(chunk, inner)
        split_rows(core, blk, (2 + chunk) * D, mm_tn(hidden, df).astype(BF), keep_ref, give_ref)
        preact_grad = (mm(df, outer) * slope).astype(BF)
        inner_grad = mm_tn(preact_grad, x).astype(BF)
        if chunk < 2:
            rest_ref[(1 + chunk) * D : (2 + chunk) * D] = inner_grad
        else:
            split_rows(core, blk, (chunk - 2) * D, inner_grad, keep_ref, give_ref)
        total = total + mm_nt(preact_grad, inner)
    return total


def put_project_back(
    core, x, dq_ref, dkv_ref, far_ref, dz, grads, final_grads, rest_ref, weight_of, keep_ref,
    give_ref,
):
    blk = keep_ref.shape[1] - 16
    side_rows(grads, final_grads, keep_ref, give_ref)
    split_rows(core, blk, 3 * D, rest_ref[...], keep_ref, give_ref)
    parts = [(dkv_ref[k].astype(F32) + far_ref[k].astype(F32)).astype(BF) for k in range(PAIRS)]
    dk = jnp.concatenate([part[:, :LANES] for part in parts], axis=1)
    dv = jnp.concatenate([part[:, LANES:] for part in parts], axis=1)
    total = dz
    for place, grad in enumerate((dq_ref[...].astype(BF), dk, dv)):
        split_rows(core, blk, place * D, mm_tn(grad, x).astype(BF), keep_ref, give_ref)
        total = total + mm_nt(grad, weight_of(place))
    return total


def full(*shape):
    return pl.BlockSpec(shape, lambda i: (0,) * len(shape), pipeline_mode=pl.Buffered(1))


KV = (PAIRS, HALF, 2 * LANES)
TABLE = (SECTIONS, 4 * D)


def project_kernel(layer, where_ref, x_ref, own_ref, *refs):
    near, (q_ref, kv_ref, weight_ref, sems) = refs[:GROUP], refs[GROUP:]
    fetch_projection(layer, where_ref, own_ref, near, weight_ref, sems)
    put_projection(own_ref, x_ref[...], q_ref, kv_ref, weight_ref, sems)


def project(places, stream, own, near, layer):
    return pl.pallas_call(
        functools.partial(project_kernel, layer),
        grid=(1,),
        in_specs=[SCALAR, full(HALF, D), *weight_specs(1)],
        out_specs=[full(HALF, D), full(*KV)],
        out_shape=[shaped(HALF, D, BF), jax.ShapeDtypeStruct(KV, BF)],
        scratch_shapes=PROJECTION,
        compiler_params=params(),
        cost_estimate=cost(2 * HALF * D * 3 * D, 4e6),
        name="project",
    )(places.where, stream, *map(in_hbm, (own, *near)))


def feed_kernel(layer, where_ref, x_ref, sum_ref, middle_ref, norm_ref, own_ref, *refs):
    near, late, refs = refs[:GROUP], refs[GROUP : 2 * GROUP], refs[2 * GROUP :]
    (
        sum_f_ref, branch_ref, next_ref, q_next_ref, kv_next_ref, feed_ref, feed_sems,
        project_ref, project_sems,
    ) = refs
    fetch_feed(layer, where_ref, own_ref, near, late, feed_ref, feed_sems)
    fetch_projection(layer + 1, where_ref, own_ref, near, project_ref, project_sems)
    middle = middle_ref[...]
    total = jnp.zeros((HALF, D), F32)
    for chunk in range(4):
        inner = feed_weight(own_ref, feed_ref, feed_sems, chunk, 0)
        hidden = gelu_parts(mm(middle, inner))[0].astype(BF)
        total = total + mm_nt(hidden, feed_weight(own_ref, feed_ref, feed_sems, chunk, 1))
    summed = middle.astype(F32) + total
    sum_f_ref[...] = summed
    branch_ref[...] = sum_ref[...] - x_ref[...].astype(F32) + total
    following = norm_forward(summed, norm_ref, layer).astype(BF)
    next_ref[...] = following
    put_projection(own_ref, following, q_next_ref, kv_next_ref, project_ref, project_sems)


def feed(places, stream, sum_a, middle, own, near, late, norms, layer):
    return pl.pallas_call(
        functools.partial(feed_kernel, layer),
        grid=(1,),
        in_specs=[SCALAR, *[full(HALF, D)] * 3, full(*TABLE), *weight_specs(2)],
        out_specs=[*[full(HALF, D)] * 4, full(*KV)],
        out_shape=[
            shaped(HALF, D, F32), shaped(HALF, D, F32), shaped(HALF, D, BF), shaped(HALF, D, BF),
            jax.ShapeDtypeStruct(KV, BF),
        ],
        scratch_shapes=[*FEED, *PROJECTION],
        compiler_params=params(18),
        cost_estimate=cost(6e9, 14e6, 1e6),
        name="feed",
    )(places.where, *map(in_hbm, (stream, sum_a, middle)), norms, *map(in_hbm, (own, *near, *late)))


def attend_kernel(
    layer, where_ref, q_ref, own_kv_ref, far_kv_ref, qs_ref, kso_ref, ksx_ref, x_ref, norm_ref,
    own_ref, *refs,
):
    near, refs = refs[:GROUP], refs[GROUP:]
    ctx_ref, lse_ref, middle_ref, sum_ref, outward_ref, outward_sem = refs
    fetch_outward(layer, where_ref, own_ref, near, outward_ref, outward_sem)
    put_attention(
        q_ref, own_kv_ref, far_kv_ref, qs_ref, kso_ref, ksx_ref, ctx_ref, lse_ref
    )
    arrived(own_ref, D, outward_ref, outward_sem)
    summed = x_ref[...].astype(F32) + mm(ctx_ref[...], outward_ref[...])
    sum_ref[...] = summed
    middle_ref[...] = norm_forward(summed, norm_ref, layer).astype(BF)


def attend(places, stream, queries, own_kv, far_kv, segs, own, near, norms, layer):
    kind = jax.ShapeDtypeStruct if layer else pltpu.HBM
    return pl.pallas_call(
        functools.partial(attend_kernel, layer),
        grid=(1,),
        in_specs=[
            SCALAR, full(HALF, D), full(*KV), full(*KV), *[full(HALF, LANES)] * 3, full(HALF, D),
            full(*TABLE), *weight_specs(1),
        ],
        out_specs=[full(HALF, D), full(HALF, LANES), full(HALF, D), full(HALF, D)],
        out_shape=[
            kind((HALF, D), BF), kind((HALF, LANES), F32), kind((HALF, D), BF),
            kind((HALF, D), F32),
        ],
        scratch_shapes=OUTWARD,
        compiler_params=params(),
        cost_estimate=cost(9e9, 10e6, 4e6),
        name="attend",
    )(places.where, queries, own_kv, far_kv, *segs, stream, norms, *map(in_hbm, (own, *near)))


def turn_kernel(
    layer, where_ref, middle_ref, x_ref, sum_ref, ctx_ref, norm_ref, branch_ref,
    a_ref, b_ref, c_ref, d_ref, live_ref, own_ref, *refs,
):
    near, late, refs = refs[:GROUP], refs[GROUP : 2 * GROUP], refs[2 * GROUP :]
    (
        result_ref, low_ref, dy_ref, final_ref, dz_ref, dctx_ref, delta_ref, grad_ref,
        feed_keep, feed_give, rest_ref,
        hidden_ref, slope_ref, outward_ref, outward_sem, feed_ref, feed_sems,
    ) = refs
    core, mine = where_ref[1], where_ref[2]
    fetch_feed(layer + 1, where_ref, own_ref, near, late, feed_ref, feed_sems)
    fetch_outward(layer, where_ref, own_ref, near, outward_ref, outward_sem)
    middle, sum_a = middle_ref[...], sum_ref[...]
    branch = sum_a - x_ref[...].astype(F32)
    total = jnp.zeros((HALF, D), F32)
    for chunk in range(4):
        inner = feed_weight(own_ref, feed_ref, feed_sems, chunk, 0)
        hidden, slope = gelu_parts(mm(middle, inner))
        hidden = hidden.astype(BF)
        hidden_ref[chunk] = hidden
        slope_ref[chunk] = slope
        total = total + mm_nt(hidden, feed_weight(own_ref, feed_ref, feed_sems, chunk, 1))
    sum_f = middle.astype(F32) + total
    last = norm_forward(sum_f, norm_ref, layer + 1)

    pieces = in_order([ref[...] for ref in (a_ref, b_ref, c_ref, d_ref)], mine)
    accum, cot = (jnp.concatenate([piece[k] for piece in pieces], axis=1) for k in range(2))
    summed = accum.astype(F32) + (branch_ref[...] + (branch + total))
    normal, _ = norm_parts(summed)
    width = D // SECTIONS
    gain, shift = (
        jnp.concatenate(
            [
                norm_ref[k : k + 1, 2 * D + part * width : 2 * D + (part + 1) * width]
                for k in range(SECTIONS)
            ],
            axis=1,
        )
        for part in range(2)
    )
    result_ref[...] = (last + normal * gain + shift).astype(BF)
    cot = cot.astype(F32) * live_ref[:, 0:1]
    dy, gain_grad, shift_grad = norm_back(summed, gain, cot)
    dy_ref[...] = dy
    low_ref[...] = dy.astype(BF)
    final_grads = jnp.concatenate([gain_grad, shift_grad], axis=0)
    final_ref[...] = final_grads

    grad, gain_grad, shift_grad = norm_back(sum_f, gain_of(norm_ref, layer + 1), cot)
    side_rows(
        jnp.concatenate([gain_grad, shift_grad], axis=0), final_grads, feed_keep, feed_give
    )
    upstream = put_feed_back(
        core, middle, lambda chunk, inner: (hidden_ref[chunk], slope_ref[chunk]),
        (grad + dy).astype(BF), grad, lambda chunk, number: feed_ref[chunk, number],
        rest_ref, feed_keep, feed_give,
    )
    arrived(own_ref, D, outward_ref, outward_sem)
    dz_ref[...] = put_outward_back(
        sum_a, upstream.astype(BF).astype(F32), dy, ctx_ref[...], gain_of(norm_ref, layer),
        lambda: outward_ref[...], dctx_ref, delta_ref, grad_ref, rest_ref,
    )


def turn(places, middle, stream, sum_a, context, own, near, late, norms, branch_sum, pieces, live):
    specs, shapes = split_shapes(places.ndp // 2, places.blk)
    return pl.pallas_call(
        functools.partial(turn_kernel, 2),
        grid=(1,),
        in_specs=[
            SCALAR, *[full(HALF, D)] * 4, full(*TABLE), full(HALF, D),
            *[full(2, HALF, D // SECTIONS)] * 4, full(HALF, LANES), *weight_specs(2),
        ],
        out_specs=[
            *[full(HALF, D)] * 3, full(2, D), full(HALF, D), full(HALF, D),
            full(HALF, LANES), full(2, D), *specs, full(3 * D, D),
        ],
        out_shape=[
            shaped(HALF, D, BF), shaped(HALF, D, BF),
            shaped(HALF, D, F32), shaped(2, D, F32), shaped(HALF, D, F32), shaped(HALF, D, BF),
            shaped(HALF, LANES, F32), shaped(2, D, F32), *shapes, shaped(3 * D, D, BF),
        ],
        scratch_shapes=[
            pltpu.VMEM((4, HALF, D), BF), pltpu.VMEM((4, HALF, D), F32), *OUTWARD, *FEED,
        ],
        compiler_params=params(28),
        cost_estimate=cost(16e9, 30e6, 2e6),
        name="turn",
    )(
        places.where, middle, stream, sum_a, context, norms, branch_sum, *pieces, live, *map(in_hbm, (own, *near, *late)),
    )


def column():
    return pl.BlockSpec((HALF, LANES), lambda i: (0, i))


def pair_block():
    return pl.BlockSpec((1, HALF, 2 * LANES), lambda i: (i, 0, 0))


def scores_back_kernel(
    q_ref, kv_ref, dctx_ref, qs_ref, ks_ref, lse_ref, delta_ref, *refs
):
    pair = pl.program_id(0)
    none = jnp.zeros((), BF)
    lane = lax.broadcasted_iota(jnp.int32, (1, LANES), 1)
    q = q_ref[...] * jnp.asarray(SCALE, BF)
    k = kv_ref[0, :, :LANES]
    k_scaled = k * jnp.asarray(SCALE, BF)
    dctx = dctx_ref[...]
    extra = jnp.where((lane >= LANES - 3), jnp.ones((), BF), none)
    keys = jnp.concatenate([k, ks_ref[...] + extra], axis=1)
    values = jnp.concatenate(
        [kv_ref[0, :, LANES:], jnp.broadcast_to(extra, (HALF, LANES))], axis=1
    )
    *before, dq_ref, dkv_ref = refs
    dq = before[0][...] if before else jnp.zeros((HALF, LANES), F32)
    dk = jnp.zeros((HALF, LANES), F32)
    dv = jnp.zeros((HALF, LANES), F32)
    for which in range(2):
        mask = head_mask(which)
        here = lane == 2 * pair + which

        def lanes_of(table, base):
            column = -jnp.sum(jnp.where(here, table, 0.0), axis=1, keepdims=True)
            high, middle, low = three_way(column)
            base = jnp.where(lane == LANES - 3, high, base)
            base = jnp.where(lane == LANES - 2, middle, base)
            return jnp.where(lane == LANES - 1, low, base)

        query_part = jnp.where(mask, q, none)
        dctx_part = jnp.where(mask, dctx, none)
        query = jnp.concatenate([query_part, lanes_of(lse_ref[...], qs_ref[...])], axis=1)
        dcontext = jnp.concatenate(
            [dctx_part, lanes_of(delta_ref[...], jnp.zeros((HALF, LANES), BF))], axis=1
        )
        probability = jnp.exp(mm_nt(keys, query))
        score_grad = (probability * mm_nt(values, dcontext)).astype(BF)
        dv = dv + mm(probability.astype(BF), dctx_part)
        dk = dk + mm(score_grad, query_part)
        dq = dq + mm_tn(score_grad, jnp.where(mask, k_scaled, none))
    dq_ref[...] = dq
    dkv_ref[0, :, :LANES] = dk.astype(dkv_ref.dtype)
    dkv_ref[0, :, LANES:] = dv.astype(dkv_ref.dtype)


def scores_back(queries, kv, dctx, qseg, kseg, lse, delta, out_type, *before):
    return pl.pallas_call(
        scores_back_kernel,
        grid=(PAIRS,),
        in_specs=[
            column(), pair_block(), column(),
            whole(HALF, LANES), whole(HALF, LANES), whole(HALF, LANES), whole(HALF, LANES),
            *[column()] * len(before),
        ],
        out_specs=[column(), pair_block()],
        out_shape=[
            shaped(HALF, D, F32), jax.ShapeDtypeStruct((PAIRS, HALF, 2 * LANES), out_type),
        ],
        compiler_params=params(),
        cost_estimate=cost(8e9, 8e6, 2e6),
        name="scores_back",
    )(queries, kv, dctx, qseg, kseg, lse, delta, *before)


def middle_kernel(
    layer, where_ref, x_ref, dq_ref, dkv_ref, far_ref, dz_ref, dy_ref, grad_ref, final_ref,
    before_ref, middle_ref, sum_f_ref, sum_a_ref, ctx_ref, norm_ref, own_ref, *refs,
):
    near, late, refs = refs[:GROUP], refs[GROUP : 2 * GROUP], refs[2 * GROUP :]
    (
        dz_out, dctx_ref, delta_ref, grad_out, project_keep, project_give, feed_keep, feed_give,
        rest_ref,
        project_ref, project_sems, feed_ref, feed_sems, outward_ref, outward_sem,
    ) = refs
    core = where_ref[1]
    fetch_projection(layer, where_ref, own_ref, near, project_ref, project_sems)
    fetch_feed(layer - 1, where_ref, own_ref, near, late, feed_ref, feed_sems)
    fetch_outward(layer - 2, where_ref, own_ref, near, outward_ref, outward_sem)
    final_grads = final_ref[...]

    def project_weight(place):
        arrived(own_ref, D, project_ref.at[place], project_sems.at[place])
        return project_ref[place]

    def outward_weight():
        arrived(own_ref, D, outward_ref, outward_sem)
        return outward_ref[...]

    upstream = put_project_back(
        core, x_ref[...], dq_ref, dkv_ref, far_ref, dz_ref[...], grad_ref[...], final_grads,
        before_ref, project_weight, project_keep, project_give,
    ).astype(BF).astype(F32)
    dy = dy_ref[...]
    grad, gain_grad, shift_grad = norm_back(
        sum_f_ref[...], gain_of(norm_ref, layer - 1), upstream
    )
    side_rows(
        jnp.concatenate([gain_grad, shift_grad], axis=0), final_grads, feed_keep, feed_give
    )
    middle = middle_ref[...]

    def hidden_of(chunk, inner):
        hidden, slope = gelu_parts(mm(middle, inner))
        return hidden.astype(BF), slope

    upstream = put_feed_back(
        core, middle, hidden_of, (grad + dy).astype(BF), grad,
        functools.partial(feed_weight, own_ref, feed_ref, feed_sems), rest_ref, feed_keep, feed_give,
    ).astype(BF).astype(F32)
    dz_out[...] = put_outward_back(
        sum_a_ref[...], upstream, dy, ctx_ref[...], gain_of(norm_ref, layer - 2),
        outward_weight, dctx_ref, delta_ref, grad_out, rest_ref,
    )


def between(
    places, stream, dq, dkv, far, dz, dy, grads, final_grads, rest, kept, own, near, late, norms
):
    context, _, middle, sum_a, sum_f = kept
    specs, shapes = split_shapes(places.ndp // 2, places.blk)
    return pl.pallas_call(
        functools.partial(middle_kernel, 2),
        grid=(1,),
        in_specs=[
            SCALAR, full(HALF, D), full(HALF, D), full(*KV), full(*KV), full(HALF, D),
            full(HALF, D), full(2, D), full(2, D), full(3 * D, D), *[full(HALF, D)] * 4,
            full(*TABLE), *weight_specs(2),
        ],
        out_specs=[
            full(HALF, D), full(HALF, D), full(HALF, LANES), full(2, D), *specs, *specs,
            full(3 * D, D),
        ],
        out_shape=[
            shaped(HALF, D, F32), shaped(HALF, D, BF), shaped(HALF, LANES, F32),
            shaped(2, D, F32), *shapes, *shapes, shaped(3 * D, D, BF),
        ],
        scratch_shapes=[*PROJECTION, *FEED, *OUTWARD],
        compiler_params=params(28),
        cost_estimate=cost(20e9, 30e6, 2e6),
        name="between",
    )(
        places.where, stream, dq, dkv, far, dz, dy, grads, final_grads, rest, middle, sum_f,
        sum_a, context, norms, *map(in_hbm, (own, *near, *late)),
    )


def project_back_kernel(
    layer, where_ref, x_ref, dq_ref, dkv_ref, far_ref, dz_ref, grad_ref, final_ref, rest_ref,
    own_ref, *refs,
):
    near, (dx_ref, keep_ref, *give, weight_ref, sems) = refs[:GROUP], refs[GROUP:]
    fetch_projection(layer, where_ref, own_ref, near, weight_ref, sems)

    def weight_of(place):
        arrived(own_ref, D, weight_ref.at[place], sems.at[place])
        return weight_ref[place]

    dx_ref[...] = put_project_back(
        where_ref[1], x_ref[...], dq_ref, dkv_ref, far_ref, dz_ref[...], grad_ref[...],
        final_ref[...], rest_ref, weight_of, keep_ref, tuple(give),
    ).astype(BF)


def project_back(places, stream, dq, dkv, far, dz, own, near, layer, grads, final_grads, rest):
    specs, shapes = split_shapes(places.ndp // 2, places.blk)
    half_specs, half_shapes = split_shapes(places.ndp // 4, places.blk)
    return pl.pallas_call(
        functools.partial(project_back_kernel, layer),
        grid=(1,),
        in_specs=[
            SCALAR, full(HALF, D), full(HALF, D), full(*KV), full(*KV), full(HALF, D),
            full(2, D), full(2, D), full(3 * D, D), *weight_specs(1),
        ],
        out_specs=[full(HALF, D), specs[0], *half_specs],
        out_shape=[shaped(HALF, D, BF), shapes[0], *half_shapes],
        scratch_shapes=PROJECTION,
        compiler_params=params(20),
        cost_estimate=cost(4 * HALF * D * 3 * D, 10e6),
        name="project_back",
    )(places.where, stream, dq, dkv, far, dz, grads, final_grads, rest, *map(in_hbm, (own, *near)))


class Places:
    def __init__(self):
        self.ndp = lax.axis_size("dp")
        self.section = lax.axis_index("section")
        self.dp = lax.axis_index("dp")
        self.core = self.dp % 2
        self.blk = 6 * D // self.ndp
        self.mine = 2 * (self.section % 2) + self.core
        self.turned = (self.dp + self.dp // 2) % 2
        self.where = jnp.stack([self.section, self.core, self.mine, self.turned]).astype(jnp.int32)
        bits = (self.section % 2 == 1, self.section // 2 == 1)
        self.is_first = self.core == 0
        self.first_bit = jnp.where(self.is_first, bits[0], bits[1])
        self.second_bit = jnp.where(self.is_first, bits[1], bits[0])

    def swap_dp(self, block, step):
        return lax.ppermute(block, "dp", [(i, i ^ step) for i in range(self.ndp)])

    def swap_core(self, block):
        return self.swap_dp(block, 1)

    def swap_plane(self, block, turn):
        return self.send(block, lambda s, d: (s ^ (1 + (d + turn) % 2), d))

    def swap_turned(self, block, turn):
        return self.send(block, lambda s, d: (s ^ (1 + (d + d // 2 + turn) % 2), d))

    def send(self, block, route):
        pairs = []
        for s in range(SECTIONS):
            for d in range(self.ndp):
                to = route(s, d)
                pairs.append((s * self.ndp + d, to[0] * self.ndp + to[1]))
        return lax.ppermute(block, ("section", "dp"), pairs)


def pick(stack, index):
    return lax.dynamic_index_in_dim(stack, index, 0, keepdims=False)


ANYWHERE = pl.BlockSpec(memory_space=pl.ANY)


def sequence_kernel(where_ref, own_ref, far_ref, qseg_ref, own_seg_ref, far_seg_ref, live_ref):
    section, core = where_ref[0], where_ref[1]
    here = core == section // 2
    row = section % 2
    lane = lax.broadcasted_iota(jnp.int32, (HALF, LANES), 1)
    spot = lax.broadcasted_iota(jnp.int32, (HALF, LANES), 0)
    own = jnp.zeros((HALF, LANES), jnp.int32)
    far = jnp.zeros((HALF, LANES), jnp.int32)
    ending = jnp.int32(0)
    for k in range(own_ref.shape[1]):
        ending = ending + jnp.where(here, own_ref[row, k], far_ref[row, k])
        own = own + (spot + core * HALF >= ending).astype(jnp.int32)
        far = far + (spot + (1 - core) * HALF >= ending).astype(jnp.int32)
    own_seg_ref[...] = jnp.where(own == lane, 1.0, 0.0).astype(BF)
    far_seg_ref[...] = jnp.where(far == lane, 1.0, 0.0).astype(BF)
    qseg_ref[...] = jnp.where((own != lane) & (lane < 32), -FAR, 0.0).astype(BF)
    live_ref[...] = jnp.where(spot + core * HALF < ending, 1.0, 0.0)


def sequences(places, lengths):
    return pl.pallas_call(
        sequence_kernel,
        grid=(1,),
        in_specs=[SCALAR] * 3,
        out_specs=[whole(HALF, LANES)] * 4,
        out_shape=[shaped(HALF, LANES, BF)] * 3 + [shaped(HALF, LANES, F32)],
        compiler_params=params(),
        cost_estimate=cost(1e6, 1e6),
        name="sequences",
    )(places.where, lengths, places.swap_core(lengths))


def gate_kernel(*refs):
    del refs


def gate(value, *earlier):
    return pl.pallas_call(
        gate_kernel,
        in_specs=[ANYWHERE] * (1 + len(earlier)),
        out_specs=ANYWHERE,
        out_shape=jax.ShapeDtypeStruct(value.shape, value.dtype),
        input_output_aliases={0: 0},
        cost_estimate=cost(0, 0),
        name="gate",
    )(value, *earlier)


def token_pieces(places, block):
    several = block.shape[0]
    pieces = jnp.swapaxes(block.reshape(several, 4, HALF, D // SECTIONS), 0, 1)
    got = []
    for turn in range(4):

        def route(s, d, turn=turn):
            piece = s ^ turn
            return 2 * (d % 2) + piece // 2, d - d % 2 + piece % 2

        got.append(places.send(pick(pieces, places.section ^ turn), route))
    return got


def in_order(pieces, mine):
    one, two = mine % 2 == 1, mine // 2 == 1
    a, b, c, d = pieces
    a, b, c, d = (
        jnp.where(one, b, a), jnp.where(one, a, b), jnp.where(one, d, c), jnp.where(one, c, d)
    )
    return (
        jnp.where(two, c, a), jnp.where(two, d, b), jnp.where(two, a, c), jnp.where(two, b, d)
    )


def deal_kernel(mine_ref, a_ref, b_ref, c_ref, later_ref, *out_refs):
    width = D // SECTIONS
    for k, ref in enumerate((a_ref, b_ref, c_ref)):
        rows = ref[...]
        features = [rows[:, f * width : (f + 1) * width] for f in range(SECTIONS)]
        for out_ref, piece in zip(out_refs, in_order(features, mine_ref[0]), strict=True):
            out_ref[k] = piece


def tokens_out(places, rows, later):
    width = D // SECTIONS
    features = pl.pallas_call(
        deal_kernel,
        grid=(1,),
        in_specs=[SCALAR, *[whole(HALF, D)] * 3, pl.BlockSpec(memory_space=pl.ANY)],
        out_specs=[pl.BlockSpec((3, HALF, width), lambda i: (0, 0, 0))] * SECTIONS,
        out_shape=[jax.ShapeDtypeStruct((3, HALF, width), BF)] * SECTIONS,
        compiler_params=params(),
        cost_estimate=cost(0, 4e6),
        name="deal",
    )(places.mine.reshape(1).astype(jnp.int32), *rows, later)
    got = []
    for turn in range(4):

        def route(s, d, turn=turn):
            return (2 * (s % 2) + d % 2) ^ turn, d - d % 2 + s // 2

        got.append(places.send(features[turn], route))
    return got


def undeal_kernel(section_ref, a_ref, b_ref, c_ref, d_ref, later_ref, x_ref, y_ref, z_ref):
    refs = (a_ref, b_ref, c_ref, d_ref)
    for k, out_ref in enumerate((x_ref, y_ref, z_ref)):
        pieces = in_order([ref[k] for ref in refs], section_ref[0])
        for number, piece in enumerate(pieces):
            out_ref[number * HALF : (number + 1) * HALF] = piece.astype(out_ref.dtype)


def tokens_placed(places, pieces, types, later):
    width = D // SECTIONS
    return pl.pallas_call(
        undeal_kernel,
        grid=(1,),
        in_specs=[SCALAR, *[pl.BlockSpec((3, HALF, width), lambda i: (0, 0, 0))] * 4, ANYWHERE],
        out_specs=[whole(4 * HALF, width)] * 3,
        out_shape=[shaped(4 * HALF, width, kind) for kind in types],
        compiler_params=params(),
        cost_estimate=cost(0, 4e6),
        name="undeal",
    )(places.section.reshape(1).astype(jnp.int32), *pieces, later)


def gather_start(places, mine, *earlier):
    one = places.swap_turned(mine, 0)
    if earlier:
        one = gate(one, *earlier)
    return one, places.swap_dp(one, 2), places.swap_turned(one, 1)


def gather_finish(places, pieces):
    return (*pieces, *(places.swap_core(piece) for piece in pieces))


def chosen_kernel(counts, parts, starts, which_ref, *refs):
    total = sum(parts)
    arrays, (out_ref, held_ref, sems) = refs[:total], refs[total:]
    blocks, rows, _ = out_ref.shape

    def copies(number, place):
        first = sum(parts[:number])
        count = blocks // parts[number]
        for k in range(parts[number]):
            source = arrays[first + k].at[:, pl.ds(starts[number], rows)]
            target = held_ref.at[place, pl.ds(k * count, count)]
            yield pltpu.make_async_copy(source, target, sems.at[place])

    first = 0
    for place, count in enumerate(counts):
        for number in range(count):

            @pl.when(which_ref[place] == number)
            def _():
                for copy in copies(first + number, place):
                    copy.start()

        first += count
    for place in range(len(counts)):
        held = held_ref.at[place]
        pltpu.make_async_copy(held, held, sems.at[place]).wait()
    for block in range(out_ref.shape[0]):
        value = held_ref[0, block].astype(F32)
        for place in range(1, len(counts)):
            value = value + held_ref[place, block].astype(F32)
        out_ref[block] = value.astype(BF)


def chosen_sum(which, groups, first, rows):
    entries = [
        array if isinstance(array, tuple) else (array,) for group in groups for array in group
    ]
    arrays = [array for entry in entries for array in entry]
    shape = (sum(array.shape[0] for array in entries[0]), rows, D)
    counts = tuple(len(group) for group in groups)
    parts = tuple(len(entry) for entry in entries)
    starts = tuple(0 if entry[0].shape[1] == rows else first for entry in entries)
    return pl.pallas_call(
        functools.partial(chosen_kernel, counts, parts, starts),
        grid=(1,),
        in_specs=[SCALAR, *[ANYWHERE] * len(arrays)],
        out_specs=full(*shape),
        out_shape=jax.ShapeDtypeStruct(shape, BF),
        scratch_shapes=[
            pltpu.VMEM((len(counts), *shape), BF), pltpu.SemaphoreType.DMA((len(counts),)),
        ],
        compiler_params=params(),
        cost_estimate=cost(1e6, 5e6),
        name="chosen_sum",
    )(
        jnp.stack([w.astype(jnp.int32) for w in which]), *[in_hbm(array) for array in arrays],
    )


class Reduction:
    def __init__(self, places):
        self.places = places
        rows = places.blk + 16
        cut = rows // 32 * 16
        self.ranges = ((0, cut), (cut, rows - cut))

    def cores(self, keep, give):
        return keep, self.places.swap_core(give)

    def total(self, which, *sections):
        groups = tuple(zip(*sections, strict=True))
        return [
            self.places.swap_plane(chosen_sum((which, which), groups, *rows), 0)
            for rows in self.ranges
        ]

    def send_early(self, one, two, three):
        places = self.places
        self.sections = (one, two, three)
        low, first = jnp.logical_not(places.first_bit), places.is_first
        which = jnp.where(low, 2, jnp.where(first, 1, 0))
        self.early = self.total(which, one, two, three)

    def plane(self, zero):
        places = self.places
        one, two, three = self.sections
        low, first = jnp.logical_not(places.first_bit), places.is_first
        which = jnp.where(low, jnp.where(first, 1, 2), 0)
        late = self.total(which, zero, one, two)
        keeps, gots = zip(zero, one, two, three, strict=True)
        other = places.section ^ jnp.where(first, 2, 1)
        sums = []
        for early_part, late_part, rows in zip(self.early, late, self.ranges, strict=True):

            def held(section, arrived=(early_part, late_part), rows=rows):
                is_late = (section == 0) | ((section == 1) & first) | ((section == 2) & (~first))
                return chosen_sum((section, section, is_late), (keeps, gots, arrived), *rows)

            got = places.swap_plane(held(other), 1)
            sums.append(held(places.section) + got)
        return sums

    def shared(self, rows):
        return jnp.where(self.places.is_first, rows, self.places.swap_core(rows))

    def depth(self, blocks, beside):
        places = self.places
        place = places.dp // 2
        if blocks.shape[0] == 4:
            near, far = place % 2, place // 2
            mine = jnp.where(places.is_first, near, 2 * far)
            theirs = jnp.where(places.is_first, 1 - near, 2 - 2 * far)
            step = 2 - places.core

            def two(first):
                return jnp.stack([pick(blocks, first), pick(blocks, first + step)])

            blocks = two(mine) + places.send(two(theirs), lambda s, d: (s, d ^ (2 + 2 * (d % 2))))
            mine = jnp.where(places.is_first, far, near)
            got = places.send(
                gate(pick(blocks, 1 - mine), beside), lambda s, d: (s, d ^ (4 - 2 * (d % 2)))
            )
            return pick(blocks, mine).astype(F32) + got.astype(F32), blocks
        bit = 1
        while blocks.shape[0] > 1:
            pairs = blocks.reshape(-1, 2, *blocks.shape[1:])
            mine = (place // bit) % 2
            keep = lax.dynamic_index_in_dim(pairs, mine, 1, keepdims=False)
            give = lax.dynamic_index_in_dim(pairs, 1 - mine, 1, keepdims=False)
            blocks = keep + places.swap_dp(give, 2 * bit)
            bit *= 2
        return blocks[0].astype(F32), blocks


def on_device(
    stream_input,
    accum_input,
    section_weights,
    section_norms,
    final_norm,
    seq_lengths,
    out_cotangent,
):
    places = Places()
    section, core = places.section, places.core
    width = D // SECTIONS
    rows = D // 2

    own = section_weights[0]
    pieces = token_pieces(places, stream_input[None])
    small = jnp.concatenate([section_norms.reshape(2 * D), final_norm.reshape(2 * width)])
    small = jnp.pad(small[None], ((0, 15), (0, 4 * D - small.shape[0])))
    near_pieces = gather_start(
        places,
        jnp.concatenate([lax.dynamic_slice(own, (core * rows, 0), (rows, 4 * D)), small], axis=0),
        *pieces,
    )
    near = gather_finish(places, near_pieces)
    stream = jnp.concatenate(in_order([piece[0] for piece in pieces], places.mine), axis=1)
    one, two, three = (piece[rows] for piece in near_pieces)
    table = in_order(
        (
            small[0], jnp.where(places.turned == 0, one, two), jnp.where(places.turned == 0, two, one),
            three,
        ),
        section,
    )
    norms = jnp.stack(table).astype(F32)
    queries, own_kv = project(places, stream, own, near, 0)
    far_kv = places.swap_core(own_kv)
    late_pieces = gather_start(
        places, lax.dynamic_slice(own, (core * rows, 4 * D), (rows, 2 * D)), queries
    )

    *segs, live = sequences(places, seq_lengths)
    qseg = segs[0]
    both = token_pieces(places, jnp.stack([accum_input, out_cotangent]))

    kept = attend(places, stream, queries, own_kv, far_kv, segs, own, near, norms, 0)
    late = gather_finish(places, [late_pieces[0], gate(late_pieces[1], kept[0]), gate(late_pieces[2], kept[0])])
    sum_f, branch_sum, turning, queries_two, own_kv_two = feed(
        places, stream, kept[3], kept[2], own, near, late, norms, 1
    )
    far_kv_two = places.swap_core(own_kv_two)
    context, lse, middle, sum_a = attend(
        places, turning, queries_two, own_kv_two, far_kv_two, segs, own, near, norms, 2
    )
    (
        result, dy_low, dy, final_grad, dz, dctx, delta, grads, keep_f, give_f, rest,
    ) = turn(
        places, middle, turning, sum_a, context, own, near, late, norms, branch_sum, both, live
    )

    reduction = Reduction(places)

    def scores(queries, own_kv, far_kv, dctx, lse, delta):
        dq, dkv_far = scores_back(queries, far_kv, dctx, qseg, segs[2], lse, delta, BF)
        from_far = places.swap_core(dkv_far)
        dq, dkv = scores_back(queries, own_kv, dctx, qseg, segs[1], lse, delta, BF, dq)
        return dq, dkv, from_far

    third = reduction.cores(keep_f, give_f)
    dq, dkv, from_far = scores(queries_two, own_kv_two, far_kv_two, dctx, lse, delta)
    dz, dctx, delta, grads_first, keep_p, give_p, keep_f, give_f, rest = between(
        places, turning, dq, dkv, from_far, dz, dy, grads, final_grad, rest, (*kept, sum_f), own,
        near, late, norms,
    )
    reduction.send_early(reduction.cores(keep_f, give_f), reduction.cores(keep_p, give_p), third)
    dq, dkv, from_far = scores(queries, own_kv, far_kv, dctx, kept[1], delta)
    upstream, keep, *give = project_back(
        places, stream, dq, dkv, from_far, dz, own, near, 0, grads_first, final_grad, rest
    )
    swapped = places.swap_core(give[0]), places.swap_core(gate(give[1], *reduction.early))
    blocks = reduction.plane((keep, swapped))
    leaving = tokens_out(places, (upstream, result, dy_low), blocks[0])
    reduced, early = zip(*(reduction.depth(part, leaving[2]) for part in blocks), strict=True)
    reduced = jnp.concatenate(reduced, axis=0)
    shared = reduction.shared(reduced[places.blk :])
    stream_out, result_out, accum_out = tokens_placed(places, leaving, (F32, BF, F32), early[1])
    slab = reduced[: places.blk].T
    cut = D // places.ndp
    norm_out = lax.dynamic_slice(reduced, (places.blk, places.dp * cut), (2, cut))
    final_out = lax.dynamic_slice(shared, (2, section * width), (2, width))

    return (
        result_out,
        stream_out,
        accum_out,
        slab[None],
        norm_out[None],
        final_out,
    )


def solution(mesh):
    placed = (
        P("dp", "section"),
        P("dp", "section"),
        P("section", None, None),
        P("section", None, None),
        P(None, "section"),
        P("dp", None),
        P("dp", "section"),
    )
    return jax.shard_map(
        on_device,
        mesh=mesh,
        in_specs=placed,
        out_specs=(
            P("dp", "section"),
            P("dp", "section"),
            P("dp", "section"),
            P("section", None, "dp"),
            P("section", None, "dp"),
            P(None, "section"),
        ),
        check_vma=False,
    )
```
